32 devices in a mesh: grp: 4 (over z), mem: 8 (over y, x, core).
Axes of the slice: x: 2, y: 2, z: 4, core: 2. Of those that a mesh axis runs over, the one named last changes fastest.
Arguments:
- candidates: bfloat16 [32768, 4096], P(('grp', 'mem')), may hold values from -1 to 1
- round_one: bfloat16 [2048, 4096], P(('grp', 'mem')), may hold values from -1 to 1
- counts: int32 [4, 8], P('grp', 'mem'), may hold values from 1 to 64, 192 in all within a row
- chosen: int32 [4, 128], P('grp'), may hold values from 0 to 191, as said below
Outputs:
- group_dist: float32 [32768], P(('grp', 'mem'))
- final_dist: float32 [32768], P(('grp', 'mem'))
The draws below stay inside these ranges and needn't reach their ends.
Inputs may be any that keep to these rules, and one draw needn't show every extreme that they name: In each group the counts sum to 192, and some device of each group has exactly 64. `chosen`: within a group the 128 positions are distinct, each below 192.
All inputs are finite; a program needn't handle non-finite values.
Results may differ from the reference program's by a relative error of at most 0.0003.
Values may be sent and summed in bfloat16 or wider, within the bound.
No kernel may reach another device: no remote copies, remote signals or barrier semaphores. Data moves between devices by JAX's collectives and lax.ppermute only.
A program may use at most 128 MiB of HBM per device.

```python
import math
import jax
import jax.numpy as jnp
import numpy as np
from jax import lax

EMBED_DIM = 4096
ROWS_DEV = 1024
ROUND_MAX = 64
KCENTERS = 128
GROUP_CENTERS = 192
ROWS_ALL = 32768
SLOTS_ALL = 2048
N_GRP = 4
N_MEM = 8


def center_table(key):
    table_key = jax.random.fold_in(key, 101)
    entry_key, scale_key = jax.random.split(table_key)
    entries = jnp.clip(jax.random.normal(entry_key, (SLOTS_ALL, EMBED_DIM), jnp.float32), -4.0, 4.0)
    row_scale = jnp.exp(jax.random.uniform(scale_key, (SLOTS_ALL,), jnp.float32, math.log(0.7), math.log(1.4)))
    return entries * (row_scale[:, None] / math.sqrt(EMBED_DIM))


def draw_round_one(key, part):
    return center_table(key).astype(jnp.bfloat16)


def draw_candidates(key, part):
    table = center_table(key)
    pick_key = jax.random.fold_in(key, 203)
    own_key, any_key, side_key, noise_key, level_key = jax.random.split(pick_key, 5)
    group_slots = ROUND_MAX * N_MEM
    row_ids = jnp.arange(ROWS_ALL, dtype=jnp.int32)
    home = row_ids // (ROWS_DEV * N_MEM)
    own_source = home * group_slots + jax.random.randint(own_key, (ROWS_ALL,), 0, group_slots)
    any_source = jax.random.randint(any_key, (ROWS_ALL,), 0, SLOTS_ALL)
    side = jax.random.randint(side_key, (ROWS_ALL,), 0, 2)
    source = jnp.where(side == 0, own_source, any_source).astype(jnp.int32)
    level = jnp.exp(jax.random.uniform(level_key, (ROWS_ALL,), jnp.float32, math.log(0.15), math.log(0.5)))
    noise = jnp.clip(jax.random.normal(noise_key, (ROWS_ALL, EMBED_DIM), jnp.float32), -4.0, 4.0)
    rows = table[source] + noise * (level[:, None] / math.sqrt(EMBED_DIM))
    return rows.astype(jnp.bfloat16)


def draw_chosen(key, part):
    group_keys = jax.random.split(key, N_GRP + 2)

    def one_group(group_key):
        return jax.random.permutation(group_key, GROUP_CENTERS - 1)[:KCENTERS]
    drawn_ids = jax.vmap(one_group)(group_keys[:N_GRP]).astype(jnp.int32)
    target_group = jax.random.randint(group_keys[N_GRP], (), 0, N_GRP)
    target_slot = jax.random.randint(group_keys[N_GRP + 1], (), 0, KCENTERS)
    group_ids = jnp.arange(N_GRP, dtype=jnp.int32)[:, None]
    slot_ids = jnp.arange(KCENTERS, dtype=jnp.int32)[None, :]
    replace_here = (group_ids == target_group) & (slot_ids == target_slot)
    return jnp.where(replace_here, GROUP_CENTERS - 1, drawn_ids).astype(jnp.int32)


def length_profile(amount, total, bound, slope):
    weights = [(1 << 20) // math.isqrt(standing ** slope) + 1 for standing in range(2, amount + 1)]
    rest, given = total - bound - (amount - 1), [1] * (amount - 1)
    while rest > 0:
        free = [i for i in range(amount - 1) if given[i] < bound]
        mass, budget = sum([weights[i] for i in free]), rest
        for i in free:
            extra = min(bound - given[i], max(1, budget * weights[i] // mass), rest)
            given[i] = given[i] + extra
            rest = rest - extra
    return np.array([bound] + given)


def ragged_sizes(rng, number_of, total, limit, lean):
    if number_of == 2:
        one = jax.random.randint(rng, (), max(1, total - limit), min(limit, total - 1) + 1)
        return jnp.stack([one, total - one])
    tallies = jnp.asarray(length_profile(number_of, total, limit, lean), jnp.int32)
    twos = (number_of - 1) // 2
    giver, sink = tallies[1:1 + 2 * twos:2], tallies[2:2 + 2 * twos:2]
    room = jnp.minimum(giver - 1, limit - sink)
    shifted = jax.random.randint(jax.random.fold_in(rng, 1), (twos,), 0, 1 << 20) % (room + 1)
    tallies = tallies.at[1:1 + 2 * twos:2].set(giver - shifted).at[2:2 + 2 * twos:2].set(sink + shifted)
    return tallies[jax.random.permutation(jax.random.fold_in(rng, 2), number_of)]


def setup_inputs(seed: int = 0) -> dict:
    arg_keys = jax.random.split(jax.random.key(seed), 5)
    return {
        "candidates": draw_candidates(jax.random.fold_in(arg_keys[4], 71), 0),
        "round_one": draw_round_one(jax.random.fold_in(arg_keys[4], 71), 0),
        "counts": jax.vmap(lambda own: ragged_sizes(own, N_MEM, GROUP_CENTERS, ROUND_MAX, 2))(jax.random.split(arg_keys[2], N_GRP)).reshape((N_GRP, N_MEM)).astype(jnp.int32),
        "chosen": draw_chosen(jax.random.fold_in(arg_keys[4], 71), 0),
    }


def sq_norms(matrix):
    return jnp.sum(jnp.square(matrix.astype(jnp.float32)), axis=1)


def distances(cand_rows, cand_norm, center_rows):
    inner = lax.dot_general(cand_rows, center_rows, (((1,), (1,)), ((), ())), preferred_element_type=jnp.float32)
    return (cand_norm[:, None] + sq_norms(center_rows)[None, :]) - 2.0 * inner


def reference(candidates, round_one, counts, chosen):
    slot_total = N_MEM * ROUND_MAX
    cand_groups = candidates.reshape(N_GRP, N_MEM * ROWS_DEV, EMBED_DIM)
    center_groups = round_one.reshape(N_GRP, slot_total, EMBED_DIM)
    slot_ids = jnp.arange(slot_total, dtype=jnp.int32)
    within = slot_ids % ROUND_MAX
    holder = slot_ids // ROUND_MAX

    def group_work(inputs):
        cand_rows, center_rows, group_counts, picked_ids = inputs
        offsets = jnp.cumsum(group_counts) - group_counts
        usable = within < group_counts[holder]
        position = offsets[holder] + within
        gaps = distances(cand_rows, sq_norms(cand_rows), center_rows)
        gaps = jnp.where(usable[None, :], gaps, jnp.inf)
        nearest = jnp.min(gaps, axis=1)
        select = ((picked_ids[:, None] == position[None, :]) & usable[None, :]).astype(jnp.float32)
        picked = jnp.dot(select, center_rows.astype(jnp.float32), precision=lax.Precision.HIGHEST).astype(jnp.bfloat16)
        return nearest, picked

    nearest, picked = lax.map(group_work, (cand_groups, center_groups, counts, chosen))
    every_center = picked.reshape(N_GRP * KCENTERS, EMBED_DIM)

    def final_work(cand_rows):
        return jnp.min(distances(cand_rows, sq_norms(cand_rows), every_center), axis=1)

    final = lax.map(final_work, cand_groups)
    return nearest.reshape(-1), final.reshape(-1)
```

```python
import jax
import jax.numpy as jnp
from jax import lax
from jax.sharding import PartitionSpec as P


def sq_norms(matrix):
    return jnp.sum(jnp.square(matrix.astype(jnp.float32)), axis=1)


def axis_bits(size):
    return [1 << b for b in range(size.bit_length() - 1)]


def flips(size):
    chip_bits = [b for b in axis_bits(size) if b > 1]
    turned = chip_bits[1:] + chip_bits[:1]
    return chip_bits, turned


def mixed_permute(block, size, stage):
    even, odd = flips(size)
    pairs = [(m, m ^ (odd[stage] if m & 1 else even[stage])) for m in range(size)]
    return lax.ppermute(block, "mem", pairs)


def core_permute(block, size):
    return lax.ppermute(block, "mem", [(m, m ^ 1) for m in range(size)])


def gather_blocks(block, size, me):
    even, odd = flips(size)
    odd_core = me & 1
    held = [(block, me)]
    for stage in range(len(even)):
        step = jnp.where(odd_core == 1, odd[stage], even[stage])
        held = held + [(mixed_permute(b, size, stage), o ^ step) for b, o in held]
    other = []
    for stage_count, (b, _) in enumerate(held):
        other.append(core_permute(b, size))
    sib = me ^ 1
    origins = [sib]
    for stage in range(len(even)):
        step = jnp.where(odd_core == 1, even[stage], odd[stage])
        origins = origins + [o ^ step for o in origins]
    return held + list(zip(other, origins))


def body(candidates, round_one, counts, chosen):
    mem_size = lax.axis_size("mem")
    grp_size = lax.axis_size("grp")
    me = lax.axis_index("mem")
    slot_max, width = round_one.shape
    picks_total = chosen.shape[1]
    share = picks_total // mem_size
    row_ids = jnp.arange(slot_max, dtype=jnp.int32)

    mark = (row_ids[:, None] >= counts[0, 0]) & (jnp.arange(width) == 0)[None, :]
    marked = jnp.where(mark, jnp.bfloat16(2.0), round_one)
    held = gather_blocks(marked, mem_size, me)
    cand_norm = sq_norms(candidates)

    live_counts = [jnp.sum((b[:, 0] < 1.5).astype(jnp.int32)) for b, _ in held]
    origins = [o for _, o in held]
    offsets = [
        sum(jnp.where(o2 < o1, n2, 0) for n2, o2 in zip(live_counts, origins)) for o1 in origins
    ]
    usable = jnp.concatenate([row_ids < n for n in live_counts])
    position = jnp.concatenate([row_ids + o for o in offsets])
    rows = jnp.concatenate([b for b, _ in held], axis=0)

    my_ids = lax.dynamic_slice_in_dim(chosen[0], me * share, share, 0)
    select = ((my_ids[:, None] == position[None, :]) & usable[None, :]).astype(jnp.bfloat16)
    picked = jnp.dot(select, rows, preferred_element_type=jnp.float32).astype(jnp.bfloat16)

    far = [
        lax.ppermute(picked, "grp", [(g, (g + k) % grp_size) for g in range(grp_size)])
        for k in range(1, grp_size)
    ]
    far_rows = jnp.concatenate(far, axis=0)
    far_blocks = [b for b, _ in gather_blocks(far_rows, mem_size, me)]

    inner = lax.dot_general(
        candidates, rows, (((1,), (1,)), ((), ())), preferred_element_type=jnp.float32
    )
    gaps = cand_norm[:, None] + sq_norms(rows)[None, :] - 2.0 * inner
    nearest = jnp.min(jnp.where(usable[None, :], gaps, jnp.inf), axis=1)
    is_pick = jnp.any((chosen[0][:, None] == position[None, :]) & usable[None, :], axis=0)
    own_final = jnp.min(jnp.where(is_pick[None, :], gaps, jnp.inf), axis=1)

    far_all = jnp.concatenate(far_blocks, axis=0)
    far_inner = lax.dot_general(
        candidates, far_all, (((1,), (1,)), ((), ())), preferred_element_type=jnp.float32
    )
    far_gaps = cand_norm[:, None] + sq_norms(far_all)[None, :] - 2.0 * far_inner
    final = jnp.minimum(own_final, jnp.min(far_gaps, axis=1))
    return nearest, final


def solution(mesh):
    in_specs = (P(("grp", "mem"), None), P(("grp", "mem"), None), P("grp", "mem"), P("grp", None))
    out_specs = (P(("grp", "mem")), P(("grp", "mem")))
    return jax.shard_map(body, mesh=mesh, in_specs=in_specs, out_specs=out_specs, check_vma=False)
```

```python
import functools

import jax
import jax.numpy as jnp
from jax import lax
from jax.experimental import pallas as pl
from jax.experimental.pallas import tpu as pltpu
from jax.sharding import PartitionSpec as P


def sq_norms(matrix):
    return jnp.sum(jnp.square(matrix.astype(jnp.float32)), axis=1)


def chip_bits(size):
    return [1 << b for b in range(1, size.bit_length() - 1)]


def xor_permute(block, size, flip):
    return lax.ppermute(block, "mem", [(m, m ^ flip) for m in range(size)])


def mixed_permute(block, size, stage):
    bits = chip_bits(size)
    even, odd = bits[stage], bits[len(bits) - 1 - stage]
    return lax.ppermute(block, "mem", [(m, m ^ (odd if m & 1 else even)) for m in range(size)])


def gather_chips(block, size):
    held = [block]
    for stage in range(len(chip_bits(size))):
        held = held + [mixed_permute(b, size, stage) for b in held]
    return held


def sibling_place(index, stages):
    place = 0
    for s in range(stages):
        if index >> s & 1:
            place |= 1 << (stages - 1 - s)
    return place


def join_cores(held, size):
    stages = len(chip_bits(size))
    other = [None] * len(held)
    for i, block in enumerate(held):
        other[sibling_place(i, stages)] = xor_permute(block, size, 1)
    return jnp.concatenate(
        [jnp.concatenate(held, axis=0), jnp.concatenate(other, axis=0)], axis=1
    )


def dense_kernel(size, picks_chip, rest_chip, counts_ref, chosen_ref, own_ref, sib_ref, *rest):
    outs, raw, sems = rest[:-2], rest[-2], rest[-1]
    me = lax.axis_index("mem")
    chip, core = me // 2, me % 2
    slots, half = own_ref.shape[0], raw.shape[1]
    columns = pl.ds(pl.multiple_of(core * half, half), half)
    copies = [
        pltpu.make_async_copy(ref.at[:, columns], raw.at[pl.ds(i * slots, slots), :], sems.at[i])
        for i, ref in enumerate((own_ref, sib_ref))
    ]
    for copy in copies:
        copy.start()

    offset_own, offset_sib = jnp.int32(0), jnp.int32(0)
    for d in range(size):
        origin, count = lax.bitwise_xor(me, d), counts_ref[0, d]
        offset_own += jnp.where(origin < me, count, 0)
        offset_sib += jnp.where(origin < lax.bitwise_xor(me, 1), count, 0)
    lane = lax.broadcasted_iota(jnp.int32, (1, 2 * slots), 1)
    first = lane < slots
    within = jnp.where(first, lane, lane - slots)
    live = within < jnp.where(first, counts_ref[0, 0], counts_ref[0, 1])
    position = jnp.where(live, within + jnp.where(first, offset_own, offset_sib), -1)
    chosen = chosen_ref[...]
    below = jnp.sum((chosen < position).astype(jnp.int32), axis=0, keepdims=True)
    taken = jnp.sum((chosen == position).astype(jnp.int32), axis=0, keepdims=True)
    rank = jnp.where(live & (taken == 0), position - below, -1)

    for copy in copies:
        copy.wait()
    rows = raw[...]
    place = lax.broadcasted_iota(jnp.int32, (rest_chip, 1), 0)
    for d, out in enumerate(outs):
        target = lax.bitwise_xor(chip, d)
        ids = chosen_ref[pl.ds(pl.multiple_of(target * picks_chip, picks_chip), picks_chip), :]
        for select, at in (
            (ids == position, pl.ds(0, picks_chip)),
            (place + target * rest_chip == rank, pl.ds(picks_chip, rest_chip)),
        ):
            one_hot = select.astype(jnp.float32).astype(jnp.bfloat16)
            out[at, :] = jnp.dot(one_hot, rows, preferred_element_type=jnp.float32).astype(
                jnp.bfloat16
            )


def dense_parts(size, picks_chip, rest_chip, counts, chosen, own, sib):
    slots, width = own.shape
    chips, half = size // 2, width // 2
    rows = picks_chip + rest_chip
    return pl.pallas_call(
        functools.partial(dense_kernel, size, picks_chip, rest_chip),
        out_shape=[jax.ShapeDtypeStruct((rows, half), jnp.bfloat16)] * chips,
        in_specs=[
            pl.BlockSpec(memory_space=pltpu.SMEM),
            pl.BlockSpec(memory_space=pltpu.VMEM),
            pl.BlockSpec(memory_space=pl.ANY),
            pl.BlockSpec(memory_space=pl.ANY),
        ],
        out_specs=[pl.BlockSpec(memory_space=pltpu.VMEM)] * chips,
        scratch_shapes=[
            pltpu.VMEM((2 * slots, half), jnp.bfloat16),
            pltpu.SemaphoreType.DMA((2,)),
        ],
        cost_estimate=pl.CostEstimate(
            flops=2 * chips * rows * 2 * slots * half,
            bytes_accessed=2 * (2 * slots + chips * rows) * half,
            transcendentals=0,
        ),
        name="dense_parts",
    )(counts, chosen, own, sib)


def body(candidates, round_one, counts, chosen):
    mem_size = lax.axis_size("mem")
    grp_size = lax.axis_size("grp")
    me = lax.axis_index("mem")
    slot_max, width = round_one.shape
    half, chips = width // 2, mem_size // 2
    picks_total = chosen.shape[1]
    live_total = mem_size * slot_max * 3 // 8
    picks_chip = picks_total // chips
    rest_chip = (live_total - picks_total) // chips
    rows_chip = picks_chip + rest_chip

    group_counts = jnp.concatenate(
        [counts] + [xor_permute(counts, mem_size, d) for d in range(1, mem_size)], axis=1
    )
    sib_rows = xor_permute(round_one, mem_size, 1)
    parts = dense_parts(
        mem_size, picks_chip, rest_chip, group_counts, chosen.reshape(-1, 1), round_one, sib_rows
    )
    own = parts[0]
    for d in range(1, chips):
        own = own + xor_permute(parts[d], mem_size, 2 * d)

    start = (me % 2) * half
    cand = jnp.concatenate(
        [
            lax.dynamic_slice_in_dim(candidates, start, half, 1),
            lax.dynamic_slice_in_dim(candidates, half - start, half, 1),
        ],
        axis=1,
    )
    cand_norm = sq_norms(candidates)

    picks = own[:picks_chip]
    far = [
        lax.ppermute(picks, "grp", [(g, (g + k) % grp_size) for g in range(grp_size)])
        for k in range(1, grp_size)
    ]

    def gaps_to(rows):
        inner = lax.dot_general(
            cand, rows, (((1,), (1,)), ((), ())), preferred_element_type=jnp.float32
        )
        return cand_norm[:, None] + sq_norms(rows)[None, :] - 2.0 * inner

    own_gaps = gaps_to(join_cores(gather_chips(own, mem_size), mem_size))
    nearest = jnp.min(own_gaps, axis=1)
    is_pick = jnp.arange(chips * rows_chip) % rows_chip < picks_chip
    final = jnp.min(jnp.where(is_pick[None, :], own_gaps, jnp.inf), axis=1)
    far_rows = [join_cores(gather_chips(block, mem_size), mem_size) for block in far]
    for rows in (jnp.concatenate(far_rows[:-1], axis=0), far_rows[-1]):
        final = jnp.minimum(final, jnp.min(gaps_to(rows), axis=1))
    return nearest, final


def solution(mesh):
    in_specs = (P(("grp", "mem"), None), P(("grp", "mem"), None), P("grp", "mem"), P("grp", None))
    out_specs = (P(("grp", "mem")), P(("grp", "mem")))
    return jax.shard_map(body, mesh=mesh, in_specs=in_specs, out_specs=out_specs, check_vma=False)
```

```python
import functools

import jax
import jax.numpy as jnp
from jax import lax
from jax.experimental import pallas as pl
from jax.experimental.pallas import tpu as pltpu
from jax.sharding import PartitionSpec as P

CHUNKS = 2
TILE = 256
MARK = 2.0
VMEM_LIMIT = 28 * 1024 * 1024
LOAD_VMEM_LIMIT = 42 * 1024 * 1024
F32, BF16 = jnp.float32, jnp.bfloat16


def chip_bits(size):
    return [1 << b for b in range(1, size.bit_length() - 1)]


def crossing(size, odd):
    return chip_bits(size)[::-1] if odd else chip_bits(size)


def mixed_permute(block, size, stage):
    even, odd = crossing(size, False)[stage], crossing(size, True)[stage]
    return lax.ppermute(block, "mem", [(m, m ^ (odd if m & 1 else even)) for m in range(size)])


def core_permute(block, size):
    return lax.ppermute(block, "mem", [(m, m ^ 1) for m in range(size)])


def gather_mem(block, size):
    held = [block]
    for stage in range(len(chip_bits(size))):
        held = held + [mixed_permute(b, size, stage) for b in held]
    return held + [core_permute(b, size) for b in held]


def block_flips(size, odd):
    flips = [0]
    for bit in crossing(size, odd):
        flips = flips + [f ^ bit for f in flips]
    return flips


def block_origins(me, size):
    odd_core = lax.rem(me, 2) == 1
    even, odd = block_flips(size, False), block_flips(size, True)
    own = [lax.bitwise_xor(me, jnp.where(odd_core, o, e)) for e, o in zip(even, odd)]
    sib = [lax.bitwise_xor(me, jnp.where(odd_core, e, o) + 1) for e, o in zip(even, odd)]
    return own + sib


def vmem_specs(count):
    return [pl.BlockSpec(memory_space=pltpu.VMEM)] * count


def call(kernel, name, out_shape, operands, flops, specs=None, scratch=(), after=(), limit=VMEM_LIMIT):
    shapes = jax.tree.leaves(out_shape)
    moved = sum(a.size * a.dtype.itemsize for a in list(operands) + shapes)
    count = len(operands)

    def run(*refs):
        kernel(*refs[:count], *refs[count + len(after) :])

    return pl.pallas_call(
        run,
        out_shape=out_shape,
        in_specs=(specs or vmem_specs(count)) + [pl.BlockSpec(memory_space=pl.ANY)] * len(after),
        out_specs=jax.tree.map(lambda _: pl.BlockSpec(memory_space=pltpu.VMEM), out_shape),
        scratch_shapes=scratch,
        compiler_params=pltpu.CompilerParams(vmem_limit_bytes=limit),
        cost_estimate=pl.CostEstimate(flops=flops, bytes_accessed=moved, transcendentals=0),
        name=name,
    )(*operands, *after)


def split_kernel(chunk, count_ref, rows_ref, out):
    slots, part = out.shape
    out[...] = rows_ref[:, chunk * part : (chunk + 1) * part]
    if chunk:
        return
    lane = lax.broadcasted_iota(jnp.int32, (slots, 128), 1)
    row = lax.broadcasted_iota(jnp.int32, (slots, 128), 0)
    dead = (lane == 0) & (row >= count_ref[0, 0])
    out[:, :128] = jnp.where(dead, MARK, rows_ref[:, :128].astype(F32)).astype(BF16)


def load_kernel(cand_hbm, cand_ref, norm_ref, sems):
    tiles = cand_ref.shape[0] // TILE
    copies = [
        pltpu.make_async_copy(
            cand_hbm.at[pl.ds(t * TILE, TILE), :], cand_ref.at[pl.ds(t * TILE, TILE), :], sems.at[t]
        )
        for t in range(tiles)
    ]
    for copy in copies:
        copy.start()
    for t, copy in enumerate(copies):
        copy.wait()
        squares = jnp.zeros((TILE, 128), F32)
        for k in range(0, cand_ref.shape[1], 128):
            entries = cand_ref[t * TILE : (t + 1) * TILE, k : k + 128].astype(F32)
            squares += entries * entries
        norm_ref[:, t * TILE : (t + 1) * TILE] = jnp.sum(squares.T, axis=0, keepdims=True)


def join_kernel(*refs):
    blocks, out = refs[:-1], refs[-1]
    out[...] = jnp.concatenate([b[...] for b in blocks], axis=0)


def select_rows(select, blocks, out):
    slots = blocks[0].shape[0]

    @pl.loop(0, out.shape[1] // TILE)
    def _(t):
        at = pl.ds(pl.multiple_of(t * TILE, TILE), TILE)
        rows = jnp.concatenate([b[:, at] for b in blocks], axis=0)
        out[:, at] = jnp.dot(select, rows, preferred_element_type=F32).astype(BF16)


def first_pick_kernel(size, chosen_ref, *refs):
    blocks, (out, select_ref, live_ref, pick_ref) = refs[:size], refs[size:]
    slots, share = blocks[0].shape[0], out.shape[0]
    picks = chosen_ref.shape[1]
    me = lax.axis_index("mem")
    origins = block_origins(me, size)
    counts = [
        jnp.sum((b[:, :1].astype(F32) < 1.5).astype(jnp.int32), axis=0, keepdims=True)
        for b in blocks
    ]
    chosen = chosen_ref[...]
    row = lax.broadcasted_iota(jnp.int32, (share, picks), 0)
    lane = lax.broadcasted_iota(jnp.int32, (share, picks), 1)
    ids = jnp.sum(jnp.where(lane == me * share + row, chosen, 0), axis=1, keepdims=True)
    across = lax.broadcasted_iota(jnp.int32, (1, slots), 1)
    down = lax.broadcasted_iota(jnp.int32, (slots, 1), 0)
    for i, count in enumerate(counts):
        offset = jnp.zeros((1, 1), jnp.int32)
        for other, origin in zip(counts, origins):
            offset += other * (origin < origins[i]).astype(jnp.int32)
        at = slice(i * slots, (i + 1) * slots)
        position = jnp.where(across < count, across + offset, -1)
        select_ref[:, at] = (ids == position).astype(F32).astype(BF16)
        live = down < count
        hit = jnp.max((chosen == down + offset).astype(F32), axis=1, keepdims=True) > 0.5
        live_ref[at, :] = jnp.where(live, 0.0, jnp.inf)
        pick_ref[at, :] = jnp.where(live & hit, 0.0, jnp.inf)
    select_rows(select_ref[...], blocks, out)


def next_pick_kernel(size, select_ref, *refs):
    select_rows(select_ref[...], refs[:size], refs[size])


def row_norms(ref):
    rows = ref[...].astype(F32)
    return jnp.sum(rows * rows, axis=1, keepdims=True)


def group_kernel(size, cand_ref, norm_ref, live_ref, pick_ref, *refs):
    blocks, (near_ref, own_ref, rows_ref, cn_ref) = refs[:-4], refs[-4:]
    slots, part = blocks[0].shape
    for i in range(size):
        at = slice(i * slots, (i + 1) * slots)
        norm = jnp.zeros((slots, 1), F32)
        for c in range(CHUNKS):
            block = blocks[c * size + i]
            rows_ref[at, c * part : (c + 1) * part] = block[...]
            norm += row_norms(block)
        cn_ref[at, :] = norm

    @pl.loop(0, cand_ref.shape[0] // TILE)
    def _(t):
        at = pl.ds(pl.multiple_of(t * TILE, TILE), TILE)
        inner = lax.dot_general(
            rows_ref[...], cand_ref[at, :], (((1,), (1,)), ((), ())), preferred_element_type=F32
        )
        gaps = cn_ref[...] - 2.0 * inner
        nearest = jnp.min(gaps + live_ref[...], axis=0, keepdims=True)
        near_ref[:, at] = nearest + norm_ref[:, at]
        own_ref[:, at] = jnp.min(gaps + pick_ref[...], axis=0, keepdims=True)


def far_gaps(chunk, cand_ref, blocks, rows_ref, cn_ref, emit):
    count, part = blocks[0].shape
    for i, block in enumerate(blocks):
        at = slice(i * count, (i + 1) * count)
        rows_ref[at, :] = block[...]
        cn_ref[at, :] = row_norms(block)

    @pl.loop(0, cand_ref.shape[0] // TILE)
    def _(t):
        at = pl.ds(pl.multiple_of(t * TILE, TILE), TILE)
        inner = lax.dot_general(
            rows_ref[...],
            cand_ref[at, chunk * part : (chunk + 1) * part],
            (((1,), (1,)), ((), ())),
            preferred_element_type=F32,
        )
        emit(at, cn_ref[...] - 2.0 * inner)


def far_kernel(chunk, cand_ref, *refs):
    blocks, (part_ref, rows_ref, cn_ref) = refs[:-3], refs[-3:]
    before = None
    if chunk:
        before, blocks = blocks[0], blocks[1:]

    def emit(at, gaps):
        part_ref[:, at] = gaps + before[:, at] if chunk else gaps

    far_gaps(chunk, cand_ref, blocks, rows_ref, cn_ref, emit)


def last_kernel(chunk, cand_ref, own_ref, norm_ref, before, *refs):
    blocks, (out, rows_ref, cn_ref) = refs[:-3], refs[-3:]

    def emit(at, gaps):
        nearest = jnp.min(gaps + before[:, at], axis=0, keepdims=True)
        out[:, at] = jnp.minimum(nearest, own_ref[:, at]) + norm_ref[:, at]

    far_gaps(chunk, cand_ref, blocks, rows_ref, cn_ref, emit)


def body(candidates, round_one, counts, chosen):
    size, groups = lax.axis_size("mem"), lax.axis_size("grp")
    slots, width = round_one.shape
    part = width // CHUNKS
    picks, rows = chosen.shape[1], candidates.shape[0]
    share = picks // size
    shape = jax.ShapeDtypeStruct
    line = shape((1, rows), F32)

    def split(chunk, *after):
        return call(
            functools.partial(split_kernel, chunk), "split", shape((slots, part), BF16),
            (counts, round_one), 0, after=after,
            specs=[pl.BlockSpec(memory_space=pltpu.SMEM)] + vmem_specs(1),
        )

    tiles = rows // TILE
    cand, norm = call(
        load_kernel, "load", [shape(candidates.shape, BF16), line], (candidates,), 0,
        specs=[pl.BlockSpec(memory_space=pltpu.HBM)], scratch=[pltpu.SemaphoreType.DMA((tiles,))],
        limit=LOAD_VMEM_LIMIT,
    )
    raw, far, shifted, near = [], [], [], None
    flops = 2 * share * size * slots * part
    out, mask = shape((share, part), BF16), shape((size * slots, 1), F32)
    for c in range(CHUNKS):
        raw.append(gather_mem(split(c, *[blocks[1] for blocks in raw[-1:]], *[norm][: len(raw)]), size))
    for c in range(CHUNKS):
        if c == 0:
            picked, select, live, pick = call(
                functools.partial(first_pick_kernel, size), "pick_first",
                [out, shape((share, size * slots), BF16), mask, mask], (chosen, *raw[c]), flops,
                after=(raw[-1][1], raw[-1][2], raw[-1][size // 2]),
            )
        else:
            picked = call(
                functools.partial(next_pick_kernel, size), "pick_next", out, (select, *raw[c]),
                flops, after=shifted,
            )
        if c == CHUNKS - 1:
            near, own = call(
                functools.partial(group_kernel, size), "group", [line] * 2,
                (cand, norm, live, pick, *sum(raw, [])), 2 * rows * size * slots * width,
                scratch=[pltpu.VMEM((size * slots, width), BF16), pltpu.VMEM((size * slots, 1), F32)],
                after=(picked,),
            )
        shifted = [
            lax.ppermute(picked, "grp", [(g, (g + k) % groups) for g in range(groups)])
            for k in range(1, groups)
        ]
        if share % 16:
            block = jnp.concatenate(shifted, axis=0)
        else:
            block = call(
                join_kernel, "join", shape(((groups - 1) * share, part), BF16), shifted, 0,
                after=() if near is None else (near,),
            )
        blocks = gather_mem(block, size)
        if blocks[0].shape[0] % 16:
            blocks = [jnp.concatenate(blocks, axis=0)]
        far.append(blocks)

    centers = (groups - 1) * picks
    scratch = [pltpu.VMEM((centers, part), BF16), pltpu.VMEM((centers, 1), F32)]
    flops = 2 * rows * centers * part
    before = ()
    for c in range(CHUNKS - 1):
        before = (
            call(
                functools.partial(far_kernel, c), "far", shape((centers, rows), F32),
                (cand, *before, *far[c]), flops, scratch=scratch,
            ),
        )
    final = call(
        functools.partial(last_kernel, CHUNKS - 1), "far_last", line,
        (cand, own, norm, *before, *far[-1]), flops, scratch=scratch,
    )
    return near.reshape(-1), final.reshape(-1)


def solution(mesh):
    in_specs = (P(("grp", "mem"), None), P(("grp", "mem"), None), P("grp", "mem"), P("grp", None))
    out_specs = (P(("grp", "mem")), P(("grp", "mem")))
    return jax.shard_map(body, mesh=mesh, in_specs=in_specs, out_specs=out_specs, check_vma=False)
```

```python
import functools

import jax
import jax.numpy as jnp
from jax import lax
from jax.experimental import pallas as pl
from jax.experimental.pallas import tpu as pltpu
from jax.sharding import PartitionSpec as P

CHUNKS = 2
TILE = 256
MARK = 2.0
MIB = 1024 * 1024
F32, BF16 = jnp.float32, jnp.bfloat16


def chip_bits(size):
    return [1 << b for b in range(1, size.bit_length() - 1)]


def crossing(size, odd):
    return chip_bits(size)[::-1] if odd else chip_bits(size)


def mixed_permute(block, size, stage):
    even, odd = crossing(size, False)[stage], crossing(size, True)[stage]
    return lax.ppermute(block, "mem", [(m, m ^ (odd if m & 1 else even)) for m in range(size)])


def core_permute(block, size):
    return lax.ppermute(block, "mem", [(m, m ^ 1) for m in range(size)])


def gather_chips(block, size):
    held = [block]
    for stage in range(len(chip_bits(size))):
        held = held + [mixed_permute(b, size, stage) for b in held]
    return held


def block_flips(size, odd):
    flips = [0]
    for bit in crossing(size, odd):
        flips = flips + [f ^ bit for f in flips]
    return flips


def sibling_place(index, size):
    return block_flips(size, True).index(block_flips(size, False)[index])


def vmem_specs(count):
    return [pl.BlockSpec(memory_space=pltpu.VMEM)] * count


def call(
    kernel, name, out_shape, operands, flops=0, specs=None, scratch=(), after=(), limit=28 * MIB
):
    shapes = jax.tree.leaves(out_shape)
    moved = sum(a.size * a.dtype.itemsize for a in list(operands) + shapes)
    count = len(operands)

    def run(*refs):
        kernel(*refs[:count], *refs[count + len(after) :])

    return pl.pallas_call(
        run,
        out_shape=out_shape,
        in_specs=(specs or vmem_specs(count)) + [pl.BlockSpec(memory_space=pl.ANY)] * len(after),
        out_specs=jax.tree.map(lambda _: pl.BlockSpec(memory_space=pltpu.VMEM), out_shape),
        scratch_shapes=scratch,
        compiler_params=pltpu.CompilerParams(vmem_limit_bytes=limit),
        cost_estimate=pl.CostEstimate(flops=flops, bytes_accessed=moved, transcendentals=0),
        name=name,
    )(*operands, *after)


def mark_kernel(count_ref, rows_ref, keep_ref, send_ref):
    slots, half = keep_ref.shape
    core = lax.rem(lax.axis_index("mem"), 2)
    lane = lax.broadcasted_iota(jnp.int32, (slots, 128), 1)
    row = lax.broadcasted_iota(jnp.int32, (slots, 128), 0)
    dead = (lane == 0) & (row >= count_ref[0, 0])
    for out, start in ((keep_ref, core * half), (send_ref, (1 - core) * half)):
        start = pl.multiple_of(start, half)
        first = rows_ref[:, pl.ds(start, 128)].astype(F32)
        out[...] = rows_ref[:, pl.ds(start, half)]
        out[:, :128] = jnp.where(dead, MARK, first).astype(BF16)


def load_kernel(cand_hbm, cand_ref, norm_ref, sems):
    half = cand_ref.shape[1] // 2
    part = half // CHUNKS
    core = lax.rem(lax.axis_index("mem"), 2)
    tiles = cand_ref.shape[0] // TILE
    copies = []
    for t in range(tiles):
        at = pl.ds(t * TILE, TILE)
        for p in range(2 * CHUNKS):
            own = core if p % 2 == 0 else 1 - core
            start = pl.multiple_of(own * half + p // 2 * part, part)
            copies.append(
                pltpu.make_async_copy(
                    cand_hbm.at[at, pl.ds(start, part)],
                    cand_ref.at[at, pl.ds(p * part, part)],
                    sems.at[len(copies)],
                )
            )
    for copy in copies:
        copy.start()
    for t in range(tiles):
        for copy in copies[t * 2 * CHUNKS : (t + 1) * 2 * CHUNKS]:
            copy.wait()
        squares = jnp.zeros((TILE, 128), F32)
        for k in range(0, cand_ref.shape[1], 128):
            entries = cand_ref[t * TILE : (t + 1) * TILE, k : k + 128].astype(F32)
            squares += entries * entries
        norm_ref[:, t * TILE : (t + 1) * TILE] = jnp.sum(squares.T, axis=0, keepdims=True)


def join_kernel(count, start, *refs):
    blocks, out = refs[:count], refs[count]
    rows = blocks[0].shape[0]
    for i, block in enumerate(blocks):
        out[i * rows : (i + 1) * rows, :] = block[:, start : start + out.shape[1]]


def beside_kernel(*refs):
    blocks, out = refs[:-1], refs[-1]
    part = blocks[0].shape[1]
    for i, block in enumerate(blocks):
        out[:, i * part : (i + 1) * part] = block[...]


def select_rows(select, blocks, outs):
    @pl.loop(0, outs[0].shape[1] // TILE)
    def _(t):
        at = pl.ds(pl.multiple_of(t * TILE, TILE), TILE)
        rows = jnp.concatenate([b[:, at] for b in blocks], axis=0)
        found = jnp.dot(select, rows, preferred_element_type=F32).astype(BF16)
        top = 0
        for out in outs:
            out[:, at] = found[top : top + out.shape[0], :]
            top += out.shape[0]


def first_pick_kernel(size, chosen_ref, *refs):
    blocks, (share_ref, dense_ref, select_ref) = refs[:-3], refs[-3:]
    slots, share, live = blocks[0].shape[0] // 2, share_ref.shape[0], dense_ref.shape[0]
    picks = chosen_ref.shape[1]
    me = lax.axis_index("mem")
    odd_core = lax.rem(me, 2) == 1
    origins, counts = [], []
    for e, o, block in zip(block_flips(size, False), block_flips(size, True), blocks):
        origin = lax.bitwise_xor(me, jnp.where(odd_core, o, e))
        alive = (block[:, :1].astype(F32) < 1.5).astype(jnp.int32)
        for h in range(2):
            origins.append(lax.bitwise_xor(origin, h))
            counts.append(jnp.sum(alive[h * slots : (h + 1) * slots], axis=0, keepdims=True))
    chosen = chosen_ref[...]
    row = lax.broadcasted_iota(jnp.int32, (share, picks), 0)
    lane = lax.broadcasted_iota(jnp.int32, (share, picks), 1)
    mine = lane == (me // 2) * share + row
    ids = jnp.sum(jnp.where(mine, chosen, 0), axis=1, keepdims=True)
    wanted = jnp.concatenate([ids, lax.broadcasted_iota(jnp.int32, (live, 1), 0)], axis=0)
    across = lax.broadcasted_iota(jnp.int32, (1, 2 * slots), 1)
    for i in range(0, size, 2):
        offsets = []
        for mine in origins[i : i + 2]:
            offset = jnp.zeros((1, 1), jnp.int32)
            for count, origin in zip(counts, origins):
                offset += count * (origin < mine).astype(jnp.int32)
            offsets.append(offset)
        first = across < slots
        within = jnp.where(first, across, across - slots)
        position = within + jnp.where(first, offsets[0], offsets[1])
        alive = within < jnp.where(first, counts[i], counts[i + 1])
        position = jnp.where(alive, position, -1)
        select_ref[:, i * slots : (i + 2) * slots] = (wanted == position).astype(F32).astype(BF16)
    select_rows(select_ref[...], blocks, (share_ref, dense_ref))


def next_pick_kernel(select_ref, *refs):
    select_rows(select_ref[...], refs[:-2], refs[-2:])


def row_norms(rows):
    rows = rows.astype(F32)
    return jnp.sum(rows * rows, axis=1, keepdims=True)


def product(rows, cand):
    return lax.dot_general(rows, cand, (((1,), (1,)), ((), ())), preferred_element_type=F32)


def group_kernel(picks, cand_ref, norm_ref, chosen_ref, own, sib, near_ref, best_ref, rows_ref, cn_ref):
    live, part = own.shape[0], own.shape[1] // CHUNKS
    for c in range(CHUNKS):
        at = slice(c * part, (c + 1) * part)
        rows_ref[:, 2 * c * part : (2 * c + 1) * part] = own[:, at]
        rows_ref[:, (2 * c + 1) * part : (2 * c + 2) * part] = sib[:, at]
    norm = row_norms(own[...]) + row_norms(sib[...])
    cn_ref[...] = norm
    down = lax.broadcasted_iota(jnp.int32, (live, 1), 0)
    hit = jnp.max((chosen_ref[...] == down).astype(F32), axis=1, keepdims=True) > 0.5
    outside = jnp.where(hit, 0.0, jnp.inf)

    @pl.loop(0, cand_ref.shape[0] // TILE)
    def _(t):
        at = pl.ds(pl.multiple_of(t * TILE, TILE), TILE)
        gaps = cn_ref[...] - 2.0 * product(rows_ref[...], cand_ref[at, :])
        near_ref[:, at] = jnp.min(gaps, axis=0, keepdims=True) + norm_ref[:, at]
        best_ref[:, at] = jnp.min(gaps + outside, axis=0, keepdims=True)


def far_rows(size, blocks, early, late, rows_ref):
    rows, part = blocks[0].shape
    last = len(blocks) - 1
    for i, block in enumerate(blocks):
        rows_ref[i * rows : (i + 1) * rows, :part] = block[...]
        top = sibling_place(i, size) * rows
        other = late[...] if i == last else early[i * rows : (i + 1) * rows, :]
        rows_ref[top : top + rows, part:] = other


def far_kernel(size, chunk, cand_ref, *refs):
    before = refs[:1] if chunk else ()
    *blocks, early, late, out, rows_ref = refs[len(before) :]
    far_rows(size, blocks, early, late, rows_ref)
    width = rows_ref.shape[1]
    norm = row_norms(rows_ref[...])

    @pl.loop(0, cand_ref.shape[0] // TILE)
    def _(t):
        at = pl.ds(pl.multiple_of(t * TILE, TILE), TILE)
        inner = product(rows_ref[...], cand_ref[at, chunk * width : (chunk + 1) * width])
        gaps = norm - 2.0 * inner
        for ref in before:
            gaps += ref[:, at]
        out[:, at] = gaps


def last_kernel(size, chunk, cand_ref, best_ref, norm_ref, *refs):
    before = refs[:1] if chunk else ()
    *blocks, early, late, out, rows_ref = refs[len(before) :]
    far_rows(size, blocks, early, late, rows_ref)
    width = rows_ref.shape[1]
    norm = row_norms(rows_ref[...])

    @pl.loop(0, cand_ref.shape[0] // TILE)
    def _(t):
        at = pl.ds(pl.multiple_of(t * TILE, TILE), TILE)
        inner = product(rows_ref[...], cand_ref[at, chunk * width : (chunk + 1) * width])
        gaps = norm - 2.0 * inner
        for ref in before:
            gaps += ref[:, at]
        nearest = jnp.minimum(jnp.min(gaps, axis=0, keepdims=True), best_ref[:, at])
        out[:, at] = nearest + norm_ref[:, at]


def body(candidates, round_one, counts, chosen):
    size, groups = lax.axis_size("mem"), lax.axis_size("grp")
    slots, width = round_one.shape
    half, chips = width // 2, size // 2
    part = half // CHUNKS
    picks, rows = chosen.shape[1], candidates.shape[0]
    share, live = picks // chips, size * slots * 3 // 8
    centers = (groups - 1) * picks

    def bf16(*dims):
        return jax.ShapeDtypeStruct(dims, BF16)

    line = jax.ShapeDtypeStruct((1, rows), F32)
    keep, send = call(
        mark_kernel, "mark", [bf16(slots, half)] * 2, (counts, round_one),
        specs=[pl.BlockSpec(memory_space=pltpu.SMEM)] + vmem_specs(1),
    )
    other = core_permute(send, size)
    cand, norm = call(
        load_kernel, "load", [bf16(rows, width), line], (candidates,),
        specs=[pl.BlockSpec(memory_space=pltpu.HBM)],
        scratch=[pltpu.SemaphoreType.DMA((rows // TILE * 2 * CHUNKS,))], limit=42 * MIB,
    )

    def join(blocks, columns, start=0, after=()):
        count = blocks[0].shape[0] * len(blocks)
        return call(
            functools.partial(join_kernel, len(blocks), start), "join", bf16(count, columns),
            blocks, after=after,
        )

    raw = []
    for c in range(CHUNKS):
        after = (*raw[-1][1:3], norm) if c else ()
        raw.append(gather_chips(join((keep, other), part, c * part, after), size))

    dense, shifted, select = [], [], None
    for c in range(CHUNKS):
        outs = [bf16(share, part), bf16(live, part)]
        flops = 2 * (share + live) * size * slots * part
        if c == 0:
            picked, found, select = call(
                functools.partial(first_pick_kernel, size), "pick_first",
                outs + [bf16(share + live, size * slots)], (chosen, *raw[c]), flops,
            )
        else:
            picked, found = call(
                next_pick_kernel, "pick_next", outs, (select, *raw[c]), flops, after=shifted[-1]
            )
        dense.append(found)
        shifted.append(
            [
                lax.ppermute(picked, "grp", [(g, (g + k) % groups) for g in range(groups)])
                for k in range(1, groups)
            ]
        )

    far, held = [], ()
    for c in range(CHUNKS):
        if c == CHUNKS - 1:
            own = call(
                beside_kernel, "beside", bf16(live, half), dense, after=(*shifted[c], *held[1:3])
            )
            near, best = call(
                functools.partial(group_kernel, picks), "group", [line] * 2,
                (cand, norm, chosen, own, core_permute(own, size)), 2 * rows * live * width,
                scratch=[pltpu.VMEM((live, width), BF16), pltpu.VMEM((live, 1), F32)],
            )
        held = gather_chips(join(shifted[c], part, after=() if c else (picked,)), size)
        early = join(held[:-1], part, after=(best,) if c == CHUNKS - 1 else ())
        far.append((*held, core_permute(early, size), core_permute(held[-1], size)))

    scratch = [pltpu.VMEM((centers, 2 * part), BF16)]
    flops = 2 * rows * centers * 2 * part
    before = ()
    for c in range(CHUNKS - 1):
        before = (
            call(
                functools.partial(far_kernel, size, c), "far",
                jax.ShapeDtypeStruct((centers, rows), F32), (cand, *before, *far[c]), flops,
                scratch=scratch,
            ),
        )
    final = call(
        functools.partial(last_kernel, size, CHUNKS - 1), "far_last", line,
        (cand, best, norm, *before, *far[-1]), flops, scratch=scratch,
    )
    return near.reshape(-1), final.reshape(-1)


def solution(mesh):
    in_specs = (P(("grp", "mem"), None), P(("grp", "mem"), None), P("grp", "mem"), P("grp", None))
    out_specs = (P(("grp", "mem")), P(("grp", "mem")))
    return jax.shard_map(body, mesh=mesh, in_specs=in_specs, out_specs=out_specs, check_vma=False)
```

```python
import functools

import jax
import jax.numpy as jnp
from jax import lax
from jax.experimental import pallas as pl
from jax.experimental.pallas import tpu as pltpu
from jax.sharding import PartitionSpec as P

CHUNKS = 1
TILE = 256
MARK = 2.0
MIB = 1024 * 1024
F32, BF16 = jnp.float32, jnp.bfloat16


def chip_bits(size):
    return [1 << b for b in range(1, size.bit_length() - 1)]


def crossing(size, odd):
    return chip_bits(size)[::-1] if odd else chip_bits(size)


def mixed_permute(block, size, stage):
    even, odd = crossing(size, False)[stage], crossing(size, True)[stage]
    return lax.ppermute(block, "mem", [(m, m ^ (odd if m & 1 else even)) for m in range(size)])


def core_permute(block, size):
    return lax.ppermute(block, "mem", [(m, m ^ 1) for m in range(size)])


def gather_chips(block, size):
    held = [block]
    for stage in range(len(chip_bits(size))):
        held = held + [mixed_permute(b, size, stage) for b in held]
    return held


def block_flips(size, odd):
    flips = [0]
    for bit in crossing(size, odd):
        flips = flips + [f ^ bit for f in flips]
    return flips


def sibling_place(index, size):
    return block_flips(size, True).index(block_flips(size, False)[index])


def vmem_specs(count):
    return [pl.BlockSpec(memory_space=pltpu.VMEM)] * count


def call(
    kernel, name, out_shape, operands, flops=0, specs=None, scratch=(), after=(), limit=28 * MIB
):
    shapes = jax.tree.leaves(out_shape)
    moved = sum(a.size * a.dtype.itemsize for a in list(operands) + shapes)
    count = len(operands)

    def run(*refs):
        kernel(*refs[:count], *refs[count + len(after) :])

    return pl.pallas_call(
        run,
        out_shape=out_shape,
        in_specs=(specs or vmem_specs(count)) + [pl.BlockSpec(memory_space=pl.ANY)] * len(after),
        out_specs=jax.tree.map(lambda _: pl.BlockSpec(memory_space=pltpu.VMEM), out_shape),
        scratch_shapes=scratch,
        compiler_params=pltpu.CompilerParams(vmem_limit_bytes=limit),
        cost_estimate=pl.CostEstimate(flops=flops, bytes_accessed=moved, transcendentals=0),
        name=name,
    )(*operands, *after)


def mark_kernel(count_ref, rows_ref, keep_ref, send_ref):
    slots, half = keep_ref.shape
    core = lax.rem(lax.axis_index("mem"), 2)
    lane = lax.broadcasted_iota(jnp.int32, (slots, 128), 1)
    row = lax.broadcasted_iota(jnp.int32, (slots, 128), 0)
    dead = (lane == 0) & (row >= count_ref[0, 0])
    for out, start in ((keep_ref, core * half), (send_ref, (1 - core) * half)):
        start = pl.multiple_of(start, half)
        first = rows_ref[:, pl.ds(start, 128)].astype(F32)
        out[...] = rows_ref[:, pl.ds(start, half)]
        out[:, :128] = jnp.where(dead, MARK, first).astype(BF16)


def load_kernel(cand_hbm, cand_ref, norm_ref, sems):
    half = cand_ref.shape[1] // 2
    part = half // CHUNKS
    core = lax.rem(lax.axis_index("mem"), 2)
    tiles = cand_ref.shape[0] // TILE
    copies = []
    for t in range(tiles):
        at = pl.ds(t * TILE, TILE)
        for p in range(2 * CHUNKS):
            own = core if p % 2 == 0 else 1 - core
            start = pl.multiple_of(own * half + p // 2 * part, part)
            copies.append(
                pltpu.make_async_copy(
                    cand_hbm.at[at, pl.ds(start, part)],
                    cand_ref.at[at, pl.ds(p * part, part)],
                    sems.at[len(copies)],
                )
            )
    for copy in copies:
        copy.start()
    for t in range(tiles):
        for copy in copies[t * 2 * CHUNKS : (t + 1) * 2 * CHUNKS]:
            copy.wait()
        squares = jnp.zeros((TILE, 128), F32)
        for k in range(0, cand_ref.shape[1], 128):
            entries = cand_ref[t * TILE : (t + 1) * TILE, k : k + 128].astype(F32)
            squares += entries * entries
        norm_ref[:, t * TILE : (t + 1) * TILE] = jnp.sum(squares.T, axis=0, keepdims=True)


def join_kernel(count, start, *refs):
    blocks, out = refs[:count], refs[count]
    rows = blocks[0].shape[0]
    for i, block in enumerate(blocks):
        out[i * rows : (i + 1) * rows, :] = block[:, start : start + out.shape[1]]


def beside_kernel(*refs):
    blocks, out = refs[:-1], refs[-1]
    part = blocks[0].shape[1]
    for i, block in enumerate(blocks):
        out[:, i * part : (i + 1) * part] = block[...]


def select_rows(select, blocks, outs):
    @pl.loop(0, outs[0].shape[1] // TILE)
    def _(t):
        at = pl.ds(pl.multiple_of(t * TILE, TILE), TILE)
        rows = jnp.concatenate([b[:, at] for b in blocks], axis=0)
        found = jnp.dot(select, rows, preferred_element_type=F32).astype(BF16)
        top = 0
        for out in outs:
            out[:, at] = found[top : top + out.shape[0], :]
            top += out.shape[0]


def first_pick_kernel(size, chosen_ref, *refs):
    blocks, (share_ref, dense_ref, select_ref) = refs[:-3], refs[-3:]
    slots, share, live = blocks[0].shape[0] // 2, share_ref.shape[0], dense_ref.shape[0]
    picks = chosen_ref.shape[1]
    me = lax.axis_index("mem")
    odd_core = lax.rem(me, 2) == 1
    origins, counts = [], []
    for e, o, block in zip(block_flips(size, False), block_flips(size, True), blocks):
        origin = lax.bitwise_xor(me, jnp.where(odd_core, o, e))
        alive = (block[:, :1].astype(F32) < 1.5).astype(jnp.int32)
        for h in range(2):
            origins.append(lax.bitwise_xor(origin, h))
            counts.append(jnp.sum(alive[h * slots : (h + 1) * slots], axis=0, keepdims=True))
    chosen = chosen_ref[...]
    row = lax.broadcasted_iota(jnp.int32, (share, picks), 0)
    lane = lax.broadcasted_iota(jnp.int32, (share, picks), 1)
    mine = lane == (me // 2) * share + row
    ids = jnp.sum(jnp.where(mine, chosen, 0), axis=1, keepdims=True)
    wanted = jnp.concatenate([ids, lax.broadcasted_iota(jnp.int32, (live, 1), 0)], axis=0)
    across = lax.broadcasted_iota(jnp.int32, (1, 2 * slots), 1)
    for i in range(0, size, 2):
        offsets = []
        for mine in origins[i : i + 2]:
            offset = jnp.zeros((1, 1), jnp.int32)
            for count, origin in zip(counts, origins):
                offset += count * (origin < mine).astype(jnp.int32)
            offsets.append(offset)
        first = across < slots
        within = jnp.where(first, across, across - slots)
        position = within + jnp.where(first, offsets[0], offsets[1])
        alive = within < jnp.where(first, counts[i], counts[i + 1])
        position = jnp.where(alive, position, -1)
        select_ref[:, i * slots : (i + 2) * slots] = (wanted == position).astype(F32).astype(BF16)
    select_rows(select_ref[...], blocks, (share_ref, dense_ref))


def next_pick_kernel(select_ref, *refs):
    select_rows(select_ref[...], refs[:-2], refs[-2:])


def row_norms(rows):
    rows = rows.astype(F32)
    return jnp.sum(rows * rows, axis=1, keepdims=True)


def product(rows, cand):
    return lax.dot_general(rows, cand, (((1,), (1,)), ((), ())), preferred_element_type=F32)


def group_kernel(picks, cand_ref, norm_ref, chosen_ref, own, sib, near_ref, best_ref, rows_ref, cn_ref):
    live, part = own.shape[0], own.shape[1] // CHUNKS
    for c in range(CHUNKS):
        at = slice(c * part, (c + 1) * part)
        rows_ref[:, 2 * c * part : (2 * c + 1) * part] = own[:, at]
        rows_ref[:, (2 * c + 1) * part : (2 * c + 2) * part] = sib[:, at]
    norm = row_norms(own[...]) + row_norms(sib[...])
    cn_ref[...] = norm
    down = lax.broadcasted_iota(jnp.int32, (live, 1), 0)
    hit = jnp.max((chosen_ref[...] == down).astype(F32), axis=1, keepdims=True) > 0.5
    outside = jnp.where(hit, 0.0, jnp.inf)

    @pl.loop(0, cand_ref.shape[0] // TILE)
    def _(t):
        at = pl.ds(pl.multiple_of(t * TILE, TILE), TILE)
        gaps = cn_ref[...] - 2.0 * product(rows_ref[...], cand_ref[at, :])
        near_ref[:, at] = jnp.min(gaps, axis=0, keepdims=True) + norm_ref[:, at]
        best_ref[:, at] = jnp.min(gaps + outside, axis=0, keepdims=True)


def far_rows(size, blocks, early, late, rows_ref):
    rows, part = blocks[0].shape
    last = len(blocks) - 1
    for i, block in enumerate(blocks):
        rows_ref[i * rows : (i + 1) * rows, :part] = block[...]
        top = sibling_place(i, size) * rows
        other = late[...] if i == last else early[i * rows : (i + 1) * rows, :]
        rows_ref[top : top + rows, part:] = other


def far_kernel(size, chunk, cand_ref, *refs):
    before = refs[:1] if chunk else ()
    *blocks, early, late, out, rows_ref = refs[len(before) :]
    far_rows(size, blocks, early, late, rows_ref)
    width = rows_ref.shape[1]
    norm = row_norms(rows_ref[...])

    @pl.loop(0, cand_ref.shape[0] // TILE)
    def _(t):
        at = pl.ds(pl.multiple_of(t * TILE, TILE), TILE)
        inner = product(rows_ref[...], cand_ref[at, chunk * width : (chunk + 1) * width])
        gaps = norm - 2.0 * inner
        for ref in before:
            gaps += ref[:, at]
        out[:, at] = gaps


def last_kernel(size, chunk, cand_ref, best_ref, norm_ref, *refs):
    before = refs[:1] if chunk else ()
    *blocks, early, late, out, rows_ref = refs[len(before) :]
    far_rows(size, blocks, early, late, rows_ref)
    width = rows_ref.shape[1]
    norm = row_norms(rows_ref[...])

    @pl.loop(0, cand_ref.shape[0] // TILE)
    def _(t):
        at = pl.ds(pl.multiple_of(t * TILE, TILE), TILE)
        inner = product(rows_ref[...], cand_ref[at, chunk * width : (chunk + 1) * width])
        gaps = norm - 2.0 * inner
        for ref in before:
            gaps += ref[:, at]
        nearest = jnp.minimum(jnp.min(gaps, axis=0, keepdims=True), best_ref[:, at])
        out[:, at] = nearest + norm_ref[:, at]


def body(candidates, round_one, counts, chosen):
    size, groups = lax.axis_size("mem"), lax.axis_size("grp")
    slots, width = round_one.shape
    half, chips = width // 2, size // 2
    part = half // CHUNKS
    picks, rows = chosen.shape[1], candidates.shape[0]
    share, live = picks // chips, size * slots * 3 // 8
    centers = (groups - 1) * picks

    def bf16(*dims):
        return jax.ShapeDtypeStruct(dims, BF16)

    line = jax.ShapeDtypeStruct((1, rows), F32)
    keep, send = call(
        mark_kernel, "mark", [bf16(slots, half)] * 2, (counts, round_one),
        specs=[pl.BlockSpec(memory_space=pltpu.SMEM)] + vmem_specs(1),
    )
    other = core_permute(send, size)
    cand, norm = call(
        load_kernel, "load", [bf16(rows, width), line], (candidates,),
        specs=[pl.BlockSpec(memory_space=pltpu.HBM)],
        scratch=[pltpu.SemaphoreType.DMA((rows // TILE * 2 * CHUNKS,))], limit=42 * MIB,
    )

    def join(blocks, columns, start=0, after=()):
        count = blocks[0].shape[0] * len(blocks)
        return call(
            functools.partial(join_kernel, len(blocks), start), "join", bf16(count, columns),
            blocks, after=after,
        )

    raw = []
    for c in range(CHUNKS):
        after = (*raw[-1][1:3], norm) if c else ()
        raw.append(gather_chips(join((keep, other), part, c * part, after), size))

    dense, shifted, select = [], [], None
    for c in range(CHUNKS):
        outs = [bf16(share, part), bf16(live, part)]
        flops = 2 * (share + live) * size * slots * part
        if c == 0:
            picked, found, select = call(
                functools.partial(first_pick_kernel, size), "pick_first",
                outs + [bf16(share + live, size * slots)], (chosen, *raw[c]), flops, after=(norm,),
            )
        else:
            picked, found = call(
                next_pick_kernel, "pick_next", outs, (select, *raw[c]), flops, after=shifted[-1]
            )
        dense.append(found)
        shifted.append(
            [
                lax.ppermute(picked, "grp", [(g, (g + k) % groups) for g in range(groups)])
                for k in range(1, groups)
            ]
        )

    far, held = [], ()
    for c in range(CHUNKS):
        if c == CHUNKS - 1:
            own = dense[0]
            if c:
                after = (*shifted[c], *held[1:3])
                own = call(beside_kernel, "beside", bf16(live, half), dense, after=after)
            near, best = call(
                functools.partial(group_kernel, picks), "group", [line] * 2,
                (cand, norm, chosen, own, core_permute(own, size)), 2 * rows * live * width,
                scratch=[pltpu.VMEM((live, width), BF16), pltpu.VMEM((live, 1), F32)],
            )
        after = (best,) if CHUNKS == 1 else () if c else (picked,)
        held = gather_chips(join(shifted[c], part, after=after), size)
        early = join(held[:-1], part, after=(best,) if c == CHUNKS - 1 else ())
        far.append((*held, core_permute(early, size), core_permute(held[-1], size)))

    scratch = [pltpu.VMEM((centers, 2 * part), BF16)]
    flops = 2 * rows * centers * 2 * part
    before = ()
    for c in range(CHUNKS - 1):
        before = (
            call(
                functools.partial(far_kernel, size, c), "far",
                jax.ShapeDtypeStruct((centers, rows), F32), (cand, *before, *far[c]), flops,
                scratch=scratch,
            ),
        )
    final = call(
        functools.partial(last_kernel, size, CHUNKS - 1), "far_last", line,
        (cand, best, norm, *before, *far[-1]), flops, scratch=scratch,
    )
    return near.reshape(-1), final.reshape(-1)


def solution(mesh):
    in_specs = (P(("grp", "mem"), None), P(("grp", "mem"), None), P("grp", "mem"), P("grp", None))
    out_specs = (P(("grp", "mem")), P(("grp", "mem")))
    return jax.shard_map(body, mesh=mesh, in_specs=in_specs, out_specs=out_specs, check_vma=False)
```

```python
import functools

import jax
import jax.numpy as jnp
from jax import lax
from jax.experimental import pallas as pl
from jax.experimental.pallas import tpu as pltpu
from jax.sharding import PartitionSpec as P

CHUNKS = 2
TILE = 256
MARK = 2.0
WEIGHT = 10**10
MIB = 1024 * 1024
F32, BF16 = jnp.float32, jnp.bfloat16


def chip_bits(size):
    return [1 << b for b in range(1, size.bit_length() - 1)]


def crossing(size, odd):
    return chip_bits(size)[::-1] if odd else chip_bits(size)


def mixed_permute(block, size, stage):
    even, odd = crossing(size, False)[stage], crossing(size, True)[stage]
    return lax.ppermute(block, "mem", [(m, m ^ (odd if m & 1 else even)) for m in range(size)])


def core_permute(block, size):
    return lax.ppermute(block, "mem", [(m, m ^ 1) for m in range(size)])


def block_flips(size, odd):
    flips = [0]
    for bit in crossing(size, odd):
        flips = flips + [f ^ bit for f in flips]
    return flips


def sibling_place(index, size):
    return block_flips(size, True).index(block_flips(size, False)[index])


def vmem_specs(count):
    return [pl.BlockSpec(memory_space=pltpu.VMEM)] * count


def call(
    kernel, name, out_shape, operands, flops=0, specs=None, scratch=(), after=(), limit=28 * MIB
):
    shapes = jax.tree.leaves(out_shape)
    moved = sum(a.size * a.dtype.itemsize for a in list(operands) + shapes)
    count = len(operands)

    def run(*refs):
        kernel(*refs[:count], *refs[count + len(after) :])

    return pl.pallas_call(
        run,
        out_shape=out_shape,
        in_specs=(specs or vmem_specs(count)) + [pl.BlockSpec(memory_space=pl.ANY)] * len(after),
        out_specs=jax.tree.map(lambda _: pl.BlockSpec(memory_space=pltpu.VMEM), out_shape),
        scratch_shapes=scratch,
        compiler_params=pltpu.CompilerParams(vmem_limit_bytes=limit),
        cost_estimate=pl.CostEstimate(flops=flops, bytes_accessed=moved, transcendentals=0),
        name=name,
    )(*operands, *after)


def mark_kernel(count_ref, rows_ref, keep_ref, send_ref):
    slots, half = keep_ref.shape
    core = lax.rem(lax.axis_index("mem"), 2)
    lane = lax.broadcasted_iota(jnp.int32, (slots, 128), 1)
    row = lax.broadcasted_iota(jnp.int32, (slots, 128), 0)
    dead = (lane == 0) & (row >= count_ref[0, 0])
    for out, start in ((keep_ref, core * half), (send_ref, (1 - core) * half)):
        start = pl.multiple_of(start, half)
        first = rows_ref[:, pl.ds(start, 128)].astype(F32)
        out[...] = rows_ref[:, pl.ds(start, half)]
        out[:, :128] = jnp.where(dead, MARK, first).astype(BF16)


def load_kernel(cand_hbm, cand_ref, norm_ref, sems):
    half = cand_ref.shape[1] // 2
    part = half // CHUNKS
    core = lax.rem(lax.axis_index("mem"), 2)
    tiles = cand_ref.shape[0] // TILE
    copies = []
    for t in range(tiles):
        at = pl.ds(t * TILE, TILE)
        for p in range(2 * CHUNKS):
            own = core if p % 2 == 0 else 1 - core
            start = pl.multiple_of(own * half + p // 2 * part, part)
            copies.append(
                pltpu.make_async_copy(
                    cand_hbm.at[at, pl.ds(start, part)],
                    cand_ref.at[at, pl.ds(p * part, part)],
                    sems.at[len(copies)],
                )
            )
    for copy in copies:
        copy.start()
    for t in range(tiles):
        for copy in copies[t * 2 * CHUNKS : (t + 1) * 2 * CHUNKS]:
            copy.wait()
        squares = jnp.zeros((TILE, 128), F32)
        for k in range(0, cand_ref.shape[1], 128):
            entries = cand_ref[t * TILE : (t + 1) * TILE, k : k + 128].astype(F32)
            squares += entries * entries
        norm_ref[:, t * TILE : (t + 1) * TILE] = jnp.sum(squares.T, axis=0, keepdims=True)


def join_kernel(count, start, *refs):
    blocks, out = refs[:count], refs[count]
    rows = blocks[0].shape[0]
    for i, block in enumerate(blocks):
        out[i * rows : (i + 1) * rows, :] = block[:, start : start + out.shape[1]]


def beside_kernel(*refs):
    blocks, out = refs[:-1], refs[-1]
    part = blocks[0].shape[1]
    for i, block in enumerate(blocks):
        out[:, i * part : (i + 1) * part] = block[...]


def select_rows(select, blocks, outs):
    @pl.loop(0, outs[0].shape[1] // TILE)
    def _(t):
        at = pl.ds(pl.multiple_of(t * TILE, TILE), TILE)
        rows = jnp.concatenate([b[:, at] for b in blocks], axis=0)
        found = jnp.dot(select, rows, preferred_element_type=F32).astype(BF16)
        top = 0
        for out in outs:
            out[:, at] = found[top : top + out.shape[0], :]
            top += out.shape[0]


def first_pick_kernel(size, chosen_ref, *refs):
    blocks, (share_ref, dense_ref, select_ref) = refs[:-3], refs[-3:]
    slots, share, live = blocks[0].shape[0] * 2 // size, share_ref.shape[0], dense_ref.shape[0]
    picks = chosen_ref.shape[1]
    me = lax.axis_index("mem")
    odd_core = lax.rem(me, 2) == 1
    origins, counts = [], []
    for e, o in zip(block_flips(size, False), block_flips(size, True)):
        origin = lax.bitwise_xor(me, jnp.where(odd_core, o, e))
        origins += [origin, lax.bitwise_xor(origin, 1)]
    for block in blocks:
        alive = (block[:, :1].astype(F32) < 1.5).astype(jnp.int32)
        for top in range(0, block.shape[0], slots):
            counts.append(jnp.sum(alive[top : top + slots], axis=0, keepdims=True))
    chosen = chosen_ref[...]
    row = lax.broadcasted_iota(jnp.int32, (share, picks), 0)
    lane = lax.broadcasted_iota(jnp.int32, (share, picks), 1)
    mine = lane == (me // 2) * share + row
    ids = jnp.sum(jnp.where(mine, chosen, 0), axis=1, keepdims=True)
    wanted = jnp.concatenate([ids, lax.broadcasted_iota(jnp.int32, (live, 1), 0)], axis=0)
    across = lax.broadcasted_iota(jnp.int32, (1, 2 * slots), 1)
    for i in range(0, size, 2):
        offsets = []
        for mine in origins[i : i + 2]:
            offset = jnp.zeros((1, 1), jnp.int32)
            for count, origin in zip(counts, origins):
                offset += count * (origin < mine).astype(jnp.int32)
            offsets.append(offset)
        first = across < slots
        within = jnp.where(first, across, across - slots)
        position = within + jnp.where(first, offsets[0], offsets[1])
        alive = within < jnp.where(first, counts[i], counts[i + 1])
        position = jnp.where(alive, position, -1)
        select_ref[:, i * slots : (i + 2) * slots] = (wanted == position).astype(F32).astype(BF16)
    select_rows(select_ref[...], blocks, (share_ref, dense_ref))


def next_pick_kernel(select_ref, *refs):
    select_rows(select_ref[...], refs[:-2], refs[-2:])


def lane_norms(rows_ref, width):
    squares = jnp.zeros((rows_ref.shape[0], 128), F32)
    for k in range(0, width, 128):
        entries = rows_ref[:, k : k + 128].astype(F32)
        squares += entries * entries
    return jnp.sum(squares.T, axis=0, keepdims=True)


def gaps_to(cand, rows_ref, norms):
    inner = lax.dot_general(
        cand, rows_ref[...], (((1,), (1,)), ((), ())), preferred_element_type=F32
    )
    return norms - 2.0 * inner


def nearest(gaps):
    least = gaps[:, :128]
    for k in range(128, gaps.shape[1], 128):
        least = jnp.minimum(least, gaps[:, k : k + 128])
    return jnp.min(least.T, axis=0, keepdims=True)


def group_kernel(picks, cand_ref, norm_ref, chosen_ref, own, sib, near_ref, best_ref, rows_ref):
    live, part = own.shape[0], own.shape[1] // CHUNKS
    for c in range(CHUNKS):
        at = slice(c * part, (c + 1) * part)
        rows_ref[:live, 2 * c * part : (2 * c + 1) * part] = own[:, at]
        rows_ref[:live, (2 * c + 1) * part : (2 * c + 2) * part] = sib[:, at]
    padded = rows_ref.shape[0]
    if padded > live:
        rows_ref[live:, :] = jnp.zeros((padded - live, rows_ref.shape[1]), BF16)
    lane = lax.broadcasted_iota(jnp.int32, (1, padded), 1)
    norms = jnp.where(lane < live, lane_norms(rows_ref, rows_ref.shape[1]), jnp.inf)
    row = lax.broadcasted_iota(jnp.int32, (padded, picks), 0)
    hit = (chosen_ref[...] == row).astype(F32)
    hits = jnp.zeros((1, padded), F32)
    for k in range(0, picks, 128):
        hits += jnp.sum(hit[:, k : k + 128].T, axis=0, keepdims=True)
    outside = jnp.where(hits > 0.5, 0.0, jnp.inf)

    @pl.loop(0, cand_ref.shape[0] // TILE)
    def _(t):
        at = pl.ds(pl.multiple_of(t * TILE, TILE), TILE)
        gaps = gaps_to(cand_ref[at, :], rows_ref, norms)
        near_ref[:, at] = nearest(gaps) + norm_ref[:, at]
        best_ref[:, at] = nearest(gaps + outside)


def far_rows(size, held, sibs, rows_ref):
    rows, part = rows_ref.shape[0] // (size // 2), held[0].shape[1]
    for i, block in enumerate(held):
        top = i * block.shape[0]
        rows_ref[top : top + block.shape[0], :part] = block[...]
    for i in range(size // 2):
        block = sibs[i * rows // sibs[0].shape[0]]
        top = i * rows % sibs[0].shape[0]
        to = sibling_place(i, size) * rows
        rows_ref[to : to + rows, part:] = block[top : top + rows, :]


def far_kernel(size, chunk, cand_ref, *refs):
    before = refs[:1] if chunk else ()
    *blocks, out, rows_ref = refs[len(before) :]
    far_rows(size, blocks[:2], blocks[2:], rows_ref)
    width = rows_ref.shape[1]
    norms = lane_norms(rows_ref, width)

    @pl.loop(0, cand_ref.shape[0] // TILE)
    def _(t):
        at = pl.ds(pl.multiple_of(t * TILE, TILE), TILE)
        gaps = gaps_to(cand_ref[at, chunk * width : (chunk + 1) * width], rows_ref, norms)
        for ref in before:
            gaps += ref[at, :]
        out[at, :] = gaps


def last_kernel(size, chunk, cand_ref, best_ref, norm_ref, *refs):
    before = refs[:1] if chunk else ()
    *blocks, out, rows_ref = refs[len(before) :]
    far_rows(size, blocks[:2], blocks[2:], rows_ref)
    width = rows_ref.shape[1]
    norms = lane_norms(rows_ref, width)

    @pl.loop(0, cand_ref.shape[0] // TILE)
    def _(t):
        at = pl.ds(pl.multiple_of(t * TILE, TILE), TILE)
        gaps = gaps_to(cand_ref[at, chunk * width : (chunk + 1) * width], rows_ref, norms)
        for ref in before:
            gaps += ref[at, :]
        out[:, at] = jnp.minimum(nearest(gaps), best_ref[:, at]) + norm_ref[:, at]


def body(candidates, round_one, counts, chosen):
    size, groups = lax.axis_size("mem"), lax.axis_size("grp")
    slots, width = round_one.shape
    half, chips = width // 2, size // 2
    part = half // CHUNKS
    picks, rows = chosen.shape[1], candidates.shape[0]
    share, live = picks // chips, size * slots * 3 // 8
    centers = (groups - 1) * picks

    def bf16(*dims):
        return jax.ShapeDtypeStruct(dims, BF16)

    line = jax.ShapeDtypeStruct((1, rows), F32)
    keep, send = call(
        mark_kernel, "mark", [bf16(slots, half)] * 2, (counts, round_one),
        specs=[pl.BlockSpec(memory_space=pltpu.SMEM)] + vmem_specs(1),
    )
    other = core_permute(send, size)

    def join(blocks, columns, start=0, after=(), weight=0):
        count = blocks[0].shape[0] * len(blocks)
        return call(
            functools.partial(join_kernel, len(blocks), start), "join", bf16(count, columns),
            blocks, weight, after=after,
        )

    def double(block, got, stages, after=(), weight=0):
        for stage in stages:
            block = join((block, got), block.shape[1], after=after, weight=weight)
            got = mixed_permute(block, size, stage)
        return block, got

    stages = range(1, len(chip_bits(size)))
    first = [join((keep, other), part, c * part) for c in range(CHUNKS)]
    got = [mixed_permute(block, size, 0) for block in first]
    raw = [double(first[0], got[0], stages)]
    cand, norm = call(
        load_kernel, "load", [bf16(rows, width), line], (candidates,),
        specs=[pl.BlockSpec(memory_space=pltpu.HBM)], after=raw[0][:1],
        scratch=[pltpu.SemaphoreType.DMA((rows // TILE * 2 * CHUNKS,))], limit=42 * MIB,
    )
    raw += [double(f, g, stages, after=(norm,)) for f, g in zip(first[1:], got[1:])]

    dense, shifted, select = [], [], None
    for c in range(CHUNKS):
        outs = [bf16(share, part), bf16(live, part)]
        flops = 2 * (share + live) * size * slots * part
        if c == 0:
            picked, found, select = call(
                functools.partial(first_pick_kernel, size), "pick_first",
                outs + [bf16(share + live, size * slots)], (chosen, *raw[c]), flops,
                after=(norm,),
            )
        else:
            picked, found = call(
                next_pick_kernel, "pick_next", outs, (select, *raw[c]), flops, after=shifted[-1]
            )
        dense.append(found)
        shifted.append(
            [
                lax.ppermute(picked, "grp", [(g, (g + k) % groups) for g in range(groups)])
                for k in range(1, groups)
            ]
        )

    scratch = [pltpu.VMEM((centers, 2 * part), BF16)]
    flops = 2 * rows * centers * 2 * part
    before, best, final = (), None, None
    for c in range(CHUNKS):
        block = join(shifted[c], part, after=() if c else (picked,))
        got = mixed_permute(block, size, 0)
        if c == CHUNKS - 1:
            own = call(beside_kernel, "beside", bf16(live, half), dense)
            near, best = call(
                functools.partial(group_kernel, picks), "group", [line] * 2,
                (cand, norm, chosen, own, core_permute(own, size)), 2 * rows * live * width,
                scratch=[pltpu.VMEM((-(-live // 128) * 128, width), BF16)], after=(block,),
            )
        weight = WEIGHT if c < CHUNKS - 1 else 0
        mine, got = double(block, got, stages, after=(best,) if best is not None else (), weight=weight)
        sent = join((got,), part, after=before) if before else got
        blocks = (mine, got, core_permute(mine, size), core_permute(sent, size))
        if c < CHUNKS - 1:
            before = (
                call(
                    functools.partial(far_kernel, size, c), "far",
                    jax.ShapeDtypeStruct((rows, centers), F32), (cand, *before, *blocks), flops,
                    scratch=scratch,
                ),
            )
        else:
            final = call(
                functools.partial(last_kernel, size, c), "far_last", line,
                (cand, best, norm, *before, *blocks), flops, scratch=scratch,
            )
    return near.reshape(-1), final.reshape(-1)


def solution(mesh):
    in_specs = (P(("grp", "mem"), None), P(("grp", "mem"), None), P("grp", "mem"), P("grp", None))
    out_specs = (P(("grp", "mem")), P(("grp", "mem")))
    return jax.shard_map(body, mesh=mesh, in_specs=in_specs, out_specs=out_specs, check_vma=False)
```

```python
import functools

import jax
import jax.numpy as jnp
from jax import lax
from jax.experimental import pallas as pl
from jax.experimental.pallas import tpu as pltpu
from jax.sharding import PartitionSpec as P

CHUNKS = 2
TILE = 256
MARK = 2.0
MIB = 1024 * 1024
WEIGHT = 10**10
F32, BF16 = jnp.float32, jnp.bfloat16


def chip_bits(size):
    return [1 << b for b in range(1, size.bit_length() - 1)]


def crossing(size, odd):
    return chip_bits(size)[::-1] if odd else chip_bits(size)


def mixed_permute(block, size, stage):
    even, odd = crossing(size, False)[stage], crossing(size, True)[stage]
    return lax.ppermute(block, "mem", [(m, m ^ (odd if m & 1 else even)) for m in range(size)])


def core_permute(block, size):
    return lax.ppermute(block, "mem", [(m, m ^ 1) for m in range(size)])


def block_flips(size, odd):
    flips = [0]
    for bit in crossing(size, odd):
        flips = flips + [f ^ bit for f in flips]
    return flips


def sibling_place(index, size):
    return block_flips(size, True).index(block_flips(size, False)[index])


def vmem_specs(count):
    return [pl.BlockSpec(memory_space=pltpu.VMEM)] * count


def call(
    kernel, name, out_shape, operands, flops=0, specs=None, scratch=(), after=(), limit=28 * MIB
):
    shapes = jax.tree.leaves(out_shape)
    moved = sum(a.size * a.dtype.itemsize for a in list(operands) + shapes)
    count = len(operands)

    def run(*refs):
        kernel(*refs[:count], *refs[count + len(after) :])

    return pl.pallas_call(
        run,
        out_shape=out_shape,
        in_specs=(specs or vmem_specs(count)) + [pl.BlockSpec(memory_space=pl.ANY)] * len(after),
        out_specs=jax.tree.map(lambda _: pl.BlockSpec(memory_space=pltpu.VMEM), out_shape),
        scratch_shapes=scratch,
        compiler_params=pltpu.CompilerParams(vmem_limit_bytes=limit),
        cost_estimate=pl.CostEstimate(flops=WEIGHT, bytes_accessed=moved, transcendentals=0),
        name=name,
    )(*operands, *after)


def mark_kernel(count_ref, rows_ref, keep_ref, send_ref):
    slots, half = keep_ref.shape
    core = lax.rem(lax.axis_index("mem"), 2)
    lane = lax.broadcasted_iota(jnp.int32, (slots, 128), 1)
    row = lax.broadcasted_iota(jnp.int32, (slots, 128), 0)
    dead = (lane == 0) & (row >= count_ref[...])
    for out, start in ((keep_ref, core * half), (send_ref, (1 - core) * half)):
        start = pl.multiple_of(start, half)
        first = rows_ref[:, pl.ds(start, 128)].astype(F32)
        out[...] = rows_ref[:, pl.ds(start, half)]
        out[:, :128] = jnp.where(dead, MARK, first).astype(BF16)


def load_kernel(cand_hbm, cand_ref, norm_ref, tile_ref, sems):
    width, rows = cand_ref.shape
    half, part = width // 2, width // (2 * CHUNKS)
    core = lax.rem(lax.axis_index("mem"), 2)
    copies = []
    for t in range(rows // TILE):
        for p in range(2 * CHUNKS):
            own = core if p % 2 == 0 else 1 - core
            start = pl.multiple_of(own * half + p // 2 * part, part)
            copies.append(
                pltpu.make_async_copy(
                    cand_hbm.at[pl.ds(t * TILE, TILE), pl.ds(start, part)],
                    tile_ref.at[pl.ds(t * TILE, TILE), pl.ds(p * part, part)],
                    sems.at[len(copies)],
                )
            )
    for copy in copies:
        copy.start()
    for t in range(rows // TILE):
        at = slice(t * TILE, (t + 1) * TILE)
        for copy in copies[t * 2 * CHUNKS : (t + 1) * 2 * CHUNKS]:
            copy.wait()

        def turn(k, squares, at=at):
            columns = pl.ds(pl.multiple_of(k * TILE, TILE), TILE)
            turned = tile_ref[at, columns].T
            cand_ref[columns, at] = turned
            entries = turned.astype(F32)
            return squares + jnp.sum(entries * entries, axis=0, keepdims=True)

        norm_ref[:, at] = lax.fori_loop(0, width // TILE, turn, jnp.zeros((1, TILE), F32))


def join_kernel(count, start, *refs):
    blocks, out = refs[:count], refs[count]
    rows = blocks[0].shape[0]
    for i, block in enumerate(blocks):
        out[i * rows : (i + 1) * rows, :] = block[:, start : start + out.shape[1]]


def beside_kernel(*refs):
    blocks, out = refs[:-1], refs[-1]
    part = blocks[0].shape[1]
    for i, block in enumerate(blocks):
        out[:, i * part : (i + 1) * part] = block[...]


def select_rows(select, blocks, outs):
    @pl.loop(0, outs[0].shape[1] // TILE)
    def _(t):
        at = pl.ds(pl.multiple_of(t * TILE, TILE), TILE)
        rows = jnp.concatenate([b[:, at] for b in blocks], axis=0)
        found = jnp.dot(select, rows, preferred_element_type=F32).astype(BF16)
        top = 0
        for out in outs:
            out[:, at] = found[top : top + out.shape[0], :]
            top += out.shape[0]


def first_pick_kernel(size, chosen_ref, *refs):
    blocks, (share_ref, dense_ref, select_ref) = refs[:-3], refs[-3:]
    slots, share, live = blocks[0].shape[0] * 2 // size, share_ref.shape[0], dense_ref.shape[0]
    picks = chosen_ref.shape[1]
    me = lax.axis_index("mem")
    odd_core = lax.rem(me, 2) == 1
    origins, counts = [], []
    for e, o in zip(block_flips(size, False), block_flips(size, True)):
        origin = lax.bitwise_xor(me, jnp.where(odd_core, o, e))
        origins += [origin, lax.bitwise_xor(origin, 1)]
    for block in blocks:
        alive = (block[:, :1].astype(F32) < 1.5).astype(jnp.int32)
        for top in range(0, block.shape[0], slots):
            counts.append(jnp.sum(alive[top : top + slots], axis=0, keepdims=True))
    chosen = chosen_ref[...]
    row = lax.broadcasted_iota(jnp.int32, (share, picks), 0)
    lane = lax.broadcasted_iota(jnp.int32, (share, picks), 1)
    mine = lane == (me // 2) * share + row
    ids = jnp.sum(jnp.where(mine, chosen, 0), axis=1, keepdims=True)
    wanted = jnp.concatenate([ids, lax.broadcasted_iota(jnp.int32, (live, 1), 0)], axis=0)
    across = lax.broadcasted_iota(jnp.int32, (1, 2 * slots), 1)
    for i in range(0, size, 2):
        offsets = []
        for mine in origins[i : i + 2]:
            offset = jnp.zeros((1, 1), jnp.int32)
            for count, origin in zip(counts, origins):
                offset += count * (origin < mine).astype(jnp.int32)
            offsets.append(offset)
        first = across < slots
        within = jnp.where(first, across, across - slots)
        position = within + jnp.where(first, offsets[0], offsets[1])
        alive = within < jnp.where(first, counts[i], counts[i + 1])
        position = jnp.where(alive, position, -1)
        select_ref[:, i * slots : (i + 2) * slots] = (wanted == position).astype(F32).astype(BF16)
    select_rows(select_ref[...], blocks, (share_ref, dense_ref))


def next_pick_kernel(select_ref, *refs):
    select_rows(select_ref[...], refs[:-2], refs[-2:])


def row_norms(rows):
    rows = rows.astype(F32)
    return jnp.sum(rows * rows, axis=1, keepdims=True)


def product(rows, cand):
    return jnp.dot(rows, cand, preferred_element_type=F32)


def group_kernel(picks, cand_ref, norm_ref, chosen_ref, own, sib, near_ref, best_ref, rows_ref):
    live, part = own.shape[0], own.shape[1] // CHUNKS
    for c in range(CHUNKS):
        at = slice(c * part, (c + 1) * part)
        rows_ref[:, 2 * c * part : (2 * c + 1) * part] = own[:, at]
        rows_ref[:, (2 * c + 1) * part : (2 * c + 2) * part] = sib[:, at]
    norms = row_norms(rows_ref[...])
    down = lax.broadcasted_iota(jnp.int32, (live, 1), 0)
    hit = jnp.max((chosen_ref[...] == down).astype(F32), axis=1, keepdims=True) > 0.5
    outside = jnp.where(hit, 0.0, jnp.inf)

    @pl.loop(0, cand_ref.shape[1] // TILE)
    def _(t):
        at = pl.ds(pl.multiple_of(t * TILE, TILE), TILE)
        gaps = norms - 2.0 * product(rows_ref[...], cand_ref[:, at])
        near_ref[:, at] = jnp.min(gaps, axis=0, keepdims=True) + norm_ref[:, at]
        best_ref[:, at] = jnp.min(gaps + outside, axis=0, keepdims=True)


def far_rows(size, held, sibs, rows_ref):
    rows, part = rows_ref.shape[0] // (size // 2), held[0].shape[1]
    for i, block in enumerate(held):
        top = i * block.shape[0]
        rows_ref[top : top + block.shape[0], :part] = block[...]
    for i in range(size // 2):
        block = sibs[i * rows // sibs[0].shape[0]]
        top = i * rows % sibs[0].shape[0]
        to = sibling_place(i, size) * rows
        rows_ref[to : to + rows, part:] = block[top : top + rows, :]


def far_gaps(size, chunk, cand_ref, before, blocks, rows_ref, emit):
    far_rows(size, blocks[:2], blocks[2:], rows_ref)
    width = rows_ref.shape[1]
    norms = row_norms(rows_ref[...])

    @pl.loop(0, cand_ref.shape[1] // TILE)
    def _(t):
        at = pl.ds(pl.multiple_of(t * TILE, TILE), TILE)
        gaps = norms - 2.0 * product(
            rows_ref[...], cand_ref[chunk * width : (chunk + 1) * width, at]
        )
        for ref in before:
            gaps += ref[:, at]
        emit(at, gaps)


def far_kernel(size, chunk, cand_ref, *refs):
    *before, mine, got, sib_mine, sib_got, out, rows_ref = refs

    def emit(at, gaps):
        out[:, at] = gaps

    far_gaps(size, chunk, cand_ref, before, (mine, got, sib_mine, sib_got), rows_ref, emit)


def last_kernel(size, chunk, cand_ref, best_ref, norm_ref, *refs):
    *before, mine, got, sib_mine, sib_got, out, rows_ref = refs

    def emit(at, gaps):
        least = jnp.minimum(jnp.min(gaps, axis=0, keepdims=True), best_ref[:, at])
        out[:, at] = least + norm_ref[:, at]

    far_gaps(size, chunk, cand_ref, before, (mine, got, sib_mine, sib_got), rows_ref, emit)


def body(candidates, round_one, counts, chosen):
    size, groups = lax.axis_size("mem"), lax.axis_size("grp")
    slots, width = round_one.shape
    half, chips = width // 2, size // 2
    part = half // CHUNKS
    picks, rows = chosen.shape[1], candidates.shape[0]
    share, live = picks // chips, size * slots * 3 // 8
    centers = (groups - 1) * picks

    def bf16(*dims):
        return jax.ShapeDtypeStruct(dims, BF16)

    line = jax.ShapeDtypeStruct((1, rows), F32)
    keep, send = call(
        mark_kernel, "mark", [bf16(slots, half)] * 2, (counts, round_one)
    )
    other = core_permute(send, size)

    def join(blocks, columns, start=0, after=()):
        count = blocks[0].shape[0] * len(blocks)
        return call(
            functools.partial(join_kernel, len(blocks), start), "join", bf16(count, columns),
            blocks, after=after,
        )

    def double(block, got, stages, after=()):
        for stage in stages:
            block = join((block, got), block.shape[1], after=after)
            got = mixed_permute(block, size, stage)
        return block, got

    stages = range(1, len(chip_bits(size)))
    first = [join((keep, other), part, c * part) for c in range(CHUNKS)]
    got = [mixed_permute(block, size, 0) for block in first]
    raw = [double(first[0], got[0], stages)]
    cand, norm = call(
        load_kernel, "load", [bf16(width, rows), line], (candidates,),
        specs=[pl.BlockSpec(memory_space=pltpu.HBM)], after=raw[0][:1],
        scratch=[
            pltpu.VMEM((rows, width), BF16),
            pltpu.SemaphoreType.DMA((rows // TILE * 2 * CHUNKS,)),
        ],
        limit=42 * MIB,
    )
    raw += [double(f, g, stages, after=(norm,)) for f, g in zip(first[1:], got[1:])]

    dense, shifted, select = [], [], None
    for c in range(CHUNKS):
        outs = [bf16(share, part), bf16(live, part)]
        flops = 2 * (share + live) * size * slots * part
        if c == 0:
            picked, found, select = call(
                functools.partial(first_pick_kernel, size), "pick_first",
                outs + [bf16(share + live, size * slots)], (chosen, *raw[c]), flops,
                after=(norm,),
            )
        else:
            picked, found = call(
                next_pick_kernel, "pick_next", outs, (select, *raw[c]), flops, after=shifted[-1]
            )
        dense.append(found)
        shifted.append(
            [
                lax.ppermute(picked, "grp", [(g, (g + k) % groups) for g in range(groups)])
                for k in range(1, groups)
            ]
        )

    scratch = [pltpu.VMEM((centers, 2 * part), BF16)]
    flops = 2 * rows * centers * 2 * part
    before, best, final = (), None, None
    for c in range(CHUNKS):
        block = join(shifted[c], part, after=() if c else (picked,))
        got = mixed_permute(block, size, 0)
        if c == CHUNKS - 1:
            own = call(beside_kernel, "beside", bf16(live, half), dense, after=(block,))
            near, best = call(
                functools.partial(group_kernel, picks), "group", [line] * 2,
                (cand, norm, chosen, own, core_permute(own, size)), 2 * rows * live * width,
                scratch=[pltpu.VMEM((live, width), BF16)],
            )
        after = (best,) if c == CHUNKS - 1 else shifted[c + 1]
        mine, got = double(block, got, stages, after=after)
        sent = join((got,), part, after=before) if before else got
        blocks = (mine, got, core_permute(mine, size), core_permute(sent, size))
        if c < CHUNKS - 1:
            before = (
                call(
                    functools.partial(far_kernel, size, c), "far",
                    jax.ShapeDtypeStruct((centers, rows), F32), (cand, *before, *blocks), flops,
                    scratch=scratch,
                ),
            )
        else:
            final = call(
                functools.partial(last_kernel, size, c), "far_last", line,
                (cand, best, norm, *before, *blocks), flops, scratch=scratch,
            )
    return near.reshape(-1), final.reshape(-1)


def solution(mesh):
    in_specs = (P(("grp", "mem"), None), P(("grp", "mem"), None), P("grp", "mem"), P("grp", None))
    out_specs = (P(("grp", "mem")), P(("grp", "mem")))
    return jax.shard_map(body, mesh=mesh, in_specs=in_specs, out_specs=out_specs, check_vma=False)
```

```python
import functools

import jax
import jax.numpy as jnp
from jax import lax
from jax.experimental import pallas as pl
from jax.experimental.pallas import tpu as pltpu
from jax.sharding import PartitionSpec as P

CHUNKS = 2
TILE = 256
MIB = 1024 * 1024
WEIGHT = 10**10
F32, BF16 = jnp.float32, jnp.bfloat16


def chip_bits(size):
    return [1 << b for b in range(1, size.bit_length() - 1)]


def crossing(size, odd):
    return chip_bits(size)[::-1] if odd else chip_bits(size)


def mixed_permute(block, size, stage):
    even, odd = crossing(size, False)[stage], crossing(size, True)[stage]
    return lax.ppermute(block, "mem", [(m, m ^ (odd if m & 1 else even)) for m in range(size)])


def core_permute(block, size):
    return lax.ppermute(block, "mem", [(m, m ^ 1) for m in range(size)])


def block_flips(size, odd):
    flips = [0]
    for bit in crossing(size, odd):
        flips = flips + [f ^ bit for f in flips]
    return flips


def sibling_place(index, size):
    return block_flips(size, True).index(block_flips(size, False)[index])


def vmem_specs(count):
    return [pl.BlockSpec(memory_space=pltpu.VMEM)] * count


def call(kernel, name, out_shape, operands, specs=None, scratch=(), after=(), limit=28 * MIB, weight=WEIGHT):
    shapes = jax.tree.leaves(out_shape)
    moved = sum(a.size * a.dtype.itemsize for a in list(operands) + shapes)
    count = len(operands)

    def run(*refs):
        kernel(*refs[:count], *refs[count + len(after) :])

    return pl.pallas_call(
        run,
        out_shape=out_shape,
        in_specs=(specs or vmem_specs(count)) + [pl.BlockSpec(memory_space=pl.ANY)] * len(after),
        out_specs=jax.tree.map(lambda _: pl.BlockSpec(memory_space=pltpu.VMEM), out_shape),
        scratch_shapes=scratch,
        compiler_params=pltpu.CompilerParams(vmem_limit_bytes=limit),
        cost_estimate=pl.CostEstimate(flops=weight, bytes_accessed=moved, transcendentals=0),
        name=name,
    )(*operands, *after)


def spread_kernel(count_ref, out):
    out[...] = jnp.broadcast_to(count_ref[0, 0], out.shape)


def pair_kernel(own, sib, out):
    lane = lax.broadcasted_iota(jnp.int32, out.shape, 1)
    out[...] = jnp.where(lane == 0, own[...], sib[...])


def split_kernel(rows_ref, keep_ref, send_ref):
    half = keep_ref.shape[1]
    core = lax.rem(lax.axis_index("mem"), 2)
    keep_ref[...] = rows_ref[:, pl.ds(pl.multiple_of(core * half, half), half)]
    send_ref[...] = rows_ref[:, pl.ds(pl.multiple_of((1 - core) * half, half), half)]


def load_kernel(cand_hbm, cand_ref, norm_ref, sems):
    half = cand_ref.shape[1] // 2
    part = half // CHUNKS
    core = lax.rem(lax.axis_index("mem"), 2)
    tiles = cand_ref.shape[0] // TILE
    copies = []
    for t in range(tiles):
        at = pl.ds(t * TILE, TILE)
        for p in range(2 * CHUNKS):
            own = core if p % 2 == 0 else 1 - core
            start = pl.multiple_of(own * half + p // 2 * part, part)
            copies.append(
                pltpu.make_async_copy(
                    cand_hbm.at[at, pl.ds(start, part)],
                    cand_ref.at[at, pl.ds(p * part, part)],
                    sems.at[len(copies)],
                )
            )
    for copy in copies:
        copy.start()
    for t in range(tiles):
        for copy in copies[t * 2 * CHUNKS : (t + 1) * 2 * CHUNKS]:
            copy.wait()
        squares = jnp.zeros((TILE, 128), F32)
        for k in range(0, cand_ref.shape[1], 128):
            entries = cand_ref[t * TILE : (t + 1) * TILE, k : k + 128].astype(F32)
            squares += entries * entries
        norm_ref[:, t * TILE : (t + 1) * TILE] = jnp.sum(squares.T, axis=0, keepdims=True)


def join_kernel(count, start, *refs):
    blocks, out = refs[:count], refs[count]
    rows = blocks[0].shape[0]
    for i, block in enumerate(blocks):
        out[i * rows : (i + 1) * rows, :] = block[:, start : start + out.shape[1]]


def owner_flips(size, odd):
    flips = [0]
    for bit in crossing(size, odd)[::-1]:
        flips = flips + [f ^ bit for f in flips]
    return flips


def dense_kernel(size, picks_chip, rest_chip, chosen_ref, *refs):
    counts, (own, sib, keep_ref, send_ref, select_ref) = refs[:-5], refs[-5:]
    slots, picks = own.shape[0], chosen_ref.shape[1]
    rows_chip = picks_chip + rest_chip
    me = lax.axis_index("mem")
    odd_core = lax.rem(me, 2) == 1
    offsets = [jnp.zeros((1, 1), jnp.int32) for _ in range(2)]
    for d, ref in enumerate(counts):
        for h in range(2):
            origin = lax.bitwise_xor(me, 2 * d + h)
            for k in range(2):
                before = (origin < lax.bitwise_xor(me, k)).astype(jnp.int32)
                offsets[k] += ref[:1, h : h + 1] * before
    lane = lax.broadcasted_iota(jnp.int32, (1, 2 * slots), 1)
    first = lane < slots
    within = jnp.where(first, lane, lane - slots)
    alive = within < jnp.where(first, counts[0][:1, :1], counts[0][:1, 1:2])
    position = jnp.where(alive, within + jnp.where(first, offsets[0], offsets[1]), -1)

    chosen = chosen_ref[...]

    def column(start, length):
        row = lax.broadcasted_iota(jnp.int32, (length, picks), 0)
        across = lax.broadcasted_iota(jnp.int32, (length, picks), 1)
        return jnp.sum(jnp.where(across == row + start, chosen, 0), axis=1, keepdims=True)

    ids = column(0, picks)
    below = jnp.sum((ids < position).astype(jnp.int32), axis=0, keepdims=True)
    taken = jnp.sum((ids == position).astype(jnp.int32), axis=0, keepdims=True)
    rank = jnp.where(alive & (taken == 0), position - below, -1)
    place = lax.broadcasted_iota(jnp.int32, (rest_chip, 1), 0)
    for n, (e, o) in enumerate(zip(owner_flips(size, False), owner_flips(size, True))):
        owner = lax.bitwise_xor(me, jnp.where(odd_core, o, e)) // 2
        top = n * rows_chip
        hit = column(owner * picks_chip, picks_chip) == position
        select_ref[top : top + picks_chip, :] = hit.astype(F32).astype(BF16)
        hit = place + owner * rest_chip == rank
        select_ref[top + picks_chip : top + rows_chip, :] = hit.astype(F32).astype(BF16)

    half_rows = keep_ref.shape[0]

    @pl.loop(0, keep_ref.shape[1] // TILE)
    def _(t):
        at = pl.ds(pl.multiple_of(t * TILE, TILE), TILE)
        rows = jnp.concatenate([own[:, at], sib[:, at]], axis=0)
        found = jnp.dot(select_ref[...], rows, preferred_element_type=F32).astype(BF16)
        keep_ref[:, at] = found[:half_rows]
        send_ref[:, at] = found[half_rows:]


def add_kernel(keep, got, *outs):
    top = 0
    for out in outs:
        rows = out.shape[0]
        out[...] = keep[top : top + rows, :] + got[top : top + rows, :]
        top += rows


def owned_kernel(keep, got, out, picks_ref):
    out[...] = keep[...] + got[...]
    picks_ref[...] = out[: picks_ref.shape[0], :]


def row_norms(rows):
    rows = rows.astype(F32)
    return jnp.sum(rows * rows, axis=1, keepdims=True)


def gaps_to(rows_ref, norms, cand):
    inner = lax.dot_general(
        rows_ref[...], cand, (((1,), (1,)), ((), ())), preferred_element_type=F32
    )
    return norms - 2.0 * inner


def group_kernel(size, picks_chip, cand_ref, norm_ref, own, sib, near_ref, best_ref, rows_ref):
    chips, half = size // 2, own.shape[1]
    part, rows_chip = half // CHUNKS, own.shape[0] // chips
    for c in range(CHUNKS):
        at = slice(c * part, (c + 1) * part)
        rows_ref[:, 2 * c * part : (2 * c + 1) * part] = own[:, at]
        for i in range(chips):
            to = sibling_place(i, size) * rows_chip
            rows_ref[to : to + rows_chip, (2 * c + 1) * part : (2 * c + 2) * part] = sib[
                i * rows_chip : (i + 1) * rows_chip, at
            ]
    norms = row_norms(rows_ref[...])
    down = lax.broadcasted_iota(jnp.int32, norms.shape, 0)
    outside = jnp.where(lax.rem(down, rows_chip) < picks_chip, 0.0, jnp.inf)

    @pl.loop(0, cand_ref.shape[0] // TILE)
    def _(t):
        at = pl.ds(pl.multiple_of(t * TILE, TILE), TILE)
        gaps = gaps_to(rows_ref, norms, cand_ref[at, :])
        near_ref[:, at] = jnp.min(gaps, axis=0, keepdims=True) + norm_ref[:, at]
        best_ref[:, at] = jnp.min(gaps + outside, axis=0, keepdims=True)


def far_rows(size, held, sibs, rows_ref):
    rows, part = rows_ref.shape[0] // (size // 2), held[0].shape[1]
    for i, block in enumerate(held):
        top = i * block.shape[0]
        rows_ref[top : top + block.shape[0], :part] = block[...]
    for i in range(size // 2):
        block = sibs[i * rows // sibs[0].shape[0]]
        top = i * rows % sibs[0].shape[0]
        to = sibling_place(i, size) * rows
        rows_ref[to : to + rows, part:] = block[top : top + rows, :]


def far_gaps(size, chunk, cand_ref, before, blocks, rows_ref, emit):
    far_rows(size, blocks[:2], blocks[2:], rows_ref)
    width = rows_ref.shape[1]
    norms = row_norms(rows_ref[...])

    @pl.loop(0, cand_ref.shape[0] // TILE)
    def _(t):
        at = pl.ds(pl.multiple_of(t * TILE, TILE), TILE)
        gaps = gaps_to(rows_ref, norms, cand_ref[at, chunk * width : (chunk + 1) * width])
        for ref in before:
            gaps += ref[:, at]
        emit(at, gaps)


def far_kernel(size, chunk, cand_ref, *refs):
    *before, mine, got, sib_mine, sib_got, out, rows_ref = refs

    def emit(at, gaps):
        out[:, at] = gaps

    far_gaps(size, chunk, cand_ref, before, (mine, got, sib_mine, sib_got), rows_ref, emit)


def last_kernel(size, chunk, cand_ref, best_ref, norm_ref, *refs):
    *before, mine, got, sib_mine, sib_got, out, rows_ref = refs

    def emit(at, gaps):
        least = jnp.minimum(jnp.min(gaps, axis=0, keepdims=True), best_ref[:, at])
        out[:, at] = least + norm_ref[:, at]

    far_gaps(size, chunk, cand_ref, before, (mine, got, sib_mine, sib_got), rows_ref, emit)


def body(candidates, round_one, counts, chosen):
    size, groups = lax.axis_size("mem"), lax.axis_size("grp")
    slots, width = round_one.shape
    half, chips = width // 2, size // 2
    part = half // CHUNKS
    picks, rows = chosen.shape[1], candidates.shape[0]
    picks_chip = picks // chips
    rest_chip = (size * slots * 3 // 8 - picks) // chips
    rows_chip = picks_chip + rest_chip
    live, centers = chips * rows_chip, (groups - 1) * picks
    stages = len(chip_bits(size))

    def bf16(*dims):
        return jax.ShapeDtypeStruct(dims, BF16)

    def join(blocks, columns, start=0, after=(), weight=WEIGHT):
        count = blocks[0].shape[0] * len(blocks)
        return call(
            functools.partial(join_kernel, len(blocks), start), "join", bf16(count, columns),
            blocks, after=after, weight=weight,
        )

    line = jax.ShapeDtypeStruct((1, rows), F32)
    tile = jax.ShapeDtypeStruct((8, 128), jnp.int32)
    count = call(
        spread_kernel, "spread", tile, (counts,), specs=[pl.BlockSpec(memory_space=pltpu.SMEM)]
    )
    pair = call(pair_kernel, "pair", tile, (count, core_permute(count, size)))
    pairs = [pair] + [
        lax.ppermute(pair, "mem", [(m, m ^ (2 * d)) for m in range(size)]) for d in range(1, chips)
    ]
    own, send = call(split_kernel, "split", [bf16(slots, half)] * 2, (round_one,))
    sib = core_permute(send, size)

    held = live // 2
    keep, send = call(
        functools.partial(dense_kernel, size, picks_chip, rest_chip), "dense",
        [bf16(held, half)] * 2, (chosen, *pairs, own, sib),
        scratch=[pltpu.VMEM((live, 2 * slots), BF16)],
    )
    cand, norm = call(
        load_kernel, "load", [bf16(rows, width), line], (candidates,),
        specs=[pl.BlockSpec(memory_space=pltpu.HBM)], after=(keep,),
        scratch=[pltpu.SemaphoreType.DMA((rows // TILE * 2 * CHUNKS,))], limit=42 * MIB,
    )
    for stage in range(stages - 1):
        held //= 2
        got = mixed_permute(send, size, stage)
        keep, send = call(
            add_kernel, "add", [bf16(held, half)] * 2, (keep, got), after=(norm,)
        )
    got = mixed_permute(send, size, stages - 1)
    owned, picked = call(
        owned_kernel, "owned", [bf16(rows_chip, half), bf16(picks_chip, half)], (keep, got)
    )

    shifted = [
        lax.ppermute(picked, "grp", [(g, (g + k) % groups) for g in range(groups)])
        for k in range(1, groups)
    ]
    dense = owned
    for stage in range(stages):
        dense = join((dense, mixed_permute(dense, size, stage)), half, weight=0)
    near, best = call(
        functools.partial(group_kernel, size, picks_chip), "group", [line] * 2,
        (cand, norm, dense, core_permute(dense, size)),
        scratch=[pltpu.VMEM((live, width), BF16)],
    )
    block = join(shifted, half, after=(best,))

    got = mixed_permute(block, size, 0)
    for stage in range(1, stages - 1):
        block = join((block, got), half)
        got = mixed_permute(block, size, stage)
    scratch = [pltpu.VMEM((centers, 2 * part), BF16)]
    mine = [join((block, got), part, c * part) for c in range(CHUNKS)]
    got = [mixed_permute(m, size, stages - 1) for m in mine]
    before, final = (), None
    for c in range(CHUNKS):
        sent = join((got[c],), part, after=before) if before else got[c]
        blocks = (mine[c], got[c], core_permute(mine[c], size), core_permute(sent, size))
        if c < CHUNKS - 1:
            before = (
                call(
                    functools.partial(far_kernel, size, c), "far",
                    jax.ShapeDtypeStruct((centers, rows), F32), (cand, *before, *blocks),
                    scratch=scratch,
                ),
            )
        else:
            final = call(
                functools.partial(last_kernel, size, c), "far_last", line,
                (cand, best, norm, *before, *blocks), scratch=scratch,
            )
    return near.reshape(-1), final.reshape(-1)


def solution(mesh):
    in_specs = (P(("grp", "mem"), None), P(("grp", "mem"), None), P("grp", "mem"), P("grp", None))
    out_specs = (P(("grp", "mem")), P(("grp", "mem")))
    return jax.shard_map(body, mesh=mesh, in_specs=in_specs, out_specs=out_specs, check_vma=False)
```

```python
import functools

import jax
import jax.numpy as jnp
from jax import lax
from jax.experimental import pallas as pl
from jax.experimental.pallas import tpu as pltpu
from jax.sharding import PartitionSpec as P

CHUNKS = (6, 2)
TILE = 256
MIB = 1024 * 1024
WEIGHT = 10**10
F32, BF16 = jnp.float32, jnp.bfloat16


def flip_permute(block, size, flip):
    return lax.ppermute(block, "mem", [(m, m ^ flip) for m in range(size)])


def to_chips(block, size):
    return [block] + [flip_permute(block, size, 2 * d) for d in range(1, size // 2)]


def vmem_specs(count):
    return [pl.BlockSpec(memory_space=pltpu.VMEM)] * count


def call(kernel, name, out_shape, operands, specs=None, scratch=(), after=(), limit=28 * MIB, weight=WEIGHT):
    shapes = jax.tree.leaves(out_shape)
    moved = sum(a.size * a.dtype.itemsize for a in list(operands) + shapes)
    count = len(operands)

    def run(*refs):
        kernel(*refs[:count], *refs[count + len(after) :])

    return pl.pallas_call(
        run,
        out_shape=out_shape,
        in_specs=(specs or vmem_specs(count)) + [pl.BlockSpec(memory_space=pl.ANY)] * len(after),
        out_specs=jax.tree.map(lambda _: pl.BlockSpec(memory_space=pltpu.VMEM), out_shape),
        scratch_shapes=scratch,
        compiler_params=pltpu.CompilerParams(vmem_limit_bytes=limit),
        cost_estimate=pl.CostEstimate(flops=weight, bytes_accessed=moved, transcendentals=0),
        name=name,
    )(*operands, *after)


def spread_kernel(count_ref, out):
    out[...] = jnp.broadcast_to(count_ref[0, 0], out.shape)


def pair_kernel(own, sib, out):
    lane = lax.broadcasted_iota(jnp.int32, out.shape, 1)
    out[...] = jnp.where(lane == 0, own[...], sib[...])


def split_kernel(rows_ref, keep_ref, send_ref):
    half = keep_ref.shape[1]
    core = lax.rem(lax.axis_index("mem"), 2)
    keep_ref[...] = rows_ref[:, pl.ds(pl.multiple_of(core * half, half), half)]
    send_ref[...] = rows_ref[:, pl.ds(pl.multiple_of((1 - core) * half, half), half)]


def chunk_bounds(half):
    bounds, start = [], 0
    for eighths in CHUNKS:
        bounds.append((start, half * eighths // 8))
        start += bounds[-1][1]
    return bounds


def load_kernel(cand_hbm, cand_ref, norm_ref, sems):
    half = cand_ref.shape[1] // 2
    core = lax.rem(lax.axis_index("mem"), 2)
    tiles, copies = cand_ref.shape[0] // TILE, []
    for t in range(tiles):
        at = pl.ds(t * TILE, TILE)
        for start, width in chunk_bounds(half):
            for k, own in enumerate((core, 1 - core)):
                origin = pl.multiple_of(own * half + start, 128)
                copies.append(
                    pltpu.make_async_copy(
                        cand_hbm.at[at, pl.ds(origin, width)],
                        cand_ref.at[at, pl.ds(2 * start + k * width, width)],
                        sems.at[len(copies)],
                    )
                )
    for copy in copies:
        copy.start()
    each = len(copies) // tiles
    for t in range(tiles):
        for copy in copies[t * each : (t + 1) * each]:
            copy.wait()
        squares = jnp.zeros((TILE, 128), F32)
        for k in range(0, cand_ref.shape[1], 128):
            entries = cand_ref[t * TILE : (t + 1) * TILE, k : k + 128].astype(F32)
            squares += entries * entries
        norm_ref[:, t * TILE : (t + 1) * TILE] = jnp.sum(squares.T, axis=0, keepdims=True)


def join_kernel(count, start, *refs):
    blocks, out = refs[:count], refs[count]
    rows = blocks[0].shape[0]
    for i, block in enumerate(blocks):
        out[i * rows : (i + 1) * rows, :] = block[:, start : start + out.shape[1]]


def dense_kernel(size, picks_chip, rest_chip, chosen_ref, *refs):
    chips = size // 2
    counts, (own, sib, *outs, select_ref) = refs[:chips], refs[chips:]
    slots, picks = own.shape[0], chosen_ref.shape[1]
    rows_chip = picks_chip + rest_chip
    me = lax.axis_index("mem")
    offsets = [jnp.zeros((1, 1), jnp.int32) for _ in range(2)]
    for d, ref in enumerate(counts):
        for h in range(2):
            origin = lax.bitwise_xor(me, 2 * d + h)
            for k in range(2):
                before = (origin < lax.bitwise_xor(me, k)).astype(jnp.int32)
                offsets[k] += ref[:1, h : h + 1] * before
    lane = lax.broadcasted_iota(jnp.int32, (1, 2 * slots), 1)
    first = lane < slots
    within = jnp.where(first, lane, lane - slots)
    alive = within < jnp.where(first, counts[0][:1, :1], counts[0][:1, 1:2])
    position = jnp.where(alive, within + jnp.where(first, offsets[0], offsets[1]), -1)

    chosen = chosen_ref[...]

    def column(start, length):
        row = lax.broadcasted_iota(jnp.int32, (length, picks), 0)
        across = lax.broadcasted_iota(jnp.int32, (length, picks), 1)
        return jnp.sum(jnp.where(across == row + start, chosen, 0), axis=1, keepdims=True)

    ids = column(0, picks)
    below = jnp.sum((ids < position).astype(jnp.int32), axis=0, keepdims=True)
    taken = jnp.sum((ids == position).astype(jnp.int32), axis=0, keepdims=True)
    rank = jnp.where(alive & (taken == 0), position - below, -1)
    place = lax.broadcasted_iota(jnp.int32, (rest_chip, 1), 0)
    for d in range(chips):
        owner = lax.bitwise_xor(me // 2, d)
        top = d * rows_chip
        hit = column(owner * picks_chip, picks_chip) == position
        select_ref[top : top + picks_chip, :] = hit.astype(F32).astype(BF16)
        hit = place + owner * rest_chip == rank
        select_ref[top + picks_chip : top + rows_chip, :] = hit.astype(F32).astype(BF16)

    @pl.loop(0, own.shape[1] // TILE)
    def _(t):
        at = pl.ds(pl.multiple_of(t * TILE, TILE), TILE)
        rows = jnp.concatenate([own[:, at], sib[:, at]], axis=0)
        found = jnp.dot(select_ref[...], rows, preferred_element_type=F32).astype(BF16)
        for d, out in enumerate(outs):
            out[:, at] = found[d * rows_chip : (d + 1) * rows_chip]


def sum_kernel(*refs):
    *parts, out, picks_ref = refs
    total = parts[0][...]
    for ref in parts[1:]:
        total += ref[...]
    out[...] = total
    picks_ref[...] = total[: picks_ref.shape[0], :]


def square_kernel(own, first, second, left, right, out):
    rows, part = left.shape
    for i, block in enumerate((own, first, second)):
        out[i * rows : (i + 1) * rows, :] = block[...]
    out[3 * rows :, :part] = left[...]
    out[3 * rows :, part:] = right[...]


def row_norms(rows):
    rows = rows.astype(F32)
    return jnp.sum(rows * rows, axis=1, keepdims=True)


def gaps_to(rows_ref, norms, cand):
    inner = lax.dot_general(
        rows_ref[...], cand, (((1,), (1,)), ((), ())), preferred_element_type=F32
    )
    return norms - 2.0 * inner


def group_kernel(rows_chip, picks_chip, cand_ref, norm_ref, own, sib, near_ref, best_ref, rows_ref):
    for start, width in chunk_bounds(own.shape[1]):
        at = slice(start, start + width)
        rows_ref[:, 2 * start : 2 * start + width] = own[:, at]
        rows_ref[:, 2 * start + width : 2 * (start + width)] = sib[:, at]
    norms = row_norms(rows_ref[...])
    down = lax.broadcasted_iota(jnp.int32, norms.shape, 0)
    outside = jnp.where(lax.rem(down, rows_chip) < picks_chip, 0.0, jnp.inf)

    @pl.loop(0, cand_ref.shape[0] // TILE)
    def _(t):
        at = pl.ds(pl.multiple_of(t * TILE, TILE), TILE)
        gaps = gaps_to(rows_ref, norms, cand_ref[at, :])
        near_ref[:, at] = jnp.min(gaps, axis=0, keepdims=True) + norm_ref[:, at]
        best_ref[:, at] = jnp.min(gaps + outside, axis=0, keepdims=True)


def far_gaps(start, cand_ref, before, blocks, rows_ref, emit):
    own, sib = blocks
    part = own.shape[1]
    rows_ref[:, :part] = own[...]
    rows_ref[:, part:] = sib[...]
    norms = row_norms(rows_ref[...])

    @pl.loop(0, cand_ref.shape[0] // TILE)
    def _(t):
        at = pl.ds(pl.multiple_of(t * TILE, TILE), TILE)
        gaps = gaps_to(rows_ref, norms, cand_ref[at, 2 * start : 2 * (start + part)])
        for ref in before:
            gaps += ref[:, at]
        emit(at, gaps)


def far_kernel(start, cand_ref, *refs):
    *before, own, sib, out, rows_ref = refs

    def emit(at, gaps):
        out[:, at] = gaps

    far_gaps(start, cand_ref, before, (own, sib), rows_ref, emit)


def last_kernel(start, cand_ref, best_ref, norm_ref, *refs):
    *before, own, sib, out, rows_ref = refs

    def emit(at, gaps):
        least = jnp.minimum(jnp.min(gaps, axis=0, keepdims=True), best_ref[:, at])
        out[:, at] = least + norm_ref[:, at]

    far_gaps(start, cand_ref, before, (own, sib), rows_ref, emit)


def body(candidates, round_one, counts, chosen):
    size, groups = lax.axis_size("mem"), lax.axis_size("grp")
    slots, width = round_one.shape
    half, chips = width // 2, size // 2
    picks, rows = chosen.shape[1], candidates.shape[0]
    picks_chip = picks // chips
    rest_chip = (size * slots * 3 // 8 - picks) // chips
    rows_chip = picks_chip + rest_chip
    live, centers = chips * rows_chip, (groups - 1) * picks

    def bf16(*dims):
        return jax.ShapeDtypeStruct(dims, BF16)

    def join(blocks, columns, start=0, after=(), weight=WEIGHT):
        count = blocks[0].shape[0] * len(blocks)
        return call(
            functools.partial(join_kernel, len(blocks), start), "join", bf16(count, columns),
            blocks, after=after, weight=weight,
        )

    line = jax.ShapeDtypeStruct((1, rows), F32)
    tile = jax.ShapeDtypeStruct((8, 128), jnp.int32)
    count = call(
        spread_kernel, "spread", tile, (counts,), specs=[pl.BlockSpec(memory_space=pltpu.SMEM)]
    )
    pair = call(pair_kernel, "pair", tile, (count, flip_permute(count, size, 1)))
    pairs = to_chips(pair, size)
    own, send = call(split_kernel, "split", [bf16(slots, half)] * 2, (round_one,))
    sib = flip_permute(send, size, 1)

    parts = call(
        functools.partial(dense_kernel, size, picks_chip, rest_chip), "dense",
        [bf16(rows_chip, half)] * chips, (chosen, *pairs, own, sib),
        scratch=[pltpu.VMEM((live, 2 * slots), BF16)],
    )
    copies = rows // TILE * 2 * len(CHUNKS)
    cand, norm = call(
        load_kernel, "load", [bf16(rows, width), line], (candidates,),
        specs=[pl.BlockSpec(memory_space=pltpu.HBM)], after=parts[:1],
        scratch=[pltpu.SemaphoreType.DMA((copies,))], limit=42 * MIB,
    )
    got = [flip_permute(parts[d], size, 2 * d) for d in range(1, chips)]
    owned, picked = call(
        sum_kernel, "owned", [bf16(rows_chip, half), bf16(picks_chip, half)], (parts[0], *got),
        after=(norm,),
    )

    shifted = [
        lax.ppermute(picked, "grp", [(g, (g + k) % groups) for g in range(groups)])
        for k in range(1, groups)
    ]
    if chips == 4:
        first, second = (flip_permute(owned, size, flip) for flip in (2, 4))
        left = flip_permute(join((first,), half // 2, weight=0), size, 4)
        right = flip_permute(join((second,), half // 2, half // 2, weight=0), size, 2)
        dense = call(
            square_kernel, "square", bf16(live, half), (owned, first, second, left, right), weight=0
        )
    else:
        dense = join(to_chips(owned, size), half)
    near, best = call(
        functools.partial(group_kernel, rows_chip, picks_chip), "group", [line] * 2,
        (cand, norm, dense, flip_permute(dense, size, 1)),
        scratch=[pltpu.VMEM((live, width), BF16)],
    )

    bounds = chunk_bounds(half)
    far = [to_chips(join(shifted, part, start, after=(dense,)), size) for start, part in bounds]
    before, final = (), None
    for c, (start, part) in enumerate(bounds):
        block = join(far[c], part, after=before or (best,))
        operands = (*before, block, flip_permute(block, size, 1))
        scratch = [pltpu.VMEM((centers, 2 * part), BF16)]
        if c < len(bounds) - 1:
            before = (
                call(
                    functools.partial(far_kernel, start), "far",
                    jax.ShapeDtypeStruct((centers, rows), F32), (cand, *operands), scratch=scratch,
                ),
            )
        else:
            final = call(
                functools.partial(last_kernel, start), "far_last", line,
                (cand, best, norm, *operands), scratch=scratch,
            )
    return near.reshape(-1), final.reshape(-1)


def solution(mesh):
    in_specs = (P(("grp", "mem"), None), P(("grp", "mem"), None), P("grp", "mem"), P("grp", None))
    out_specs = (P(("grp", "mem")), P(("grp", "mem")))
    return jax.shard_map(body, mesh=mesh, in_specs=in_specs, out_specs=out_specs, check_vma=False)
```

```python
import functools

import jax
import jax.numpy as jnp
from jax import lax
from jax.experimental import pallas as pl
from jax.experimental.pallas import tpu as pltpu
from jax.sharding import PartitionSpec as P

TILE = 256
MIB = 1024 * 1024
WEIGHT = 10**10
F32, BF16 = jnp.float32, jnp.bfloat16


def flip_permute(block, size, flip):
    return lax.ppermute(block, "mem", [(m, m ^ flip) for m in range(size)])


def to_chips(block, size):
    return [block] + [flip_permute(block, size, 2 * d) for d in range(1, size // 2)]


def vmem_specs(count):
    return [pl.BlockSpec(memory_space=pltpu.VMEM)] * count


def call(kernel, name, out_shape, operands, specs=None, scratch=(), after=(), limit=28 * MIB, weight=WEIGHT):
    shapes = jax.tree.leaves(out_shape)
    moved = sum(a.size * a.dtype.itemsize for a in list(operands) + shapes)
    count = len(operands)

    def run(*refs):
        kernel(*refs[:count], *refs[count + len(after) :])

    return pl.pallas_call(
        run,
        out_shape=out_shape,
        in_specs=(specs or vmem_specs(count)) + [pl.BlockSpec(memory_space=pl.ANY)] * len(after),
        out_specs=jax.tree.map(lambda _: pl.BlockSpec(memory_space=pltpu.VMEM), out_shape),
        scratch_shapes=scratch,
        compiler_params=pltpu.CompilerParams(vmem_limit_bytes=limit),
        cost_estimate=pl.CostEstimate(flops=weight, bytes_accessed=moved, transcendentals=0),
        name=name,
    )(*operands, *after)


def spread_kernel(count_ref, out):
    out[...] = jnp.broadcast_to(count_ref[0, 0], out.shape)


def pack_kernel(*refs):
    *counts, out = refs
    lane = lax.broadcasted_iota(jnp.int32, out.shape, 1)
    total = counts[0][...]
    for d, ref in enumerate(counts):
        total = jnp.where(lane == d, ref[...], total)
    out[...] = total


def split_kernel(rows_ref, keep_ref, send_ref):
    half = keep_ref.shape[1]
    core = lax.rem(lax.axis_index("mem"), 2)
    keep_ref[...] = rows_ref[:, pl.ds(pl.multiple_of(core * half, half), half)]
    send_ref[...] = rows_ref[:, pl.ds(pl.multiple_of((1 - core) * half, half), half)]


def load_kernel(cand_hbm, cand_ref, norm_ref, sems):
    half = cand_ref.shape[1] // 2
    core = lax.rem(lax.axis_index("mem"), 2)
    tiles, copies = cand_ref.shape[0] // TILE, []
    for t in range(tiles):
        at = pl.ds(t * TILE, TILE)
        for k, own in enumerate((core, 1 - core)):
            copies.append(
                pltpu.make_async_copy(
                    cand_hbm.at[at, pl.ds(pl.multiple_of(own * half, half), half)],
                    cand_ref.at[at, pl.ds(k * half, half)],
                    sems.at[len(copies)],
                )
            )
    for copy in copies:
        copy.start()
    for t in range(tiles):
        for copy in copies[2 * t : 2 * t + 2]:
            copy.wait()
        squares = jnp.zeros((TILE, 128), F32)
        for k in range(0, cand_ref.shape[1], 128):
            entries = cand_ref[t * TILE : (t + 1) * TILE, k : k + 128].astype(F32)
            squares += entries * entries
        norm_ref[:, t * TILE : (t + 1) * TILE] = jnp.sum(squares.T, axis=0, keepdims=True)


def join_kernel(count, start, *refs):
    blocks, out = refs[:count], refs[count]
    rows = blocks[0].shape[0]
    for i, block in enumerate(blocks):
        out[i * rows : (i + 1) * rows, :] = block[:, start : start + out.shape[1]]


def dense_kernel(size, picks_chip, rest_chip, chosen_ref, *refs):
    chips = size // 2
    *counts, own, sib = refs[:4]
    outs, select_ref = refs[4:-1], refs[-1]
    slots, picks = own.shape[0], chosen_ref.shape[1]
    rows_chip = picks_chip + rest_chip
    me = lax.axis_index("mem")
    offsets = [jnp.zeros((1, 1), jnp.int32) for _ in range(2)]
    for d in range(chips):
        for h, ref in enumerate(counts):
            origin = lax.bitwise_xor(me, 2 * d + h)
            for k in range(2):
                before = (origin < lax.bitwise_xor(me, k)).astype(jnp.int32)
                offsets[k] += ref[:1, d : d + 1] * before
    lane = lax.broadcasted_iota(jnp.int32, (1, 2 * slots), 1)
    first = lane < slots
    within = jnp.where(first, lane, lane - slots)
    alive = within < jnp.where(first, counts[0][:1, :1], counts[1][:1, :1])
    position = jnp.where(alive, within + jnp.where(first, offsets[0], offsets[1]), -1)

    chosen = chosen_ref[...]

    def column(start, length):
        row = lax.broadcasted_iota(jnp.int32, (length, picks), 0)
        across = lax.broadcasted_iota(jnp.int32, (length, picks), 1)
        return jnp.sum(jnp.where(across == row + start, chosen, 0), axis=1, keepdims=True)

    ids = column(0, picks)
    below = jnp.sum((ids < position).astype(jnp.int32), axis=0, keepdims=True)
    taken = jnp.sum((ids == position).astype(jnp.int32), axis=0, keepdims=True)
    rank = jnp.where(alive & (taken == 0), position - below, -1)
    place = lax.broadcasted_iota(jnp.int32, (rest_chip, 1), 0)
    for d in range(chips):
        owner = lax.bitwise_xor(me // 2, d)
        top = d * rows_chip
        hit = column(owner * picks_chip, picks_chip) == position
        select_ref[top : top + picks_chip, :] = hit.astype(F32).astype(BF16)
        hit = place + owner * rest_chip == rank
        select_ref[top + picks_chip : top + rows_chip, :] = hit.astype(F32).astype(BF16)

    @pl.loop(0, own.shape[1] // TILE)
    def _(t):
        at = pl.ds(pl.multiple_of(t * TILE, TILE), TILE)
        rows = jnp.concatenate([own[:, at], sib[:, at]], axis=0)
        found = jnp.dot(select_ref[...], rows, preferred_element_type=F32).astype(BF16)
        for d, out in enumerate(outs):
            out[:, at] = found[d * rows_chip : (d + 1) * rows_chip]


def sum_kernel(*refs):
    *parts, out, picks_ref = refs
    total = parts[0][...]
    for ref in parts[1:]:
        total += ref[...]
    out[...] = total
    picks_ref[...] = total[: picks_ref.shape[0], :]


def square_kernel(own, first, second, left, right, out):
    rows, part = left.shape
    for i, block in enumerate((own, first, second)):
        out[i * rows : (i + 1) * rows, :] = block[...]
    out[3 * rows :, :part] = left[...]
    out[3 * rows :, part:] = right[...]


def row_norms(rows):
    rows = rows.astype(F32)
    return jnp.sum(rows * rows, axis=1, keepdims=True)


def gaps_to(rows_ref, norms, cand):
    inner = lax.dot_general(
        rows_ref[...], cand, (((1,), (1,)), ((), ())), preferred_element_type=F32
    )
    return norms - 2.0 * inner


def tiles_of(cand_ref):
    return [slice(t, t + TILE) for t in range(0, cand_ref.shape[0], TILE)]


def group_kernel(rows_chip, picks_chip, cand_ref, norm_ref, own, sib, near_ref, best_ref, rows_ref):
    half = own.shape[1]
    rows_ref[:, :half] = own[...]
    rows_ref[:, half:] = sib[...]
    norms = row_norms(rows_ref[...])
    down = lax.broadcasted_iota(jnp.int32, norms.shape, 0)
    outside = jnp.where(lax.rem(down, rows_chip) < picks_chip, 0.0, jnp.inf)
    for at in tiles_of(cand_ref):
        gaps = gaps_to(rows_ref, norms, cand_ref[at, :])
        near_ref[:, at] = jnp.min(gaps, axis=0, keepdims=True) + norm_ref[:, at]
        best_ref[:, at] = jnp.min(gaps + outside, axis=0, keepdims=True)


def far_kernel(cand_ref, best_ref, own, sib, out, rows_ref):
    half = own.shape[1]
    rows_ref[:, :half] = own[...]
    rows_ref[:, half:] = sib[...]
    norms = row_norms(rows_ref[...])
    for at in tiles_of(cand_ref):
        gaps = gaps_to(rows_ref, norms, cand_ref[at, :])
        out[:, at] = jnp.minimum(jnp.min(gaps, axis=0, keepdims=True), best_ref[:, at])


def last_kernel(cand_ref, best_ref, norm_ref, *refs):
    *parts, out, rows_ref = refs
    start = 0
    for part in parts:
        rows_ref[:, start : start + part.shape[1]] = part[...]
        start += part.shape[1]
    norms = row_norms(rows_ref[...])
    for at in tiles_of(cand_ref):
        gaps = gaps_to(rows_ref, norms, cand_ref[at, :])
        least = jnp.minimum(jnp.min(gaps, axis=0, keepdims=True), best_ref[:, at])
        out[:, at] = least + norm_ref[:, at]


def body(candidates, round_one, counts, chosen):
    size, groups = lax.axis_size("mem"), lax.axis_size("grp")
    slots, width = round_one.shape
    half, chips = width // 2, size // 2
    picks, rows = chosen.shape[1], candidates.shape[0]
    picks_chip = picks // chips
    rest_chip = (size * slots * 3 // 8 - picks) // chips
    rows_chip = picks_chip + rest_chip
    live = chips * rows_chip

    def bf16(*dims):
        return jax.ShapeDtypeStruct(dims, BF16)

    def join(blocks, columns, start=0, after=(), weight=WEIGHT):
        count = blocks[0].shape[0] * len(blocks)
        return call(
            functools.partial(join_kernel, len(blocks), start), "join", bf16(count, columns),
            blocks, after=after, weight=weight,
        )

    line = jax.ShapeDtypeStruct((1, rows), F32)
    tile = jax.ShapeDtypeStruct((8, 128), jnp.int32)
    count = call(
        spread_kernel, "spread", tile, (counts,), specs=[pl.BlockSpec(memory_space=pltpu.SMEM)]
    )
    mine = call(pack_kernel, "pack", tile, to_chips(count, size), weight=0)
    theirs = flip_permute(mine, size, 1)
    own, send = call(split_kernel, "split", [bf16(slots, half)] * 2, (round_one,))
    sib = flip_permute(send, size, 1)

    parts = call(
        functools.partial(dense_kernel, size, picks_chip, rest_chip), "dense",
        [bf16(rows_chip, half)] * chips, (chosen, mine, theirs, own, sib),
        scratch=[pltpu.VMEM((live, 2 * slots), BF16)],
    )
    cand, norm = call(
        load_kernel, "load", [bf16(rows, width), line], (candidates,),
        specs=[pl.BlockSpec(memory_space=pltpu.HBM)], after=parts[:1],
        scratch=[pltpu.SemaphoreType.DMA((rows // TILE * 2,))], limit=42 * MIB,
    )
    got = [flip_permute(parts[d], size, 2 * d) for d in range(1, chips)]
    owned, picked = call(
        sum_kernel, "owned", [bf16(rows_chip, half), bf16(picks_chip, half)], (parts[0], *got),
        after=(norm,),
    )

    shifted = [
        lax.ppermute(picked, "grp", [(g, (g + k) % groups) for g in range(groups)])
        for k in range(1, groups)
    ]
    def corner(first, second, weight):
        left = flip_permute(join((first,), half // 2, weight=weight), size, 4)
        right = flip_permute(join((second,), half // 2, half // 2, weight=weight), size, 2)
        return left, right

    if chips == 4:
        first, second = (flip_permute(owned, size, flip) for flip in (2, 4))
        dense = call(
            square_kernel, "square", bf16(live, half),
            (owned, first, second, *corner(first, second, 0)), weight=0,
        )
    else:
        dense = join(to_chips(owned, size), half)
    near, best = call(
        functools.partial(group_kernel, rows_chip, picks_chip), "group", [line] * 2,
        (cand, norm, dense, flip_permute(dense, size, 1)),
        scratch=[pltpu.VMEM((live, width), BF16)],
    )

    block = join(shifted, half, after=(dense,))
    if chips == 4:
        first, second = (flip_permute(block, size, flip) for flip in (2, 4))
        blocks, last = (block, first, second), corner(first, second, 0)
    else:
        *blocks, end = to_chips(block, size)
        last = (end,)
    early = join(blocks, half, after=(best,))
    best = call(
        far_kernel, "far", line, (cand, best, early, flip_permute(early, size, 1)),
        scratch=[pltpu.VMEM((early.shape[0], width), BF16)],
    )
    sent = [join((part,), part.shape[1], after=(best,), weight=0) for part in last]
    final = call(
        last_kernel, "far_last", line,
        (cand, best, norm, *last, *[flip_permute(part, size, 1) for part in sent]),
        scratch=[pltpu.VMEM((block.shape[0], width), BF16)],
    )
    return near.reshape(-1), final.reshape(-1)


def solution(mesh):
    in_specs = (P(("grp", "mem"), None), P(("grp", "mem"), None), P("grp", "mem"), P("grp", None))
    out_specs = (P(("grp", "mem")), P(("grp", "mem")))
    return jax.shard_map(body, mesh=mesh, in_specs=in_specs, out_specs=out_specs, check_vma=False)
```

```python
import functools

import jax
import jax.numpy as jnp
from jax import lax
from jax.experimental import pallas as pl
from jax.experimental.pallas import tpu as pltpu
from jax.sharding import PartitionSpec as P

TILE = 256
MIB = 1024 * 1024
WEIGHT = 10**10
F32, BF16 = jnp.float32, jnp.bfloat16


def flip_permute(block, size, flip):
    return lax.ppermute(block, "mem", [(m, m ^ flip) for m in range(size)])


def to_chips(block, size):
    return [block] + [flip_permute(block, size, 2 * d) for d in range(1, size // 2)]


def vmem_specs(count):
    return [pl.BlockSpec(memory_space=pltpu.VMEM)] * count


def call(kernel, name, out_shape, operands, specs=None, scratch=(), after=(), limit=28 * MIB, weight=WEIGHT):
    shapes = jax.tree.leaves(out_shape)
    moved = sum(a.size * a.dtype.itemsize for a in list(operands) + shapes)
    count = len(operands)

    def run(*refs):
        kernel(*refs[:count], *refs[count + len(after) :])

    return pl.pallas_call(
        run,
        out_shape=out_shape,
        in_specs=(specs or vmem_specs(count)) + [pl.BlockSpec(memory_space=pl.ANY)] * len(after),
        out_specs=jax.tree.map(lambda _: pl.BlockSpec(memory_space=pltpu.VMEM), out_shape),
        scratch_shapes=scratch,
        compiler_params=pltpu.CompilerParams(vmem_limit_bytes=limit),
        cost_estimate=pl.CostEstimate(flops=weight, bytes_accessed=moved, transcendentals=0),
        name=name,
    )(*operands, *after)


def spread_kernel(count_ref, out):
    out[...] = jnp.broadcast_to(count_ref[0, 0], out.shape)


def pair_kernel(own, sib, out):
    lane = lax.broadcasted_iota(jnp.int32, out.shape, 1)
    out[...] = jnp.where(lane == 0, own[...], sib[...])


def split_kernel(rows_ref, keep_ref, send_ref):
    half = keep_ref.shape[1]
    core = lax.rem(lax.axis_index("mem"), 2)
    keep_ref[...] = rows_ref[:, pl.ds(pl.multiple_of(core * half, half), half)]
    send_ref[...] = rows_ref[:, pl.ds(pl.multiple_of((1 - core) * half, half), half)]


def load_kernel(cand_hbm, cand_ref, norm_ref, sems):
    half = cand_ref.shape[1] // 2
    core = lax.rem(lax.axis_index("mem"), 2)
    tiles, copies = cand_ref.shape[0] // TILE, []
    for t in range(tiles):
        at = pl.ds(t * TILE, TILE)
        for k, own in enumerate((core, 1 - core)):
            copies.append(
                pltpu.make_async_copy(
                    cand_hbm.at[at, pl.ds(pl.multiple_of(own * half, half), half)],
                    cand_ref.at[at, pl.ds(k * half, half)],
                    sems.at[len(copies)],
                )
            )
    for copy in copies:
        copy.start()
    for t in range(tiles):
        for copy in copies[2 * t : 2 * t + 2]:
            copy.wait()
        squares = jnp.zeros((TILE, 128), F32)
        for k in range(0, cand_ref.shape[1], 128):
            entries = cand_ref[t * TILE : (t + 1) * TILE, k : k + 128].astype(F32)
            squares += entries * entries
        norm_ref[:, t * TILE : (t + 1) * TILE] = jnp.sum(squares.T, axis=0, keepdims=True)


def stack_kernel(start, *refs):
    *blocks, out = refs
    top = 0
    for block in blocks:
        rows = block.shape[0]
        out[top : top + rows, :] = block[:, start : start + out.shape[1]]
        top += rows


def dense_kernel(size, picks_chip, rest_chip, chosen_ref, *refs):
    chips = size // 2
    counts, (own, sib, *outs, select_ref) = refs[:chips], refs[chips:]
    slots, picks = own.shape[0], chosen_ref.shape[1]
    rows_chip = picks_chip + rest_chip
    me = lax.axis_index("mem")
    offsets = [jnp.zeros((1, 1), jnp.int32) for _ in range(2)]
    for d, ref in enumerate(counts):
        for h in range(2):
            origin = lax.bitwise_xor(me, 2 * d + h)
            for k in range(2):
                before = (origin < lax.bitwise_xor(me, k)).astype(jnp.int32)
                offsets[k] += ref[:1, h : h + 1] * before
    lane = lax.broadcasted_iota(jnp.int32, (1, 2 * slots), 1)
    first = lane < slots
    within = jnp.where(first, lane, lane - slots)
    alive = within < jnp.where(first, counts[0][:1, :1], counts[0][:1, 1:2])
    position = jnp.where(alive, within + jnp.where(first, offsets[0], offsets[1]), -1)

    chosen = chosen_ref[...]

    def column(start, length):
        row = lax.broadcasted_iota(jnp.int32, (length, picks), 0)
        across = lax.broadcasted_iota(jnp.int32, (length, picks), 1)
        return jnp.sum(jnp.where(across == row + start, chosen, 0), axis=1, keepdims=True)

    ids = column(0, picks)
    below = jnp.sum((ids < position).astype(jnp.int32), axis=0, keepdims=True)
    taken = jnp.sum((ids == position).astype(jnp.int32), axis=0, keepdims=True)
    rank = jnp.where(alive & (taken == 0), position - below, -1)
    place = lax.broadcasted_iota(jnp.int32, (rest_chip, 1), 0)
    for d in range(chips):
        owner = lax.bitwise_xor(me // 2, d)
        top = d * rows_chip
        hit = column(owner * picks_chip, picks_chip) == position
        select_ref[top : top + picks_chip, :] = hit.astype(F32).astype(BF16)
        hit = place + owner * rest_chip == rank
        select_ref[top + picks_chip : top + rows_chip, :] = hit.astype(F32).astype(BF16)

    @pl.loop(0, own.shape[1] // TILE)
    def _(t):
        at = pl.ds(pl.multiple_of(t * TILE, TILE), TILE)
        rows = jnp.concatenate([own[:, at], sib[:, at]], axis=0)
        found = jnp.dot(select_ref[...], rows, preferred_element_type=F32).astype(BF16)
        for d, out in enumerate(outs):
            out[:, at] = found[d * rows_chip : (d + 1) * rows_chip]


def sum_kernel(*refs):
    *parts, out, picks_ref = refs
    total = parts[0][...]
    for ref in parts[1:]:
        total += ref[...]
    out[...] = total
    picks_ref[...] = total[: picks_ref.shape[0], :]


def row_norms(rows):
    rows = rows.astype(F32)
    return jnp.sum(rows * rows, axis=1, keepdims=True)


def gaps_to(rows_ref, norms, cand):
    inner = lax.dot_general(
        rows_ref[...], cand, (((1,), (1,)), ((), ())), preferred_element_type=F32
    )
    return norms - 2.0 * inner


def tiles_of(cand_ref):
    return [slice(t, t + TILE) for t in range(0, cand_ref.shape[0], TILE)]


def lay_out(row_blocks, rows_ref):
    top = 0
    for parts in row_blocks:
        left, rows = 0, parts[0].shape[0]
        for part in parts:
            rows_ref[top : top + rows, left : left + part.shape[1]] = part[...]
            left += part.shape[1]
        top += rows
    return row_norms(rows_ref[...])


def row_masks(picks_chip, rows_chip, mixed_chip, mixed, rows):
    row = lax.broadcasted_iota(jnp.int32, (rows, 1), 0)
    place = lax.rem(row, mixed_chip)
    own = (row < mixed) & (place < rows_chip)
    pick = (row >= mixed) | (place < picks_chip) | (place >= rows_chip)
    return jnp.where(own, 0.0, jnp.inf), jnp.where(pick, 0.0, jnp.inf)


def least(gaps):
    return jnp.min(gaps, axis=0, keepdims=True)


def first_kernel(chip_rows, cand_ref, own, sib, near_ref, best_ref, rows_ref):
    norms = lay_out([(own, sib)], rows_ref)
    no_row, no_pick = row_masks(*chip_rows, norms.shape[0], norms.shape[0])
    for at in tiles_of(cand_ref):
        gaps = gaps_to(rows_ref, norms, cand_ref[at, :])
        near_ref[:, at] = least(gaps + no_row)
        best_ref[:, at] = least(gaps + no_pick)


def last_kernel(
    chip_rows, cand_ref, norm_ref, near_ref, best_ref, mid, mid_sib, *refs
):
    *corner, near_out, best_out, rows_ref = refs
    norms = lay_out([corner, (mid, mid_sib)], rows_ref)
    no_row, no_pick = row_masks(*chip_rows, corner[0].shape[0], norms.shape[0])
    for at in tiles_of(cand_ref):
        gaps = gaps_to(rows_ref, norms, cand_ref[at, :])
        near_out[:, at] = jnp.minimum(least(gaps + no_row), near_ref[:, at]) + norm_ref[:, at]
        best_out[:, at] = jnp.minimum(least(gaps + no_pick), best_ref[:, at]) + norm_ref[:, at]


def body(candidates, round_one, counts, chosen):
    size, groups = lax.axis_size("mem"), lax.axis_size("grp")
    slots, width = round_one.shape
    half, chips = width // 2, size // 2
    picks, rows = chosen.shape[1], candidates.shape[0]
    picks_chip = picks // chips
    rest_chip = (size * slots * 3 // 8 - picks) // chips
    rows_chip = picks_chip + rest_chip
    live = chips * rows_chip

    def bf16(*dims):
        return jax.ShapeDtypeStruct(dims, BF16)

    def stack(blocks, columns=half, start=0, after=()):
        return call(
            functools.partial(stack_kernel, start), "stack",
            bf16(sum(b.shape[0] for b in blocks), columns), blocks, after=after, weight=0,
        )

    line = jax.ShapeDtypeStruct((1, rows), F32)
    tile = jax.ShapeDtypeStruct((8, 128), jnp.int32)
    count = call(
        spread_kernel, "spread", tile, (counts,), specs=[pl.BlockSpec(memory_space=pltpu.SMEM)]
    )
    pair = call(pair_kernel, "pair", tile, (count, flip_permute(count, size, 1)))
    pairs = to_chips(pair, size)
    own, send = call(split_kernel, "split", [bf16(slots, half)] * 2, (round_one,))
    sib = flip_permute(send, size, 1)

    parts = call(
        functools.partial(dense_kernel, size, picks_chip, rest_chip), "dense",
        [bf16(rows_chip, half)] * chips, (chosen, *pairs, own, sib),
        scratch=[pltpu.VMEM((live, 2 * slots), BF16)],
    )
    cand, norm = call(
        load_kernel, "load", [bf16(rows, width), line], (candidates,),
        specs=[pl.BlockSpec(memory_space=pltpu.HBM)], after=parts[:1],
        scratch=[pltpu.SemaphoreType.DMA((rows // TILE * 2,))], limit=42 * MIB,
    )
    got = [flip_permute(parts[d], size, 2 * d) for d in range(1, chips)]
    owned, picked = call(
        sum_kernel, "owned", [bf16(rows_chip, half), bf16(picks_chip, half)], (parts[0], *got),
        after=(norm,),
    )

    middle = groups // 2
    shifted = [
        lax.ppermute(picked, "grp", [(g, (g + k) % groups) for g in range(groups)])
        for k in range(1, groups)
    ]
    far = [shifted[k - 1] for k in range(1, groups) if k != middle]

    if chips == 4:
        own_x, own_y = (flip_permute(owned, size, flip) for flip in (2, 4))
        close = stack(far, after=(own_x, own_y))
        close_x, close_y = (flip_permute(close, size, flip) for flip in (2, 4))
        early = stack((owned, close, own_x, close_x, own_y, close_y), after=shifted[middle - 1 : middle])
        left = stack((own_x, close_x), half // 2)
        right = stack((own_y, close_y), half // 2, half // 2)
        corner = (flip_permute(left, size, 4), flip_permute(right, size, 2))
    else:
        close = stack(far)
        *early, end = to_chips(stack((owned, close)), size)
        early, corner = stack(early), (end,)
    mid = to_chips(shifted[middle - 1], size)

    chip_rows = (picks_chip, rows_chip, owned.shape[0] + close.shape[0])
    near, best = call(
        functools.partial(first_kernel, chip_rows), "products", [line] * 2,
        (cand, early, flip_permute(early, size, 1)),
        scratch=[pltpu.VMEM((early.shape[0], width), BF16)], weight=WEIGHT // 3,
    )
    mid = stack(mid, after=(best,))
    sent = [stack((part,), part.shape[1], after=(best,)) for part in corner]
    near, final = call(
        functools.partial(last_kernel, chip_rows), "products_last", [line] * 2,
        (
            cand, norm, near, best, mid, flip_permute(mid, size, 1),
            *corner, *[flip_permute(part, size, 1) for part in sent],
        ),
        scratch=[pltpu.VMEM((corner[0].shape[0] + mid.shape[0], width), BF16)],
    )
    return near.reshape(-1), final.reshape(-1)


def solution(mesh):
    in_specs = (P(("grp", "mem"), None), P(("grp", "mem"), None), P("grp", "mem"), P("grp", None))
    out_specs = (P(("grp", "mem")), P(("grp", "mem")))
    return jax.shard_map(body, mesh=mesh, in_specs=in_specs, out_specs=out_specs, check_vma=False)
```

```python
import functools

import jax
import jax.numpy as jnp
from jax import lax
from jax.experimental import pallas as pl
from jax.experimental.pallas import tpu as pltpu
from jax.sharding import PartitionSpec as P

TILE = 256
MIB = 1024 * 1024
WEIGHT = 10**10
F32, BF16 = jnp.float32, jnp.bfloat16


def flip_permute(block, size, flip):
    return lax.ppermute(block, "mem", [(m, m ^ flip) for m in range(size)])


def to_chips(block, size):
    return [block] + [flip_permute(block, size, 2 * d) for d in range(1, size // 2)]


def vmem_specs(count):
    return [pl.BlockSpec(memory_space=pltpu.VMEM)] * count


def call(kernel, name, out_shape, operands, specs=None, scratch=(), after=(), limit=28 * MIB, weight=WEIGHT):
    shapes = jax.tree.leaves(out_shape)
    moved = sum(a.size * a.dtype.itemsize for a in list(operands) + shapes)
    count = len(operands)

    def run(*refs):
        kernel(*refs[:count], *refs[count + len(after) :])

    return pl.pallas_call(
        run,
        out_shape=out_shape,
        in_specs=(specs or vmem_specs(count)) + [pl.BlockSpec(memory_space=pl.ANY)] * len(after),
        out_specs=jax.tree.map(lambda _: pl.BlockSpec(memory_space=pltpu.VMEM), out_shape),
        scratch_shapes=scratch,
        compiler_params=pltpu.CompilerParams(vmem_limit_bytes=limit),
        cost_estimate=pl.CostEstimate(flops=weight, bytes_accessed=moved, transcendentals=0),
        name=name,
    )(*operands, *after)


def spread_kernel(count_ref, out):
    out[...] = jnp.broadcast_to(count_ref[0, 0], out.shape)


def pair_kernel(own, sib, out):
    lane = lax.broadcasted_iota(jnp.int32, out.shape, 1)
    out[...] = jnp.where(lane == 0, own[...], sib[...])


def split_kernel(rows_ref, keep_ref, send_ref):
    half = keep_ref.shape[1]
    core = lax.rem(lax.axis_index("mem"), 2)
    keep_ref[...] = rows_ref[:, pl.ds(pl.multiple_of(core * half, half), half)]
    send_ref[...] = rows_ref[:, pl.ds(pl.multiple_of((1 - core) * half, half), half)]


def load_kernel(cand_hbm, cand_ref, norm_ref, sems):
    half = cand_ref.shape[1] // 2
    core = lax.rem(lax.axis_index("mem"), 2)
    tiles, copies = cand_ref.shape[0] // TILE, []
    for t in range(tiles):
        at = pl.ds(t * TILE, TILE)
        for k, own in enumerate((core, 1 - core)):
            copies.append(
                pltpu.make_async_copy(
                    cand_hbm.at[at, pl.ds(pl.multiple_of(own * half, half), half)],
                    cand_ref.at[at, pl.ds(k * half, half)],
                    sems.at[len(copies)],
                )
            )
    for copy in copies:
        copy.start()
    for t in range(tiles):
        for copy in copies[2 * t : 2 * t + 2]:
            copy.wait()
        squares = jnp.zeros((TILE, 128), F32)
        for k in range(0, cand_ref.shape[1], 128):
            entries = cand_ref[t * TILE : (t + 1) * TILE, k : k + 128].astype(F32)
            squares += entries * entries
        norm_ref[:, t * TILE : (t + 1) * TILE] = jnp.sum(squares.T, axis=0, keepdims=True)


def stack_kernel(start, *refs):
    *blocks, out = refs
    top = 0
    for block in blocks:
        rows = block.shape[0]
        out[top : top + rows, :] = block[:, start : start + out.shape[1]]
        top += rows


def dense_kernel(size, picks_chip, rest_chip, chosen_ref, *refs):
    chips = size // 2
    counts, (own, sib, *outs, select_ref) = refs[:chips], refs[chips:]
    slots, picks = own.shape[0], chosen_ref.shape[1]
    rows_chip = picks_chip + rest_chip
    me = lax.axis_index("mem")
    offsets = [jnp.zeros((1, 1), jnp.int32) for _ in range(2)]
    for d, ref in enumerate(counts):
        for h in range(2):
            origin = lax.bitwise_xor(me, 2 * d + h)
            for k in range(2):
                before = (origin < lax.bitwise_xor(me, k)).astype(jnp.int32)
                offsets[k] += ref[:1, h : h + 1] * before
    lane = lax.broadcasted_iota(jnp.int32, (1, 2 * slots), 1)
    first = lane < slots
    within = jnp.where(first, lane, lane - slots)
    alive = within < jnp.where(first, counts[0][:1, :1], counts[0][:1, 1:2])
    position = jnp.where(alive, within + jnp.where(first, offsets[0], offsets[1]), -1)

    chosen = chosen_ref[...]

    def column(start, length):
        row = lax.broadcasted_iota(jnp.int32, (length, picks), 0)
        across = lax.broadcasted_iota(jnp.int32, (length, picks), 1)
        return jnp.sum(jnp.where(across == row + start, chosen, 0), axis=1, keepdims=True)

    ids = column(0, picks)
    below = jnp.sum((ids < position).astype(jnp.int32), axis=0, keepdims=True)
    taken = jnp.sum((ids == position).astype(jnp.int32), axis=0, keepdims=True)
    rank = jnp.where(alive & (taken == 0), position - below, -1)
    place = lax.broadcasted_iota(jnp.int32, (rest_chip, 1), 0)
    for d in range(chips):
        owner = lax.bitwise_xor(me // 2, d)
        top = d * rows_chip
        hit = column(owner * picks_chip, picks_chip) == position
        select_ref[top : top + picks_chip, :] = hit.astype(F32).astype(BF16)
        hit = place + owner * rest_chip == rank
        select_ref[top + picks_chip : top + rows_chip, :] = hit.astype(F32).astype(BF16)

    @pl.loop(0, own.shape[1] // TILE)
    def _(t):
        at = pl.ds(pl.multiple_of(t * TILE, TILE), TILE)
        rows = jnp.concatenate([own[:, at], sib[:, at]], axis=0)
        found = jnp.dot(select_ref[...], rows, preferred_element_type=F32).astype(BF16)
        for d, out in enumerate(outs):
            out[:, at] = found[d * rows_chip : (d + 1) * rows_chip]


def sum_kernel(*refs):
    *parts, out, picks_ref = refs
    total = parts[0][...]
    for ref in parts[1:]:
        total += ref[...]
    out[...] = total
    picks_ref[...] = total[: picks_ref.shape[0], :]


def row_norms(rows):
    rows = rows.astype(F32)
    return jnp.sum(rows * rows, axis=1, keepdims=True)


def gaps_to(rows_ref, norms, cand):
    inner = lax.dot_general(
        rows_ref[...], cand, (((1,), (1,)), ((), ())), preferred_element_type=F32
    )
    return norms - 2.0 * inner


def tiles_of(cand_ref):
    return [slice(t, t + TILE) for t in range(0, cand_ref.shape[0], TILE)]


def lay_out(row_blocks, rows_ref):
    top = 0
    for parts in row_blocks:
        left, rows = 0, parts[0].shape[0]
        for part in parts:
            rows_ref[top : top + rows, left : left + part.shape[1]] = part[...]
            left += part.shape[1]
        top += rows
    return row_norms(rows_ref[...])


def row_masks(picks_chip, rows_chip, mixed_chip, mixed, rows):
    row = lax.broadcasted_iota(jnp.int32, (rows, 1), 0)
    place = lax.rem(row, mixed_chip)
    own = (row < mixed) & (place < rows_chip)
    pick = (row >= mixed) | (place < picks_chip) | (place >= rows_chip)
    return jnp.where(own, 0.0, jnp.inf), jnp.where(pick, 0.0, jnp.inf)


def least(gaps):
    return jnp.min(gaps, axis=0, keepdims=True)


def first_kernel(chip_rows, cand_ref, own, sib, near_ref, best_ref, rows_ref):
    norms = lay_out([(own, sib)], rows_ref)
    no_row, no_pick = row_masks(*chip_rows, norms.shape[0], norms.shape[0])
    for at in tiles_of(cand_ref):
        gaps = gaps_to(rows_ref, norms, cand_ref[at, :])
        near_ref[:, at] = least(gaps + no_row)
        best_ref[:, at] = least(gaps + no_pick)


def last_kernel(
    chip_rows, cand_ref, norm_ref, near_ref, best_ref, mid, mid_sib, *refs
):
    *corner, near_out, best_out, rows_ref = refs
    norms = lay_out([corner, (mid, mid_sib)], rows_ref)
    no_row, no_pick = row_masks(*chip_rows, corner[0].shape[0], norms.shape[0])
    for at in tiles_of(cand_ref):
        gaps = gaps_to(rows_ref, norms, cand_ref[at, :])
        near_out[:, at] = jnp.minimum(least(gaps + no_row), near_ref[:, at]) + norm_ref[:, at]
        best_out[:, at] = jnp.minimum(least(gaps + no_pick), best_ref[:, at]) + norm_ref[:, at]


def body(candidates, round_one, counts, chosen):
    size, groups = lax.axis_size("mem"), lax.axis_size("grp")
    slots, width = round_one.shape
    half, chips = width // 2, size // 2
    picks, rows = chosen.shape[1], candidates.shape[0]
    picks_chip = picks // chips
    rest_chip = (size * slots * 3 // 8 - picks) // chips
    rows_chip = picks_chip + rest_chip
    live = chips * rows_chip

    def bf16(*dims):
        return jax.ShapeDtypeStruct(dims, BF16)

    def stack(blocks, columns=half, start=0, after=()):
        return call(
            functools.partial(stack_kernel, start), "stack",
            bf16(sum(b.shape[0] for b in blocks), columns), blocks, after=after, weight=0,
        )

    line = jax.ShapeDtypeStruct((1, rows), F32)
    tile = jax.ShapeDtypeStruct((8, 128), jnp.int32)
    count = call(
        spread_kernel, "spread", tile, (counts,), specs=[pl.BlockSpec(memory_space=pltpu.SMEM)]
    )
    pair = call(pair_kernel, "pair", tile, (count, flip_permute(count, size, 1)))
    pairs = to_chips(pair, size)
    own, send = call(split_kernel, "split", [bf16(slots, half)] * 2, (round_one,))
    sib = flip_permute(send, size, 1)

    parts = call(
        functools.partial(dense_kernel, size, picks_chip, rest_chip), "dense",
        [bf16(rows_chip, half)] * chips, (chosen, *pairs, own, sib),
        scratch=[pltpu.VMEM((live, 2 * slots), BF16)],
    )
    cand, norm = call(
        load_kernel, "load", [bf16(rows, width), line], (candidates,),
        specs=[pl.BlockSpec(memory_space=pltpu.HBM)], after=parts[:1],
        scratch=[pltpu.SemaphoreType.DMA((rows // TILE * 2,))], limit=42 * MIB,
    )
    got = [flip_permute(parts[d], size, 2 * d) for d in range(1, chips)]
    owned, picked = call(
        sum_kernel, "owned", [bf16(rows_chip, half), bf16(picks_chip, half)], (parts[0], *got),
        after=(norm,),
    )

    middle = groups // 2
    shifted = [
        lax.ppermute(picked, "grp", [(g, (g + k) % groups) for g in range(groups)])
        for k in range(1, groups)
    ]
    far = [shifted[k - 1] for k in range(1, groups) if k != middle]

    if chips == 4:
        own_x, own_y = (flip_permute(owned, size, flip) for flip in (2, 4))
        close = stack(far, after=(own_x, own_y))
        close_x, close_y = (flip_permute(close, size, flip) for flip in (2, 4))
        early = stack((owned, close, own_x, close_x, own_y, close_y), after=shifted[middle - 1 : middle])
        left = stack((own_x, close_x), half // 2)
        right = stack((own_y, close_y), half // 2, half // 2)
        corner = (flip_permute(left, size, 4), flip_permute(right, size, 2))
    else:
        close = stack(far)
        *early, end = to_chips(stack((owned, close)), size)
        early, corner = stack(early), (end,)
    mid = to_chips(shifted[middle - 1], size)

    chip_rows = (picks_chip, rows_chip, owned.shape[0] + close.shape[0])
    near, best = call(
        functools.partial(first_kernel, chip_rows), "products", [line] * 2,
        (cand, early, flip_permute(early, size, 1)),
        scratch=[pltpu.VMEM((early.shape[0], width), BF16)], weight=WEIGHT // 3,
    )
    mid = stack(mid, after=(best, *corner))
    sent = [stack((part,), part.shape[1], after=(best,)) for part in corner]
    near, final = call(
        functools.partial(last_kernel, chip_rows), "products_last", [line] * 2,
        (
            cand, norm, near, best, mid, flip_permute(mid, size, 1),
            *corner, *[flip_permute(part, size, 1) for part in sent],
        ),
        scratch=[pltpu.VMEM((corner[0].shape[0] + mid.shape[0], width), BF16)],
    )
    return near.reshape(-1), final.reshape(-1)


def solution(mesh):
    in_specs = (P(("grp", "mem"), None), P(("grp", "mem"), None), P("grp", "mem"), P("grp", None))
    out_specs = (P(("grp", "mem")), P(("grp", "mem")))
    return jax.shard_map(body, mesh=mesh, in_specs=in_specs, out_specs=out_specs, check_vma=False)
```

```python
import functools

import jax
import jax.numpy as jnp
from jax import lax
from jax.experimental import pallas as pl
from jax.experimental.pallas import tpu as pltpu
from jax.sharding import PartitionSpec as P

TILE = 256
MIB = 1024 * 1024
WEIGHT = 10**10
F32, BF16 = jnp.float32, jnp.bfloat16


def flip_permute(block, size, flip):
    return lax.ppermute(block, "mem", [(m, m ^ flip) for m in range(size)])


def to_chips(block, size):
    return [block] + [flip_permute(block, size, 2 * d) for d in range(1, size // 2)]


def vmem_specs(count):
    return [pl.BlockSpec(memory_space=pltpu.VMEM)] * count


def call(kernel, name, out_shape, operands, specs=None, scratch=(), after=(), limit=28 * MIB, weight=WEIGHT):
    shapes = jax.tree.leaves(out_shape)
    moved = sum(a.size * a.dtype.itemsize for a in list(operands) + shapes)
    count = len(operands)

    def run(*refs):
        kernel(*refs[:count], *refs[count + len(after) :])

    return pl.pallas_call(
        run,
        out_shape=out_shape,
        in_specs=(specs or vmem_specs(count)) + [pl.BlockSpec(memory_space=pl.ANY)] * len(after),
        out_specs=jax.tree.map(lambda _: pl.BlockSpec(memory_space=pltpu.VMEM), out_shape),
        scratch_shapes=scratch,
        compiler_params=pltpu.CompilerParams(vmem_limit_bytes=limit),
        cost_estimate=pl.CostEstimate(flops=weight, bytes_accessed=moved, transcendentals=0),
        name=name,
    )(*operands, *after)


def spread_kernel(count_ref, out):
    out[...] = jnp.broadcast_to(count_ref[0, 0], out.shape)


def pair_kernel(own, sib, out):
    lane = lax.broadcasted_iota(jnp.int32, out.shape, 1)
    out[...] = jnp.where(lane == 0, own[...], sib[...])


def split_kernel(rows_ref, keep_ref, send_ref):
    half = keep_ref.shape[1]
    core = lax.rem(lax.axis_index("mem"), 2)
    keep_ref[...] = rows_ref[:, pl.ds(pl.multiple_of(core * half, half), half)]
    send_ref[...] = rows_ref[:, pl.ds(pl.multiple_of((1 - core) * half, half), half)]


def load_kernel(cand_hbm, cand_ref, norm_ref, sems):
    half = cand_ref.shape[1] // 2
    core = lax.rem(lax.axis_index("mem"), 2)
    tiles, copies = cand_ref.shape[0] // TILE, []
    for t in range(tiles):
        at = pl.ds(t * TILE, TILE)
        for k, own in enumerate((core, 1 - core)):
            copies.append(
                pltpu.make_async_copy(
                    cand_hbm.at[at, pl.ds(pl.multiple_of(own * half, half), half)],
                    cand_ref.at[at, pl.ds(k * half, half)],
                    sems.at[len(copies)],
                )
            )
    for copy in copies:
        copy.start()
    for t in range(tiles):
        for copy in copies[2 * t : 2 * t + 2]:
            copy.wait()
        squares = jnp.zeros((TILE, 128), F32)
        for k in range(0, cand_ref.shape[1], 128):
            entries = cand_ref[t * TILE : (t + 1) * TILE, k : k + 128].astype(F32)
            squares += entries * entries
        norm_ref[:, t * TILE : (t + 1) * TILE] = jnp.sum(squares.T, axis=0, keepdims=True)


def stack_kernel(start, *refs):
    *blocks, out = refs
    top = 0
    for block in blocks:
        rows = block.shape[0]
        out[top : top + rows, :] = block[:, start : start + out.shape[1]]
        top += rows


def dense_kernel(size, picks_chip, rest_chip, chosen_ref, *refs):
    chips = size // 2
    counts, (own, sib, *outs, select_ref) = refs[:chips], refs[chips:]
    slots, picks = own.shape[0], chosen_ref.shape[1]
    rows_chip = picks_chip + rest_chip
    me = lax.axis_index("mem")
    offsets = [jnp.zeros((1, 1), jnp.int32) for _ in range(2)]
    for d, ref in enumerate(counts):
        for h in range(2):
            origin = lax.bitwise_xor(me, 2 * d + h)
            for k in range(2):
                before = (origin < lax.bitwise_xor(me, k)).astype(jnp.int32)
                offsets[k] += ref[:1, h : h + 1] * before
    lane = lax.broadcasted_iota(jnp.int32, (1, 2 * slots), 1)
    first = lane < slots
    within = jnp.where(first, lane, lane - slots)
    alive = within < jnp.where(first, counts[0][:1, :1], counts[0][:1, 1:2])
    position = jnp.where(alive, within + jnp.where(first, offsets[0], offsets[1]), -1)

    chosen = chosen_ref[...]

    def column(start, length):
        row = lax.broadcasted_iota(jnp.int32, (length, picks), 0)
        across = lax.broadcasted_iota(jnp.int32, (length, picks), 1)
        return jnp.sum(jnp.where(across == row + start, chosen, 0), axis=1, keepdims=True)

    ids = column(0, picks)
    below = jnp.sum((ids < position).astype(jnp.int32), axis=0, keepdims=True)
    taken = jnp.sum((ids == position).astype(jnp.int32), axis=0, keepdims=True)
    rank = jnp.where(alive & (taken == 0), position - below, -1)
    place = lax.broadcasted_iota(jnp.int32, (rest_chip, 1), 0)
    for d in range(chips):
        owner = lax.bitwise_xor(me // 2, d)
        top = d * rows_chip
        hit = column(owner * picks_chip, picks_chip) == position
        select_ref[top : top + picks_chip, :] = hit.astype(F32).astype(BF16)
        hit = place + owner * rest_chip == rank
        select_ref[top + picks_chip : top + rows_chip, :] = hit.astype(F32).astype(BF16)

    @pl.loop(0, own.shape[1] // TILE)
    def _(t):
        at = pl.ds(pl.multiple_of(t * TILE, TILE), TILE)
        rows = jnp.concatenate([own[:, at], sib[:, at]], axis=0)
        found = jnp.dot(select_ref[...], rows, preferred_element_type=F32).astype(BF16)
        for d, out in enumerate(outs):
            out[:, at] = found[d * rows_chip : (d + 1) * rows_chip]


def sum_kernel(*refs):
    *parts, out, picks_ref = refs
    total = parts[0][...]
    for ref in parts[1:]:
        total += ref[...]
    out[...] = total
    picks_ref[...] = total[: picks_ref.shape[0], :]


def row_norms(rows):
    rows = rows.astype(F32)
    return jnp.sum(rows * rows, axis=1, keepdims=True)


def gaps_to(rows_ref, norms, cand):
    inner = lax.dot_general(
        rows_ref[...], cand, (((1,), (1,)), ((), ())), preferred_element_type=F32
    )
    return norms - 2.0 * inner


def tiles_of(cand_ref):
    return [slice(t, t + TILE) for t in range(0, cand_ref.shape[0], TILE)]


def lay_out(row_blocks, rows_ref):
    top = 0
    for parts in row_blocks:
        left, rows = 0, parts[0].shape[0]
        for part in parts:
            rows_ref[top : top + rows, left : left + part.shape[1]] = part[...]
            left += part.shape[1]
        top += rows
    return row_norms(rows_ref[...])


def row_masks(picks_chip, rows_chip, all_chip, rows):
    place = lax.rem(lax.broadcasted_iota(jnp.int32, (rows, 1), 0), all_chip)
    own = place < rows_chip
    pick = (place < picks_chip) | ~own
    return jnp.where(own, 0.0, jnp.inf), jnp.where(pick, 0.0, jnp.inf)


def least(gaps):
    return jnp.min(gaps, axis=0, keepdims=True)


def first_kernel(chip_rows, cand_ref, own, sib, near_ref, best_ref, rows_ref):
    norms = lay_out([(own, sib)], rows_ref)
    no_row, no_pick = row_masks(*chip_rows, norms.shape[0])
    for at in tiles_of(cand_ref):
        gaps = gaps_to(rows_ref, norms, cand_ref[at, :])
        near_ref[:, at] = least(gaps + no_row)
        best_ref[:, at] = least(gaps + no_pick)


def half_kernel(cand_ref, *refs):
    *corner, out, rows_ref = refs
    norms = lay_out([corner], rows_ref)
    for at in tiles_of(cand_ref):
        out[:, at] = gaps_to(rows_ref, norms, cand_ref[at, : rows_ref.shape[1]])


def last_kernel(chip_rows, cand_ref, norm_ref, near_ref, best_ref, part_ref, *refs):
    *corner, near_out, best_out, rows_ref = refs
    norms = lay_out([corner], rows_ref)
    no_row, no_pick = row_masks(*chip_rows, norms.shape[0])
    for at in tiles_of(cand_ref):
        gaps = part_ref[:, at] + gaps_to(rows_ref, norms, cand_ref[at, rows_ref.shape[1] :])
        near_out[:, at] = jnp.minimum(least(gaps + no_row), near_ref[:, at]) + norm_ref[:, at]
        best_out[:, at] = jnp.minimum(least(gaps + no_pick), best_ref[:, at]) + norm_ref[:, at]


def body(candidates, round_one, counts, chosen):
    size, groups = lax.axis_size("mem"), lax.axis_size("grp")
    slots, width = round_one.shape
    half, chips = width // 2, size // 2
    picks, rows = chosen.shape[1], candidates.shape[0]
    picks_chip = picks // chips
    rest_chip = (size * slots * 3 // 8 - picks) // chips
    rows_chip = picks_chip + rest_chip
    live = chips * rows_chip

    def bf16(*dims):
        return jax.ShapeDtypeStruct(dims, BF16)

    def stack(blocks, columns=half, start=0, after=()):
        return call(
            functools.partial(stack_kernel, start), "stack",
            bf16(sum(b.shape[0] for b in blocks), columns), blocks, after=after, weight=0,
        )

    line = jax.ShapeDtypeStruct((1, rows), F32)
    tile = jax.ShapeDtypeStruct((8, 128), jnp.int32)
    count = call(
        spread_kernel, "spread", tile, (counts,), specs=[pl.BlockSpec(memory_space=pltpu.SMEM)]
    )
    pair = call(pair_kernel, "pair", tile, (count, flip_permute(count, size, 1)))
    pairs = to_chips(pair, size)
    own, send = call(split_kernel, "split", [bf16(slots, half)] * 2, (round_one,))
    sib = flip_permute(send, size, 1)

    parts = call(
        functools.partial(dense_kernel, size, picks_chip, rest_chip), "dense",
        [bf16(rows_chip, half)] * chips, (chosen, *pairs, own, sib),
        scratch=[pltpu.VMEM((live, 2 * slots), BF16)],
    )
    cand, norm = call(
        load_kernel, "load", [bf16(rows, width), line], (candidates,),
        specs=[pl.BlockSpec(memory_space=pltpu.HBM)], after=parts[:1],
        scratch=[pltpu.SemaphoreType.DMA((rows // TILE * 2,))], limit=42 * MIB,
    )
    got = [flip_permute(parts[d], size, 2 * d) for d in range(1, chips)]
    owned, picked = call(
        sum_kernel, "owned", [bf16(rows_chip, half), bf16(picks_chip, half)], (parts[0], *got),
        after=(norm,),
    )

    shifted = [
        lax.ppermute(picked, "grp", [(g, (g + k) % groups) for g in range(groups)])
        for k in range(1, groups)
    ]

    if chips == 4:
        own_x, own_y = (flip_permute(owned, size, flip) for flip in (2, 4))
        far = stack(shifted, after=(own_x, own_y))
        far_x, far_y = (flip_permute(far, size, flip) for flip in (2, 4))
        left = stack((own_x, far_x), half // 2)
        right = stack((own_y, far_y), half // 2, half // 2)
        early = stack((owned, far, own_x, far_x, own_y, far_y))
        corner = (flip_permute(left, size, 4), flip_permute(right, size, 2))
    else:
        far = stack(shifted)
        *early, end = to_chips(stack((owned, far)), size)
        early, corner = stack(early), (end,)

    chip_rows = (picks_chip, rows_chip, owned.shape[0] + far.shape[0])
    near, best = call(
        functools.partial(first_kernel, chip_rows), "products", [line] * 2,
        (cand, early, flip_permute(early, size, 1)),
        scratch=[pltpu.VMEM((early.shape[0], width), BF16)], weight=WEIGHT // 3,
    )
    sent = [stack((part,), part.shape[1], after=(best,)) for part in corner]
    swapped = [flip_permute(part, size, 1) for part in sent]
    rows_end = corner[0].shape[0]
    scratch = [pltpu.VMEM((rows_end, half), BF16)]
    part = call(
        half_kernel, "products_half", jax.ShapeDtypeStruct((rows_end, rows), F32), (cand, *corner),
        scratch=scratch, after=(best,),
    )
    near, final = call(
        functools.partial(last_kernel, chip_rows), "products_last", [line] * 2,
        (cand, norm, near, best, part, *swapped), scratch=scratch,
    )
    return near.reshape(-1), final.reshape(-1)


def solution(mesh):
    in_specs = (P(("grp", "mem"), None), P(("grp", "mem"), None), P("grp", "mem"), P("grp", None))
    out_specs = (P(("grp", "mem")), P(("grp", "mem")))
    return jax.shard_map(body, mesh=mesh, in_specs=in_specs, out_specs=out_specs, check_vma=False)
```

```python
import functools

import jax
import jax.numpy as jnp
from jax import lax
from jax.experimental import pallas as pl
from jax.experimental.pallas import tpu as pltpu
from jax.sharding import PartitionSpec as P

TILE = 256
MIB = 1024 * 1024
WEIGHT = 10**10
F32, BF16 = jnp.float32, jnp.bfloat16


def flip_permute(block, size, flip):
    return lax.ppermute(block, "mem", [(m, m ^ flip) for m in range(size)])


def to_chips(block, size):
    return [block] + [flip_permute(block, size, 2 * d) for d in range(1, size // 2)]


def vmem_specs(count):
    return [pl.BlockSpec(memory_space=pltpu.VMEM)] * count


def call(kernel, name, out_shape, operands, specs=None, scratch=(), after=(), limit=28 * MIB, weight=WEIGHT):
    shapes = jax.tree.leaves(out_shape)
    moved = sum(a.size * a.dtype.itemsize for a in list(operands) + shapes)
    count = len(operands)

    def run(*refs):
        kernel(*refs[:count], *refs[count + len(after) :])

    return pl.pallas_call(
        run,
        out_shape=out_shape,
        in_specs=(specs or vmem_specs(count)) + [pl.BlockSpec(memory_space=pl.ANY)] * len(after),
        out_specs=jax.tree.map(lambda _: pl.BlockSpec(memory_space=pltpu.VMEM), out_shape),
        scratch_shapes=scratch,
        compiler_params=pltpu.CompilerParams(vmem_limit_bytes=limit),
        cost_estimate=pl.CostEstimate(flops=weight, bytes_accessed=moved, transcendentals=0),
        name=name,
    )(*operands, *after)


def spread_kernel(count_ref, out):
    out[...] = jnp.broadcast_to(count_ref[0, 0], out.shape)


def pair_kernel(own, sib, out):
    lane = lax.broadcasted_iota(jnp.int32, out.shape, 1)
    out[...] = jnp.where(lane == 0, own[...], sib[...])


def split_kernel(rows_ref, keep_ref, send_ref):
    half = keep_ref.shape[1]
    core = lax.rem(lax.axis_index("mem"), 2)
    keep_ref[...] = rows_ref[:, pl.ds(pl.multiple_of(core * half, half), half)]
    send_ref[...] = rows_ref[:, pl.ds(pl.multiple_of((1 - core) * half, half), half)]


def load_kernel(cand_hbm, cand_ref, norm_ref, sems):
    half = cand_ref.shape[1] // 2
    core = lax.rem(lax.axis_index("mem"), 2)
    tiles, copies = cand_ref.shape[0] // TILE, []
    for t in range(tiles):
        at = pl.ds(t * TILE, TILE)
        for k, own in enumerate((core, 1 - core)):
            copies.append(
                pltpu.make_async_copy(
                    cand_hbm.at[at, pl.ds(pl.multiple_of(own * half, half), half)],
                    cand_ref.at[at, pl.ds(k * half, half)],
                    sems.at[len(copies)],
                )
            )
    for copy in copies:
        copy.start()
    for t in range(tiles):
        for copy in copies[2 * t : 2 * t + 2]:
            copy.wait()
        squares = jnp.zeros((TILE, 128), F32)
        for k in range(0, cand_ref.shape[1], 128):
            entries = cand_ref[t * TILE : (t + 1) * TILE, k : k + 128].astype(F32)
            squares += entries * entries
        norm_ref[:, t * TILE : (t + 1) * TILE] = jnp.sum(squares.T, axis=0, keepdims=True)


def stack_kernel(layout, *refs):
    out, top = refs[-1], 0
    for parts in layout:
        left, rows = 0, refs[parts[0][0]].shape[0]
        for index, start, columns in parts:
            out[top : top + rows, left : left + columns] = refs[index][:, start : start + columns]
            left += columns
        top += rows


def dense_kernel(size, picks_chip, rest_chip, chosen_ref, *refs):
    chips = size // 2
    counts, (own, sib, *outs, select_ref) = refs[:chips], refs[chips:]
    slots, picks = own.shape[0], chosen_ref.shape[1]
    rows_chip = picks_chip + rest_chip
    me = lax.axis_index("mem")
    offsets = [jnp.zeros((1, 1), jnp.int32) for _ in range(2)]
    for d, ref in enumerate(counts):
        for h in range(2):
            origin = lax.bitwise_xor(me, 2 * d + h)
            for k in range(2):
                before = (origin < lax.bitwise_xor(me, k)).astype(jnp.int32)
                offsets[k] += ref[:1, h : h + 1] * before
    lane = lax.broadcasted_iota(jnp.int32, (1, 2 * slots), 1)
    first = lane < slots
    within = jnp.where(first, lane, lane - slots)
    alive = within < jnp.where(first, counts[0][:1, :1], counts[0][:1, 1:2])
    position = jnp.where(alive, within + jnp.where(first, offsets[0], offsets[1]), -1)

    chosen = chosen_ref[...]

    def column(start, length):
        row = lax.broadcasted_iota(jnp.int32, (length, picks), 0)
        across = lax.broadcasted_iota(jnp.int32, (length, picks), 1)
        return jnp.sum(jnp.where(across == row + start, chosen, 0), axis=1, keepdims=True)

    ids = column(0, picks)
    below = jnp.sum((ids < position).astype(jnp.int32), axis=0, keepdims=True)
    taken = jnp.sum((ids == position).astype(jnp.int32), axis=0, keepdims=True)
    rank = jnp.where(alive & (taken == 0), position - below, -1)
    place = lax.broadcasted_iota(jnp.int32, (rest_chip, 1), 0)
    for d in range(chips):
        owner = lax.bitwise_xor(me // 2, d)
        top = d * rows_chip
        hit = column(owner * picks_chip, picks_chip) == position
        select_ref[top : top + picks_chip, :] = hit.astype(F32).astype(BF16)
        hit = place + owner * rest_chip == rank
        select_ref[top + picks_chip : top + rows_chip, :] = hit.astype(F32).astype(BF16)

    @pl.loop(0, own.shape[1] // TILE)
    def _(t):
        at = pl.ds(pl.multiple_of(t * TILE, TILE), TILE)
        rows = jnp.concatenate([own[:, at], sib[:, at]], axis=0)
        found = jnp.dot(select_ref[...], rows, preferred_element_type=F32).astype(BF16)
        for d, out in enumerate(outs):
            out[:, at] = found[d * rows_chip : (d + 1) * rows_chip]


def sum_kernel(*refs):
    *parts, out, picks_ref = refs
    total = parts[0][...]
    for ref in parts[1:]:
        total += ref[...]
    out[...] = total
    picks_ref[...] = total[: picks_ref.shape[0], :]


def row_norms(rows):
    rows = rows.astype(F32)
    return jnp.sum(rows * rows, axis=1, keepdims=True)


def gaps_to(rows_ref, norms, cand):
    inner = lax.dot_general(
        rows_ref[...], cand, (((1,), (1,)), ((), ())), preferred_element_type=F32
    )
    return norms - 2.0 * inner


def tiles_of(cand_ref):
    return [slice(t, t + TILE) for t in range(0, cand_ref.shape[0], TILE)]


def lay_out(parts, rows_ref):
    left = 0
    for part in parts:
        rows_ref[:, left : left + part.shape[1]] = part[...]
        left += part.shape[1]
    return row_norms(rows_ref[...])


def row_masks(picks_chip, rows_chip, own_rows, rows):
    row = lax.broadcasted_iota(jnp.int32, (rows, 1), 0)
    own = row < own_rows
    pick = (lax.rem(row, rows_chip) < picks_chip) | ~own
    return jnp.where(own, 0.0, jnp.inf), jnp.where(pick, 0.0, jnp.inf)


def least(gaps):
    return jnp.min(gaps, axis=0, keepdims=True)


def first_kernel(chip_rows, cand_ref, own, sib, near_ref, best_ref, rows_ref):
    norms = lay_out((own, sib), rows_ref)
    no_row, no_pick = row_masks(*chip_rows, norms.shape[0])
    for at in tiles_of(cand_ref):
        gaps = gaps_to(rows_ref, norms, cand_ref[at, :])
        near_ref[:, at] = least(gaps + no_row)
        best_ref[:, at] = least(gaps + no_pick)


def next_kernel(blocks, cand_ref, best_ref, *refs):
    *parts, out, rows_ref = refs
    norms, count, rows = [], len(parts) // blocks, rows_ref.shape[0] // blocks
    for b in range(blocks):
        block = rows_ref.at[b * rows : (b + 1) * rows, :]
        norms.append(lay_out(parts[b * count : (b + 1) * count], block))
    norms = jnp.concatenate(norms, axis=0)
    for at in tiles_of(cand_ref):
        gaps = gaps_to(rows_ref, norms, cand_ref[at, :])
        out[:, at] = jnp.minimum(least(gaps), best_ref[:, at])


def half_kernel(cand_ref, *refs):
    *corner, out, rows_ref = refs
    norms = lay_out(corner, rows_ref)
    for at in tiles_of(cand_ref):
        out[:, at] = gaps_to(rows_ref, norms, cand_ref[at, : rows_ref.shape[1]])


def last_kernel(chip_rows, cand_ref, norm_ref, near_ref, best_ref, part_ref, *refs):
    *corner, near_out, best_out, rows_ref = refs
    norms = lay_out(corner, rows_ref)
    no_row, no_pick = row_masks(*chip_rows, norms.shape[0])
    for at in tiles_of(cand_ref):
        gaps = part_ref[:, at] + gaps_to(rows_ref, norms, cand_ref[at, rows_ref.shape[1] :])
        near_out[:, at] = jnp.minimum(least(gaps + no_row), near_ref[:, at]) + norm_ref[:, at]
        best_out[:, at] = jnp.minimum(least(gaps + no_pick), best_ref[:, at]) + norm_ref[:, at]


def body(candidates, round_one, counts, chosen):
    size, groups = lax.axis_size("mem"), lax.axis_size("grp")
    slots, width = round_one.shape
    half, chips = width // 2, size // 2
    picks, rows = chosen.shape[1], candidates.shape[0]
    picks_chip = picks // chips
    rest_chip = (size * slots * 3 // 8 - picks) // chips
    rows_chip = picks_chip + rest_chip
    live = chips * rows_chip

    def bf16(*dims):
        return jax.ShapeDtypeStruct(dims, BF16)

    def stack(*blocks, after=()):
        operands, layout = [], []
        for block in blocks:
            parts = [p if isinstance(p, tuple) else (p, 0, p.shape[1]) for p in block]
            layout.append([(len(operands) + i, *p[1:]) for i, p in enumerate(parts)])
            operands += [p[0] for p in parts]
        shape = bf16(
            sum(operands[parts[0][0]].shape[0] for parts in layout), sum(p[2] for p in layout[0])
        )
        return call(
            functools.partial(stack_kernel, layout), "stack", shape, operands, after=after, weight=0
        )

    line = jax.ShapeDtypeStruct((1, rows), F32)
    tile = jax.ShapeDtypeStruct((8, 128), jnp.int32)
    count = call(
        spread_kernel, "spread", tile, (counts,), specs=[pl.BlockSpec(memory_space=pltpu.SMEM)]
    )
    pair = call(pair_kernel, "pair", tile, (count, flip_permute(count, size, 1)))
    pairs = to_chips(pair, size)
    own, send = call(split_kernel, "split", [bf16(slots, half)] * 2, (round_one,))
    sib = flip_permute(send, size, 1)

    parts = call(
        functools.partial(dense_kernel, size, picks_chip, rest_chip), "dense",
        [bf16(rows_chip, half)] * chips, (chosen, *pairs, own, sib),
        scratch=[pltpu.VMEM((live, 2 * slots), BF16)],
    )
    cand, norm = call(
        load_kernel, "load", [bf16(rows, width), line], (candidates,),
        specs=[pl.BlockSpec(memory_space=pltpu.HBM)], after=parts[:1],
        scratch=[pltpu.SemaphoreType.DMA((rows // TILE * 2,))], limit=42 * MIB,
    )
    got = [flip_permute(parts[d], size, 2 * d) for d in range(1, chips)]
    owned, picked = call(
        sum_kernel, "owned", [bf16(rows_chip, half), bf16(picks_chip, half)], (parts[0], *got),
        after=(norm,),
    )

    shifted = [
        lax.ppermute(picked, "grp", [(g, (g + k) % groups) for g in range(groups)])
        for k in range(1, groups)
    ]

    if chips == 4:
        quarter = half // 2
        own_x, own_y = (flip_permute(owned, size, flip) for flip in (2, 4))
        wait = (own_x, own_y)
        low = stack(*[[(b, 0, quarter)] for b in shifted], after=wait)
        high = stack(*[[(b, quarter, quarter)] for b in shifted], after=wait)
        low_x, high_y = flip_permute(low, size, 2), flip_permute(high, size, 4)
        high_x, low_y = flip_permute(high, size, 2), flip_permute(low, size, 4)
        first, chips_first = stack([owned], [own_x], [own_y], [low, high]), chips - 1
        others = ([low_x, high_x], [low_y, high_y])
    else:
        far = to_chips(stack(*[[b] for b in shifted]), size)
        *own_blocks, own_end = to_chips(owned, size)
        first, chips_first = stack(*[[b] for b in own_blocks], [far[0]]), chips - 1
        others = [[b] for b in far[1:-1]]

    near, best = call(
        functools.partial(first_kernel, (picks_chip, rows_chip, chips_first * rows_chip)),
        "products", [line] * 2, (cand, first, flip_permute(first, size, 1)),
        scratch=[pltpu.VMEM((first.shape[0], width), BF16)], weight=WEIGHT // 10,
    )
    if chips == 4:
        left = stack([(own_x, 0, quarter)], [low_x], after=(best,))
        right = stack([(own_y, quarter, quarter)], [high_y], after=(best,))
        corner = (flip_permute(left, size, 4), flip_permute(right, size, 2))
    else:
        corner = (stack([own_end], [far[-1]]),)
    operands = []
    for block in others:
        operands += [*block, *[flip_permute(stack([b], after=(best,)), size, 1) for b in block]]
    best = call(
        functools.partial(next_kernel, len(others)), "products_next", line, (cand, best, *operands),
        scratch=[pltpu.VMEM((len(others) * others[0][0].shape[0], width), BF16)], weight=0,
    )
    sent = [stack([part], after=(best,)) for part in corner]
    swapped = [flip_permute(part, size, 1) for part in sent]
    rows_end = corner[0].shape[0]
    scratch = [pltpu.VMEM((rows_end, half), BF16)]
    part = call(
        half_kernel, "products_half", jax.ShapeDtypeStruct((rows_end, rows), F32), (cand, *corner),
        scratch=scratch, after=(best,),
    )
    near, final = call(
        functools.partial(last_kernel, (picks_chip, rows_chip, rows_chip)), "products_last",
        [line] * 2, (cand, norm, near, best, part, *swapped), scratch=scratch,
    )
    return near.reshape(-1), final.reshape(-1)


def solution(mesh):
    in_specs = (P(("grp", "mem"), None), P(("grp", "mem"), None), P("grp", "mem"), P("grp", None))
    out_specs = (P(("grp", "mem")), P(("grp", "mem")))
    return jax.shard_map(body, mesh=mesh, in_specs=in_specs, out_specs=out_specs, check_vma=False)
```

```python
import functools

import jax
import jax.numpy as jnp
from jax import lax
from jax.experimental import pallas as pl
from jax.experimental.pallas import tpu as pltpu
from jax.sharding import PartitionSpec as P

TILE = 256
MIB = 1024 * 1024
WEIGHT = 10**10
F32, BF16 = jnp.float32, jnp.bfloat16


def flip_permute(block, size, flip):
    return lax.ppermute(block, "mem", [(m, m ^ flip) for m in range(size)])


def to_chips(block, size):
    return [block] + [flip_permute(block, size, 2 * d) for d in range(1, size // 2)]


def vmem_specs(count):
    return [pl.BlockSpec(memory_space=pltpu.VMEM)] * count


def call(kernel, name, out_shape, operands, specs=None, scratch=(), after=(), limit=28 * MIB, weight=WEIGHT):
    shapes = jax.tree.leaves(out_shape)
    moved = sum(a.size * a.dtype.itemsize for a in list(operands) + shapes)
    count = len(operands)

    def run(*refs):
        kernel(*refs[:count], *refs[count + len(after) :])

    return pl.pallas_call(
        run,
        out_shape=out_shape,
        in_specs=(specs or vmem_specs(count)) + [pl.BlockSpec(memory_space=pl.ANY)] * len(after),
        out_specs=jax.tree.map(lambda _: pl.BlockSpec(memory_space=pltpu.VMEM), out_shape),
        scratch_shapes=scratch,
        compiler_params=pltpu.CompilerParams(vmem_limit_bytes=limit),
        cost_estimate=pl.CostEstimate(flops=weight, bytes_accessed=moved, transcendentals=0),
        name=name,
    )(*operands, *after)


def spread_kernel(count_ref, out):
    out[...] = jnp.broadcast_to(count_ref[0, 0], out.shape)


def pair_kernel(own, sib, out):
    lane = lax.broadcasted_iota(jnp.int32, out.shape, 1)
    out[...] = jnp.where(lane == 0, own[...], sib[...])


def split_kernel(rows_ref, keep_ref, send_ref):
    half = keep_ref.shape[1]
    core = lax.rem(lax.axis_index("mem"), 2)
    keep_ref[...] = rows_ref[:, pl.ds(pl.multiple_of(core * half, half), half)]
    send_ref[...] = rows_ref[:, pl.ds(pl.multiple_of((1 - core) * half, half), half)]


def load_kernel(cand_hbm, cand_ref, norm_ref, sems):
    half = cand_ref.shape[1] // 2
    core = lax.rem(lax.axis_index("mem"), 2)
    tiles, copies = cand_ref.shape[0] // TILE, []
    for t in range(tiles):
        at = pl.ds(t * TILE, TILE)
        for k, own in enumerate((core, 1 - core)):
            copies.append(
                pltpu.make_async_copy(
                    cand_hbm.at[at, pl.ds(pl.multiple_of(own * half, half), half)],
                    cand_ref.at[at, pl.ds(k * half, half)],
                    sems.at[len(copies)],
                )
            )
    for copy in copies:
        copy.start()
    for t in range(tiles):
        for copy in copies[2 * t : 2 * t + 2]:
            copy.wait()
        squares = jnp.zeros((TILE, 128), F32)
        for k in range(0, cand_ref.shape[1], 128):
            entries = cand_ref[t * TILE : (t + 1) * TILE, k : k + 128].astype(F32)
            squares += entries * entries
        norm_ref[:, t * TILE : (t + 1) * TILE] = jnp.sum(squares.T, axis=0, keepdims=True)


def stack_kernel(layout, *refs):
    out, top = refs[-1], 0
    for parts in layout:
        left, rows = 0, refs[parts[0][0]].shape[0]
        for index, start, columns in parts:
            out[top : top + rows, left : left + columns] = refs[index][:, start : start + columns]
            left += columns
        top += rows


def copy_kernel(block, out):
    rows = min(block.shape[0], out.shape[0])
    out[:rows, :] = block[:rows, :]
    if out.shape[0] > rows:
        out[rows:, :] = block[: out.shape[0] - rows, :]


def dense_kernel(size, picks_chip, rest_chip, chosen_ref, *refs):
    chips = size // 2
    counts, (own, sib, *outs, select_ref) = refs[:chips], refs[chips:]
    slots, picks = own.shape[0], chosen_ref.shape[1]
    rows_chip = picks_chip + rest_chip
    me = lax.axis_index("mem")
    offsets = [jnp.zeros((1, 1), jnp.int32) for _ in range(2)]
    for d, ref in enumerate(counts):
        for h in range(2):
            origin = lax.bitwise_xor(me, 2 * d + h)
            for k in range(2):
                before = (origin < lax.bitwise_xor(me, k)).astype(jnp.int32)
                offsets[k] += ref[:1, h : h + 1] * before
    lane = lax.broadcasted_iota(jnp.int32, (1, 2 * slots), 1)
    first = lane < slots
    within = jnp.where(first, lane, lane - slots)
    alive = within < jnp.where(first, counts[0][:1, :1], counts[0][:1, 1:2])
    position = jnp.where(alive, within + jnp.where(first, offsets[0], offsets[1]), -1)

    chosen = chosen_ref[...]

    def column(start, length):
        row = lax.broadcasted_iota(jnp.int32, (length, picks), 0)
        across = lax.broadcasted_iota(jnp.int32, (length, picks), 1)
        return jnp.sum(jnp.where(across == row + start, chosen, 0), axis=1, keepdims=True)

    ids = column(0, picks)
    below = jnp.sum((ids < position).astype(jnp.int32), axis=0, keepdims=True)
    taken = jnp.sum((ids == position).astype(jnp.int32), axis=0, keepdims=True)
    rank = jnp.where(alive & (taken == 0), position - below, -1)
    place = lax.broadcasted_iota(jnp.int32, (rest_chip, 1), 0)
    for d in range(chips):
        owner = lax.bitwise_xor(me // 2, d)
        top = d * rows_chip
        hit = column(owner * picks_chip, picks_chip) == position
        select_ref[top : top + picks_chip, :] = hit.astype(F32).astype(BF16)
        hit = place + owner * rest_chip == rank
        select_ref[top + picks_chip : top + rows_chip, :] = hit.astype(F32).astype(BF16)

    for t in range(0, own.shape[1], TILE):
        at = slice(t, t + TILE)
        rows = jnp.concatenate([own[:, at], sib[:, at]], axis=0)
        found = jnp.dot(select_ref[...], rows, preferred_element_type=F32).astype(BF16)
        for d, out in enumerate(outs):
            out[:, at] = found[d * rows_chip : (d + 1) * rows_chip]


def sum_kernel(*refs):
    *parts, out, picks_ref = refs
    total = parts[0][...]
    for ref in parts[1:]:
        total += ref[...]
    out[...] = total
    picks_ref[...] = total[: picks_ref.shape[0], :]


def row_norms(rows):
    rows = rows.astype(F32)
    return jnp.sum(rows * rows, axis=1, keepdims=True)


def gaps_to(rows_ref, norms, cand):
    inner = lax.dot_general(
        rows_ref[...], cand, (((1,), (1,)), ((), ())), preferred_element_type=F32
    )
    return norms - 2.0 * inner


def tiles_of(cand_ref):
    return [slice(t, t + TILE) for t in range(0, cand_ref.shape[0], TILE)]


def lay_out(parts, rows_ref):
    left = 0
    for part in parts:
        rows_ref[:, left : left + part.shape[1]] = part[: rows_ref.shape[0], :]
        left += part.shape[1]
    return row_norms(rows_ref[...])


def row_masks(picks_chip, rows_chip, own_rows, rows):
    row = lax.broadcasted_iota(jnp.int32, (rows, 1), 0)
    own = row < own_rows
    pick = (lax.rem(row, rows_chip) < picks_chip) | ~own
    return jnp.where(own, 0.0, jnp.inf), jnp.where(pick, 0.0, jnp.inf)


def least(gaps):
    return jnp.min(gaps, axis=0, keepdims=True)


def first_kernel(chip_rows, cand_ref, norm_ref, own, sib, near_ref, best_ref, rows_ref):
    norms = lay_out((own, sib), rows_ref)
    no_row, no_pick = row_masks(*chip_rows, norms.shape[0])
    for at in tiles_of(cand_ref):
        gaps = gaps_to(rows_ref, norms, cand_ref[at, :])
        near_ref[:, at] = least(gaps + no_row) + norm_ref[:, at]
        best_ref[:, at] = least(gaps + no_pick)


def next_kernel(blocks, cand_ref, best_ref, *refs):
    *parts, out, rows_ref = refs
    norms, count, rows = [], len(parts) // blocks, rows_ref.shape[0] // blocks
    for b in range(blocks):
        block = rows_ref.at[b * rows : (b + 1) * rows, :]
        norms.append(lay_out(parts[b * count : (b + 1) * count], block))
    norms = jnp.concatenate(norms, axis=0)
    for at in tiles_of(cand_ref):
        gaps = gaps_to(rows_ref, norms, cand_ref[at, :])
        out[:, at] = jnp.minimum(least(gaps), best_ref[:, at])


def half_kernel(cand_ref, *refs):
    *corner, out, rows_ref = refs
    norms = lay_out(corner, rows_ref)
    for at in tiles_of(cand_ref):
        out[:, at] = gaps_to(rows_ref, norms, cand_ref[at, : rows_ref.shape[1]])


def last_kernel(cand_ref, norm_ref, best_ref, part_ref, *refs):
    *corner, out, rows_ref = refs
    norms = lay_out(corner, rows_ref)
    for at in tiles_of(cand_ref):
        gaps = part_ref[:, at] + gaps_to(rows_ref, norms, cand_ref[at, rows_ref.shape[1] :])
        out[:, at] = jnp.minimum(least(gaps), best_ref[:, at]) + norm_ref[:, at]


def body(candidates, round_one, counts, chosen):
    size, groups = lax.axis_size("mem"), lax.axis_size("grp")
    slots, width = round_one.shape
    half, chips = width // 2, size // 2
    picks, rows = chosen.shape[1], candidates.shape[0]
    picks_chip = picks // chips
    rest_chip = (size * slots * 3 // 8 - picks) // chips
    rows_chip = picks_chip + rest_chip
    live = chips * rows_chip

    def bf16(*dims):
        return jax.ShapeDtypeStruct(dims, BF16)

    def stack(*blocks, after=()):
        operands, layout = [], []
        for block in blocks:
            parts = [p if isinstance(p, tuple) else (p, 0, p.shape[1]) for p in block]
            layout.append([(len(operands) + i, *p[1:]) for i, p in enumerate(parts)])
            operands += [p[0] for p in parts]
        shape = bf16(
            sum(operands[parts[0][0]].shape[0] for parts in layout), sum(p[2] for p in layout[0])
        )
        return call(
            functools.partial(stack_kernel, layout), "stack", shape, operands, after=after, weight=0
        )

    def copy(block, count, after):
        shape = bf16(count, block.shape[1])
        return call(copy_kernel, "copy", shape, (block,), after=after, weight=0)

    line = jax.ShapeDtypeStruct((1, rows), F32)
    tile = jax.ShapeDtypeStruct((8, 128), jnp.int32)
    count = call(
        spread_kernel, "spread", tile, (counts,), specs=[pl.BlockSpec(memory_space=pltpu.SMEM)]
    )
    pair = call(pair_kernel, "pair", tile, (count, flip_permute(count, size, 1)))
    pairs = to_chips(pair, size)
    own, send = call(split_kernel, "split", [bf16(slots, half)] * 2, (round_one,))
    sib = flip_permute(send, size, 1)

    parts = call(
        functools.partial(dense_kernel, size, picks_chip, rest_chip), "dense",
        [bf16(rows_chip, half)] * chips, (chosen, *pairs, own, sib),
        scratch=[pltpu.VMEM((live, 2 * slots), BF16)],
    )
    cand, norm = call(
        load_kernel, "load", [bf16(rows, width), line], (candidates,),
        specs=[pl.BlockSpec(memory_space=pltpu.HBM)], after=parts[:1],
        scratch=[pltpu.SemaphoreType.DMA((rows // TILE * 2,))], limit=42 * MIB,
    )
    got = [flip_permute(parts[d], size, 2 * d) for d in range(1, chips)]
    owned, picked = call(
        sum_kernel, "owned", [bf16(rows_chip, half), bf16(picks_chip, half)], (parts[0], *got),
        after=(norm,),
    )

    shifted = [
        lax.ppermute(picked, "grp", [(g, (g + k) % groups) for g in range(groups)])
        for k in range(1, groups)
    ]

    if chips == 4:
        quarter = half // 2
        own_x, own_y = (flip_permute(owned, size, flip) for flip in (2, 4))
        own_left = flip_permute(stack([(own_x, 0, quarter)]), size, 4)
        own_right = flip_permute(stack([(own_y, quarter, quarter)]), size, 2)
        wait = (own_left, own_right)
        low = stack(*[[(b, 0, quarter)] for b in shifted], after=wait)
        high = stack(*[[(b, quarter, quarter)] for b in shifted], after=wait)
        low_x, high_y = flip_permute(low, size, 2), flip_permute(high, size, 4)
        high_x, low_y = flip_permute(high, size, 2), flip_permute(low, size, 4)
        first = stack([owned], [own_x], [own_y], [own_left, own_right], [low, high])
        others = ([low_x, high_x], [low_y, high_y])
    else:
        far = to_chips(stack(*[[b] for b in shifted]), size)
        first = stack(*[[b] for b in to_chips(owned, size)], [far[0]])
        others = [[b] for b in far[1:-1]]

    near, best = call(
        functools.partial(first_kernel, (picks_chip, rows_chip, live)),
        "products", [line] * 2, (cand, norm, first, flip_permute(first, size, 1)),
        scratch=[pltpu.VMEM((first.shape[0], width), BF16)], weight=WEIGHT // 10,
    )
    rows_end = (groups - 1) * picks_chip
    if chips == 4:
        left = copy(low_x, rows_end + 16, (best,))
        right = copy(high_y, rows_end + 16, (best,))
        corner = (flip_permute(left, size, 4), flip_permute(right, size, 2))
    else:
        corner = (far[-1],)
    operands, handed = [], (left, right) if chips == 4 else ()
    for block in others:
        operands += block
        for b in block:
            after = (best, *handed) if chips == 4 and b is not low_x else (best,)
            operands.append(flip_permute(stack([b], after=after), size, 1))
    best = call(
        functools.partial(next_kernel, len(others)), "products_next", line, (cand, best, *operands),
        scratch=[pltpu.VMEM((len(others) * others[0][0].shape[0], width), BF16)], weight=0,
    )
    sent = [copy(part, rows_end, (best,)) for part in corner]
    swapped = [flip_permute(part, size, 1) for part in sent]
    scratch = [pltpu.VMEM((rows_end, half), BF16)]
    part = call(
        half_kernel, "products_half", jax.ShapeDtypeStruct((rows_end, rows), F32), (cand, *corner),
        scratch=scratch, after=(best,),
    )
    final = call(
        last_kernel, "products_last", line, (cand, norm, best, part, *swapped), scratch=scratch
    )
    return near.reshape(-1), final.reshape(-1)


def solution(mesh):
    in_specs = (P(("grp", "mem"), None), P(("grp", "mem"), None), P("grp", "mem"), P("grp", None))
    out_specs = (P(("grp", "mem")), P(("grp", "mem")))
    return jax.shard_map(body, mesh=mesh, in_specs=in_specs, out_specs=out_specs, check_vma=False)
```

```python
import functools

import jax
import jax.numpy as jnp
from jax import lax
from jax.experimental import pallas as pl
from jax.experimental.pallas import tpu as pltpu
from jax.sharding import PartitionSpec as P

TILE = 256
MIB = 1024 * 1024
WEIGHT = 10**10
F32, BF16 = jnp.float32, jnp.bfloat16


def flip_permute(block, size, flip):
    return lax.ppermute(block, "mem", [(m, m ^ flip) for m in range(size)])


def to_chips(block, size):
    return [block] + [flip_permute(block, size, 2 * d) for d in range(1, size // 2)]


def vmem_specs(count):
    return [pl.BlockSpec(memory_space=pltpu.VMEM)] * count


def call(kernel, name, out_shape, operands, specs=None, scratch=(), after=(), limit=28 * MIB, weight=WEIGHT):
    shapes = jax.tree.leaves(out_shape)
    moved = sum(a.size * a.dtype.itemsize for a in list(operands) + shapes)
    count = len(operands)

    def run(*refs):
        kernel(*refs[:count], *refs[count + len(after) :])

    return pl.pallas_call(
        run,
        out_shape=out_shape,
        in_specs=(specs or vmem_specs(count)) + [pl.BlockSpec(memory_space=pl.ANY)] * len(after),
        out_specs=jax.tree.map(lambda _: pl.BlockSpec(memory_space=pltpu.VMEM), out_shape),
        scratch_shapes=scratch,
        compiler_params=pltpu.CompilerParams(vmem_limit_bytes=limit),
        cost_estimate=pl.CostEstimate(flops=weight, bytes_accessed=moved, transcendentals=0),
        name=name,
    )(*operands, *after)


def spread_kernel(count_ref, out):
    out[...] = jnp.broadcast_to(count_ref[0, 0], out.shape)


def pair_kernel(own, sib, out):
    lane = lax.broadcasted_iota(jnp.int32, out.shape, 1)
    out[...] = jnp.where(lane == 0, own[...], sib[...])


def split_kernel(rows_ref, keep_ref, send_ref):
    half = keep_ref.shape[1]
    core = lax.rem(lax.axis_index("mem"), 2)
    keep_ref[...] = rows_ref[:, pl.ds(pl.multiple_of(core * half, half), half)]
    send_ref[...] = rows_ref[:, pl.ds(pl.multiple_of((1 - core) * half, half), half)]


def load_kernel(cand_hbm, cand_ref, norm_ref, sems):
    half = cand_ref.shape[1] // 2
    core = lax.rem(lax.axis_index("mem"), 2)
    tiles, copies = cand_ref.shape[0] // TILE, []
    for t in range(tiles):
        at = pl.ds(t * TILE, TILE)
        for k, own in enumerate((core, 1 - core)):
            copies.append(
                pltpu.make_async_copy(
                    cand_hbm.at[at, pl.ds(pl.multiple_of(own * half, half), half)],
                    cand_ref.at[at, pl.ds(k * half, half)],
                    sems.at[len(copies)],
                )
            )
    for copy in copies:
        copy.start()
    for t in range(tiles):
        for copy in copies[2 * t : 2 * t + 2]:
            copy.wait()
        squares = jnp.zeros((TILE, 128), F32)
        for k in range(0, cand_ref.shape[1], 128):
            entries = cand_ref[t * TILE : (t + 1) * TILE, k : k + 128].astype(F32)
            squares += entries * entries
        norm_ref[:, t * TILE : (t + 1) * TILE] = jnp.sum(squares.T, axis=0, keepdims=True)


def stack_kernel(layout, *refs):
    out, top = refs[-1], 0
    for parts in layout:
        left, rows = 0, refs[parts[0][0]].shape[0]
        for index, start, columns in parts:
            out[top : top + rows, left : left + columns] = refs[index][:, start : start + columns]
            left += columns
        top += rows


def copy_kernel(block, out):
    rows = min(block.shape[0], out.shape[0])
    out[:rows, :] = block[:rows, :]
    if out.shape[0] > rows:
        out[rows:, :] = block[: out.shape[0] - rows, :]


def dense_kernel(size, picks_chip, rest_chip, chosen_ref, *refs):
    chips = size // 2
    counts, (own, sib, *outs, select_ref) = refs[:chips], refs[chips:]
    slots, picks = own.shape[0], chosen_ref.shape[1]
    rows_chip = picks_chip + rest_chip
    me = lax.axis_index("mem")
    offsets = [jnp.zeros((1, 1), jnp.int32) for _ in range(2)]
    for d, ref in enumerate(counts):
        for h in range(2):
            origin = lax.bitwise_xor(me, 2 * d + h)
            for k in range(2):
                before = (origin < lax.bitwise_xor(me, k)).astype(jnp.int32)
                offsets[k] += ref[:1, h : h + 1] * before
    lane = lax.broadcasted_iota(jnp.int32, (1, 2 * slots), 1)
    first = lane < slots
    within = jnp.where(first, lane, lane - slots)
    alive = within < jnp.where(first, counts[0][:1, :1], counts[0][:1, 1:2])
    position = jnp.where(alive, within + jnp.where(first, offsets[0], offsets[1]), -1)

    chosen = chosen_ref[...]

    def column(start, length):
        row = lax.broadcasted_iota(jnp.int32, (length, picks), 0)
        across = lax.broadcasted_iota(jnp.int32, (length, picks), 1)
        return jnp.sum(jnp.where(across == row + start, chosen, 0), axis=1, keepdims=True)

    ids = column(0, picks)
    below = jnp.sum((ids < position).astype(jnp.int32), axis=0, keepdims=True)
    taken = jnp.sum((ids == position).astype(jnp.int32), axis=0, keepdims=True)
    rank = jnp.where(alive & (taken == 0), position - below, -1)
    place = lax.broadcasted_iota(jnp.int32, (rest_chip, 1), 0)
    for d in range(chips):
        owner = lax.bitwise_xor(me // 2, d)
        top = d * rows_chip
        hit = column(owner * picks_chip, picks_chip) == position
        select_ref[top : top + picks_chip, :] = hit.astype(F32).astype(BF16)
        hit = place + owner * rest_chip == rank
        select_ref[top + picks_chip : top + rows_chip, :] = hit.astype(F32).astype(BF16)

    for t in range(0, own.shape[1], TILE):
        at = slice(t, t + TILE)
        rows = jnp.concatenate([own[:, at], sib[:, at]], axis=0)
        found = jnp.dot(select_ref[...], rows, preferred_element_type=F32).astype(BF16)
        for d, out in enumerate(outs):
            out[:, at] = found[d * rows_chip : (d + 1) * rows_chip]


def sum_kernel(*refs):
    *parts, out, picks_ref = refs
    total = parts[0][...]
    for ref in parts[1:]:
        total += ref[...]
    out[...] = total
    picks_ref[...] = total[: picks_ref.shape[0], :]


def row_norms(rows):
    rows = rows.astype(F32)
    return jnp.sum(rows * rows, axis=1, keepdims=True)


def gaps_to(rows_ref, norms, cand):
    inner = lax.dot_general(
        rows_ref[...], cand, (((1,), (1,)), ((), ())), preferred_element_type=F32
    )
    return norms - 2.0 * inner


def tiles_of(cand_ref):
    return [slice(t, t + TILE) for t in range(0, cand_ref.shape[0], TILE)]


def lay_out(parts, rows_ref):
    left = 0
    for part in parts:
        rows_ref[:, left : left + part.shape[1]] = part[: rows_ref.shape[0], :]
        left += part.shape[1]
    return row_norms(rows_ref[...])


def row_masks(picks_chip, rows_chip, own_rows, rows):
    row = lax.broadcasted_iota(jnp.int32, (rows, 1), 0)
    own = row < own_rows
    pick = (lax.rem(row, rows_chip) < picks_chip) | ~own
    return jnp.where(own, 0.0, jnp.inf), jnp.where(pick, 0.0, jnp.inf)


def least(gaps):
    return jnp.min(gaps, axis=0, keepdims=True)


def first_kernel(chip_rows, cand_ref, norm_ref, own, sib, near_ref, best_ref, rows_ref):
    norms = lay_out((own, sib), rows_ref)
    no_row, no_pick = row_masks(*chip_rows, norms.shape[0])
    for at in tiles_of(cand_ref):
        gaps = gaps_to(rows_ref, norms, cand_ref[at, :])
        near_ref[:, at] = least(gaps + no_row) + norm_ref[:, at]
        best_ref[:, at] = least(gaps + no_pick)


def next_kernel(blocks, count, cand_ref, best_ref, *refs):
    *parts, out, part_ref, own_ref, sib_ref = refs
    rows, half = sib_ref.shape
    each = rows // blocks
    own_norms, sib_norms = [], []
    for b in range(blocks):
        at = slice(b * each, (b + 1) * each)
        own_norms.append(lay_out(parts[:count], own_ref.at[at, :]))
        sib_norms.append(lay_out(parts[count : 2 * count], sib_ref.at[at, :]))
        parts = parts[2 * count :]
    own_norms.append(lay_out(parts, own_ref.at[rows:, :]))
    own_norms = jnp.concatenate(own_norms, axis=0)
    sib_norms = jnp.concatenate(sib_norms, axis=0)
    for at in tiles_of(cand_ref):
        gaps = gaps_to(own_ref, own_norms, cand_ref[at, :half])
        part_ref[:, at] = gaps[rows:]
        gaps = gaps[:rows] + gaps_to(sib_ref, sib_norms, cand_ref[at, half:])
        out[:, at] = jnp.minimum(least(gaps), best_ref[:, at])


def last_kernel(cand_ref, norm_ref, best_ref, part_ref, *refs):
    *corner, out, rows_ref = refs
    norms = lay_out(corner, rows_ref)
    for at in tiles_of(cand_ref):
        gaps = part_ref[:, at] + gaps_to(rows_ref, norms, cand_ref[at, rows_ref.shape[1] :])
        out[:, at] = jnp.minimum(least(gaps), best_ref[:, at]) + norm_ref[:, at]


def body(candidates, round_one, counts, chosen):
    size, groups = lax.axis_size("mem"), lax.axis_size("grp")
    slots, width = round_one.shape
    half, chips = width // 2, size // 2
    picks, rows = chosen.shape[1], candidates.shape[0]
    picks_chip = picks // chips
    rest_chip = (size * slots * 3 // 8 - picks) // chips
    rows_chip = picks_chip + rest_chip
    live = chips * rows_chip

    def bf16(*dims):
        return jax.ShapeDtypeStruct(dims, BF16)

    def stack(*blocks, after=()):
        operands, layout = [], []
        for block in blocks:
            parts = [p if isinstance(p, tuple) else (p, 0, p.shape[1]) for p in block]
            layout.append([(len(operands) + i, *p[1:]) for i, p in enumerate(parts)])
            operands += [p[0] for p in parts]
        shape = bf16(
            sum(operands[parts[0][0]].shape[0] for parts in layout), sum(p[2] for p in layout[0])
        )
        return call(
            functools.partial(stack_kernel, layout), "stack", shape, operands, after=after, weight=0
        )

    def copy(block, count, after):
        shape = bf16(count, block.shape[1])
        return call(copy_kernel, "copy", shape, (block,), after=after, weight=0)

    line = jax.ShapeDtypeStruct((1, rows), F32)
    tile = jax.ShapeDtypeStruct((8, 128), jnp.int32)
    count = call(
        spread_kernel, "spread", tile, (counts,), specs=[pl.BlockSpec(memory_space=pltpu.SMEM)]
    )
    pair = call(pair_kernel, "pair", tile, (count, flip_permute(count, size, 1)))
    pairs = to_chips(pair, size)
    own, send = call(split_kernel, "split", [bf16(slots, half)] * 2, (round_one,))
    sib = flip_permute(send, size, 1)

    parts = call(
        functools.partial(dense_kernel, size, picks_chip, rest_chip), "dense",
        [bf16(rows_chip, half)] * chips, (chosen, *pairs, own, sib),
        scratch=[pltpu.VMEM((live, 2 * slots), BF16)],
    )
    cand, norm = call(
        load_kernel, "load", [bf16(rows, width), line], (candidates,),
        specs=[pl.BlockSpec(memory_space=pltpu.HBM)], after=parts[:1],
        scratch=[pltpu.SemaphoreType.DMA((rows // TILE * 2,))], limit=42 * MIB,
    )
    got = [flip_permute(parts[d], size, 2 * d) for d in range(1, chips)]
    owned, picked = call(
        sum_kernel, "owned", [bf16(rows_chip, half), bf16(picks_chip, half)], (parts[0], *got),
        after=(norm,),
    )

    shifted = [
        lax.ppermute(picked, "grp", [(g, (g + k) % groups) for g in range(groups)])
        for k in range(1, groups)
    ]

    if chips == 4:
        quarter = half // 2
        own_x, own_y = (flip_permute(owned, size, flip) for flip in (2, 4))
        own_left = flip_permute(stack([(own_x, 0, quarter)]), size, 4)
        own_right = flip_permute(stack([(own_y, quarter, quarter)]), size, 2)
        wait = (own_left, own_right)
        low = stack(*[[(b, 0, quarter)] for b in shifted], after=wait)
        high = stack(*[[(b, quarter, quarter)] for b in shifted], after=wait)
        low_x, high_y = flip_permute(low, size, 2), flip_permute(high, size, 4)
        high_x, low_y = flip_permute(high, size, 2), flip_permute(low, size, 4)
        first = stack([owned], [own_x], [own_y], [own_left, own_right], [low, high])
        others = ([low_x, high_x], [low_y, high_y])
    else:
        far = to_chips(stack(*[[b] for b in shifted]), size)
        first = stack(*[[b] for b in to_chips(owned, size)], [far[0]])
        others = [[b] for b in far[1:-1]]

    near, best = call(
        functools.partial(first_kernel, (picks_chip, rows_chip, live)),
        "products", [line] * 2, (cand, norm, first, flip_permute(first, size, 1)),
        scratch=[pltpu.VMEM((first.shape[0], width), BF16)], weight=WEIGHT // 10,
    )
    rows_end = (groups - 1) * picks_chip
    if chips == 4:
        left = copy(low_x, rows_end + 16, (best,))
        right = copy(high_y, rows_end + 16, (best,))
        corner = (flip_permute(left, size, 4), flip_permute(right, size, 2))
    else:
        corner = (far[-1],)
    operands, handed = [], (left, right) if chips == 4 else ()
    for block in others:
        operands += block
        for b in block:
            after = (best, *handed) if chips == 4 and b is not low_x else (best,)
            operands.append(flip_permute(stack([b], after=after), size, 1))
    swapped = [flip_permute(copy(part, rows_end, (operands[-1],)), size, 1) for part in corner]
    rows_next = len(others) * rows_end
    best, part = call(
        functools.partial(next_kernel, len(others), len(others[0])), "products_next",
        [line, jax.ShapeDtypeStruct((rows_end, rows), F32)], (cand, best, *operands, *corner),
        scratch=[
            pltpu.VMEM((rows_next + rows_end, half), BF16), pltpu.VMEM((rows_next, half), BF16)
        ],
        weight=WEIGHT // 3,
    )
    scratch = [pltpu.VMEM((rows_end, half), BF16)]
    final = call(
        last_kernel, "products_last", line, (cand, norm, best, part, *swapped), scratch=scratch
    )
    return near.reshape(-1), final.reshape(-1)


def solution(mesh):
    in_specs = (P(("grp", "mem"), None), P(("grp", "mem"), None), P("grp", "mem"), P("grp", None))
    out_specs = (P(("grp", "mem")), P(("grp", "mem")))
    return jax.shard_map(body, mesh=mesh, in_specs=in_specs, out_specs=out_specs, check_vma=False)
```

```python
import functools

import jax
import jax.numpy as jnp
from jax import lax
from jax.experimental import pallas as pl
from jax.experimental.pallas import tpu as pltpu
from jax.sharding import PartitionSpec as P

TILE = 256
MIB = 1024 * 1024
WEIGHT = 10**10
F32, BF16 = jnp.float32, jnp.bfloat16


def flip_permute(block, size, flip):
    return lax.ppermute(block, "mem", [(m, m ^ flip) for m in range(size)])


def to_chips(block, size):
    return [block] + [flip_permute(block, size, 2 * d) for d in range(1, size // 2)]


def vmem_specs(count):
    return [pl.BlockSpec(memory_space=pltpu.VMEM)] * count


def call(kernel, name, out_shape, operands, specs=None, scratch=(), after=(), limit=28 * MIB, weight=WEIGHT):
    shapes = jax.tree.leaves(out_shape)
    moved = sum(a.size * a.dtype.itemsize for a in list(operands) + shapes)
    count = len(operands)

    def run(*refs):
        kernel(*refs[:count], *refs[count + len(after) :])

    return pl.pallas_call(
        run,
        out_shape=out_shape,
        in_specs=(specs or vmem_specs(count)) + [pl.BlockSpec(memory_space=pl.ANY)] * len(after),
        out_specs=jax.tree.map(lambda _: pl.BlockSpec(memory_space=pltpu.VMEM), out_shape),
        scratch_shapes=scratch,
        compiler_params=pltpu.CompilerParams(vmem_limit_bytes=limit),
        cost_estimate=pl.CostEstimate(flops=weight, bytes_accessed=moved, transcendentals=0),
        name=name,
    )(*operands, *after)


def spread_kernel(count_ref, out):
    out[...] = jnp.broadcast_to(count_ref[0, 0], out.shape)


def pair_kernel(own, sib, out):
    lane = lax.broadcasted_iota(jnp.int32, out.shape, 1)
    out[...] = jnp.where(lane == 0, own[...], sib[...])


def split_kernel(rows_ref, keep_ref, send_ref):
    half = keep_ref.shape[1]
    core = lax.rem(lax.axis_index("mem"), 2)
    keep_ref[...] = rows_ref[:, pl.ds(pl.multiple_of(core * half, half), half)]
    send_ref[...] = rows_ref[:, pl.ds(pl.multiple_of((1 - core) * half, half), half)]


def load_kernel(cand_hbm, cand_ref, norm_ref, sems):
    half = cand_ref.shape[1] // 2
    core = lax.rem(lax.axis_index("mem"), 2)
    tiles, copies = cand_ref.shape[0] // TILE, []
    for t in range(tiles):
        at = pl.ds(t * TILE, TILE)
        for k, own in enumerate((core, 1 - core)):
            copies.append(
                pltpu.make_async_copy(
                    cand_hbm.at[at, pl.ds(pl.multiple_of(own * half, half), half)],
                    cand_ref.at[at, pl.ds(k * half, half)],
                    sems.at[len(copies)],
                )
            )
    for copy in copies:
        copy.start()
    for t in range(tiles):
        for copy in copies[2 * t : 2 * t + 2]:
            copy.wait()
        squares = jnp.zeros((TILE, 128), F32)
        for k in range(0, cand_ref.shape[1], 128):
            entries = cand_ref[t * TILE : (t + 1) * TILE, k : k + 128].astype(F32)
            squares += entries * entries
        norm_ref[:, t * TILE : (t + 1) * TILE] = jnp.sum(squares.T, axis=0, keepdims=True)


def stack_kernel(layout, *refs):
    out, top = refs[-1], 0
    for parts in layout:
        left, rows = 0, refs[parts[0][0]].shape[0]
        for index, start, columns in parts:
            out[top : top + rows, left : left + columns] = refs[index][:, start : start + columns]
            left += columns
        top += rows


def copy_kernel(block, out):
    rows = min(block.shape[0], out.shape[0])
    out[:rows, :] = block[:rows, :]
    if out.shape[0] > rows:
        out[rows:, :] = block[: out.shape[0] - rows, :]


def dense_kernel(size, picks_chip, rest_chip, chosen_ref, *refs):
    chips = size // 2
    counts, (own, sib, *outs, select_ref) = refs[:chips], refs[chips:]
    slots, picks = own.shape[0], chosen_ref.shape[1]
    rows_chip = picks_chip + rest_chip
    me = lax.axis_index("mem")
    offsets = [jnp.zeros((1, 1), jnp.int32) for _ in range(2)]
    for d, ref in enumerate(counts):
        for h in range(2):
            origin = lax.bitwise_xor(me, 2 * d + h)
            for k in range(2):
                before = (origin < lax.bitwise_xor(me, k)).astype(jnp.int32)
                offsets[k] += ref[:1, h : h + 1] * before
    lane = lax.broadcasted_iota(jnp.int32, (1, 2 * slots), 1)
    first = lane < slots
    within = jnp.where(first, lane, lane - slots)
    alive = within < jnp.where(first, counts[0][:1, :1], counts[0][:1, 1:2])
    position = jnp.where(alive, within + jnp.where(first, offsets[0], offsets[1]), -1)

    chosen = chosen_ref[...]

    def column(start, length):
        row = lax.broadcasted_iota(jnp.int32, (length, picks), 0)
        across = lax.broadcasted_iota(jnp.int32, (length, picks), 1)
        return jnp.sum(jnp.where(across == row + start, chosen, 0), axis=1, keepdims=True)

    ids = column(0, picks)
    below = jnp.sum((ids < position).astype(jnp.int32), axis=0, keepdims=True)
    taken = jnp.sum((ids == position).astype(jnp.int32), axis=0, keepdims=True)
    rank = jnp.where(alive & (taken == 0), position - below, -1)
    place = lax.broadcasted_iota(jnp.int32, (rest_chip, 1), 0)
    for d in range(chips):
        owner = lax.bitwise_xor(me // 2, d)
        top = d * rows_chip
        hit = column(owner * picks_chip, picks_chip) == position
        select_ref[top : top + picks_chip, :] = hit.astype(F32).astype(BF16)
        hit = place + owner * rest_chip == rank
        select_ref[top + picks_chip : top + rows_chip, :] = hit.astype(F32).astype(BF16)

    for t in range(0, own.shape[1], TILE):
        at = slice(t, t + TILE)
        rows = jnp.concatenate([own[:, at], sib[:, at]], axis=0)
        found = jnp.dot(select_ref[...], rows, preferred_element_type=F32).astype(BF16)
        for d, out in enumerate(outs):
            out[:, at] = found[d * rows_chip : (d + 1) * rows_chip]


def sum_kernel(*refs):
    *parts, out, picks_ref = refs
    total = parts[0][...]
    for ref in parts[1:]:
        total += ref[...]
    out[...] = total
    picks_ref[...] = total[: picks_ref.shape[0], :]


def row_norms(rows):
    rows = rows.astype(F32)
    return jnp.sum(rows * rows, axis=1, keepdims=True)


def gaps_to(rows_ref, norms, cand):
    inner = lax.dot_general(
        rows_ref[...], cand, (((1,), (1,)), ((), ())), preferred_element_type=F32
    )
    return norms - 2.0 * inner


def tiles_of(cand_ref):
    return [slice(t, t + TILE) for t in range(0, cand_ref.shape[0], TILE)]


def lay_out(parts, rows_ref):
    left = 0
    for part in parts:
        rows_ref[:, left : left + part.shape[1]] = part[: rows_ref.shape[0], :]
        left += part.shape[1]
    return row_norms(rows_ref[...])


def row_masks(picks_chip, rows_chip, own_rows, rows):
    row = lax.broadcasted_iota(jnp.int32, (rows, 1), 0)
    own = row < own_rows
    pick = (lax.rem(row, rows_chip) < picks_chip) | ~own
    return jnp.where(own, 0.0, jnp.inf), jnp.where(pick, 0.0, jnp.inf)


def least(gaps):
    return jnp.min(gaps, axis=0, keepdims=True)


def first_kernel(chip_rows, cand_ref, norm_ref, own, sib, near_ref, best_ref, rows_ref):
    norms = lay_out((own, sib), rows_ref)
    no_row, no_pick = row_masks(*chip_rows, norms.shape[0])
    for at in tiles_of(cand_ref):
        gaps = gaps_to(rows_ref, norms, cand_ref[at, :])
        near_ref[:, at] = least(gaps + no_row) + norm_ref[:, at]
        best_ref[:, at] = least(gaps + no_pick)


def next_kernel(blocks, cand_ref, best_ref, *refs):
    *parts, out, rows_ref = refs
    norms, count, rows = [], len(parts) // blocks, rows_ref.shape[0] // blocks
    for b in range(blocks):
        block = rows_ref.at[b * rows : (b + 1) * rows, :]
        norms.append(lay_out(parts[b * count : (b + 1) * count], block))
    norms = jnp.concatenate(norms, axis=0)
    for at in tiles_of(cand_ref):
        gaps = gaps_to(rows_ref, norms, cand_ref[at, :])
        out[:, at] = jnp.minimum(least(gaps), best_ref[:, at])


def half_kernel(cand_ref, *refs):
    *corner, out, rows_ref = refs
    norms = lay_out(corner, rows_ref)
    for at in tiles_of(cand_ref):
        out[:, at] = gaps_to(rows_ref, norms, cand_ref[at, : rows_ref.shape[1]])


def last_kernel(cand_ref, norm_ref, best_ref, part_ref, *refs):
    *corner, out, rows_ref = refs
    norms = lay_out(corner, rows_ref)
    for at in tiles_of(cand_ref):
        gaps = part_ref[:, at] + gaps_to(rows_ref, norms, cand_ref[at, rows_ref.shape[1] :])
        out[:, at] = jnp.minimum(least(gaps), best_ref[:, at]) + norm_ref[:, at]


def body(candidates, round_one, counts, chosen):
    size, groups = lax.axis_size("mem"), lax.axis_size("grp")
    slots, width = round_one.shape
    half, chips = width // 2, size // 2
    picks, rows = chosen.shape[1], candidates.shape[0]
    picks_chip = picks // chips
    rest_chip = (size * slots * 3 // 8 - picks) // chips
    rows_chip = picks_chip + rest_chip
    live = chips * rows_chip

    def bf16(*dims):
        return jax.ShapeDtypeStruct(dims, BF16)

    def stack(*blocks, after=()):
        operands, layout = [], []
        for block in blocks:
            parts = [p if isinstance(p, tuple) else (p, 0, p.shape[1]) for p in block]
            layout.append([(len(operands) + i, *p[1:]) for i, p in enumerate(parts)])
            operands += [p[0] for p in parts]
        shape = bf16(
            sum(operands[parts[0][0]].shape[0] for parts in layout), sum(p[2] for p in layout[0])
        )
        return call(
            functools.partial(stack_kernel, layout), "stack", shape, operands, after=after, weight=0
        )

    def copy(block, count, after):
        shape = bf16(count, block.shape[1])
        return call(copy_kernel, "copy", shape, (block,), after=after, weight=0)

    line = jax.ShapeDtypeStruct((1, rows), F32)
    tile = jax.ShapeDtypeStruct((8, 128), jnp.int32)
    count = call(
        spread_kernel, "spread", tile, (counts,), specs=[pl.BlockSpec(memory_space=pltpu.SMEM)]
    )
    pair = call(pair_kernel, "pair", tile, (count, flip_permute(count, size, 1)))
    pairs = to_chips(pair, size)
    own, send = call(split_kernel, "split", [bf16(slots, half)] * 2, (round_one,))
    sib = flip_permute(send, size, 1)

    parts = call(
        functools.partial(dense_kernel, size, picks_chip, rest_chip), "dense",
        [bf16(rows_chip, half)] * chips, (chosen, *pairs, own, sib),
        scratch=[pltpu.VMEM((live, 2 * slots), BF16)],
    )
    cand, norm = call(
        load_kernel, "load", [bf16(rows, width), line], (candidates,),
        specs=[pl.BlockSpec(memory_space=pltpu.HBM)], after=parts[:1],
        scratch=[pltpu.SemaphoreType.DMA((rows // TILE * 2,))], limit=42 * MIB,
    )
    got = [flip_permute(parts[d], size, 2 * d) for d in range(1, chips)]
    owned, picked = call(
        sum_kernel, "owned", [bf16(rows_chip, half), bf16(picks_chip, half)], (parts[0], *got),
        after=(norm,),
    )

    shifted = [
        lax.ppermute(picked, "grp", [(g, (g + k) % groups) for g in range(groups)])
        for k in range(1, groups)
    ]

    if chips == 4:
        quarter = half // 2
        own_x, own_y = (flip_permute(owned, size, flip) for flip in (2, 4))
        own_left = flip_permute(stack([(own_x, 0, quarter)]), size, 4)
        own_right = flip_permute(stack([(own_y, quarter, quarter)]), size, 2)
        wait = (own_left, own_right)
        low = stack(*[[(b, 0, quarter)] for b in shifted], after=wait)
        high = stack(*[[(b, quarter, quarter)] for b in shifted], after=wait)
        low_x, high_y = flip_permute(low, size, 2), flip_permute(high, size, 4)
        high_x, low_y = flip_permute(high, size, 2), flip_permute(low, size, 4)
        first = stack([owned], [own_x], [own_y], [own_left, own_right], [low, high])
        others = ([low_x, high_x], [low_y, high_y])
    else:
        far = to_chips(stack(*[[b] for b in shifted]), size)
        first = stack(*[[b] for b in to_chips(owned, size)], [far[0]])
        others = [[b] for b in far[1:-1]]

    near, best = call(
        functools.partial(first_kernel, (picks_chip, rows_chip, live)),
        "products", [line] * 2, (cand, norm, first, flip_permute(first, size, 1)),
        scratch=[pltpu.VMEM((first.shape[0], width), BF16)], weight=WEIGHT // 10,
    )
    rows_end = (groups - 1) * picks_chip
    if chips == 4:
        left = copy(low_x, rows_end + 16, (best,))
        right = copy(high_y, rows_end + 16, (best,))
        corner = (flip_permute(left, size, 4), flip_permute(right, size, 2))
    else:
        corner = (far[-1],)
    operands, handed = [], (left, right) if chips == 4 else ()
    for block in others:
        operands += block
        for b in block:
            after = (best, *handed)
            operands.append(flip_permute(stack([b], after=after), size, 1))
    best = call(
        functools.partial(next_kernel, len(others)), "products_next", line, (cand, best, *operands),
        scratch=[pltpu.VMEM((len(others) * others[0][0].shape[0], width), BF16)], weight=0,
    )
    sent = [copy(part, rows_end, (best,)) for part in corner]
    swapped = [flip_permute(part, size, 1) for part in sent]
    scratch = [pltpu.VMEM((rows_end, half), BF16)]
    part = call(
        half_kernel, "products_half", jax.ShapeDtypeStruct((rows_end, rows), F32), (cand, *corner),
        scratch=scratch, after=(best,),
    )
    final = call(
        last_kernel, "products_last", line, (cand, norm, best, part, *swapped), scratch=scratch
    )
    return near.reshape(-1), final.reshape(-1)


def solution(mesh):
    in_specs = (P(("grp", "mem"), None), P(("grp", "mem"), None), P("grp", "mem"), P("grp", None))
    out_specs = (P(("grp", "mem")), P(("grp", "mem")))
    return jax.shard_map(body, mesh=mesh, in_specs=in_specs, out_specs=out_specs, check_vma=False)
```

```python
import functools

import jax
import jax.numpy as jnp
from jax import lax
from jax.experimental import pallas as pl
from jax.experimental.pallas import tpu as pltpu
from jax.sharding import PartitionSpec as P

TILE = 256
MIB = 1024 * 1024
WEIGHT = 10**10
F32, BF16 = jnp.float32, jnp.bfloat16


def flip_permute(block, size, flip):
    return lax.ppermute(block, "mem", [(m, m ^ flip) for m in range(size)])


def to_chips(block, size):
    return [block] + [flip_permute(block, size, 2 * d) for d in range(1, size // 2)]


def vmem_specs(count):
    return [pl.BlockSpec(memory_space=pltpu.VMEM)] * count


def call(kernel, name, out_shape, operands, specs=None, scratch=(), after=(), limit=28 * MIB, weight=WEIGHT):
    shapes = jax.tree.leaves(out_shape)
    moved = sum(a.size * a.dtype.itemsize for a in list(operands) + shapes)
    count = len(operands)

    def run(*refs):
        kernel(*refs[:count], *refs[count + len(after) :])

    return pl.pallas_call(
        run,
        out_shape=out_shape,
        in_specs=(specs or vmem_specs(count)) + [pl.BlockSpec(memory_space=pl.ANY)] * len(after),
        out_specs=jax.tree.map(lambda _: pl.BlockSpec(memory_space=pltpu.VMEM), out_shape),
        scratch_shapes=scratch,
        compiler_params=pltpu.CompilerParams(vmem_limit_bytes=limit),
        cost_estimate=pl.CostEstimate(flops=weight, bytes_accessed=moved, transcendentals=0),
        name=name,
    )(*operands, *after)


def spread_kernel(count_ref, out):
    out[...] = jnp.broadcast_to(count_ref[0, 0], out.shape)


def pair_kernel(own, sib, out):
    lane = lax.broadcasted_iota(jnp.int32, out.shape, 1)
    out[...] = jnp.where(lane == 0, own[...], sib[...])


def more_kernel(known, counts, got, out):
    out[...] = counts[...]
    out[known : 2 * known, :] = got[:known, :]


def split_kernel(rows_ref, keep_ref, send_ref):
    half = keep_ref.shape[1]
    core = lax.rem(lax.axis_index("mem"), 2)
    keep_ref[...] = rows_ref[:, pl.ds(pl.multiple_of(core * half, half), half)]
    send_ref[...] = rows_ref[:, pl.ds(pl.multiple_of((1 - core) * half, half), half)]


def load_kernel(cand_hbm, cand_ref, norm_ref, sems):
    half = cand_ref.shape[1] // 2
    core = lax.rem(lax.axis_index("mem"), 2)
    tiles, copies = cand_ref.shape[0] // TILE, []
    for t in range(tiles):
        at = pl.ds(t * TILE, TILE)
        for k, own in enumerate((core, 1 - core)):
            copies.append(
                pltpu.make_async_copy(
                    cand_hbm.at[at, pl.ds(pl.multiple_of(own * half, half), half)],
                    cand_ref.at[at, pl.ds(k * half, half)],
                    sems.at[len(copies)],
                )
            )
    for copy in copies:
        copy.start()
    for t in range(tiles):
        for copy in copies[2 * t : 2 * t + 2]:
            copy.wait()
        squares = jnp.zeros((TILE, 128), F32)
        for k in range(0, cand_ref.shape[1], 128):
            entries = cand_ref[t * TILE : (t + 1) * TILE, k : k + 128].astype(F32)
            squares += entries * entries
        norm_ref[:, t * TILE : (t + 1) * TILE] = jnp.sum(squares.T, axis=0, keepdims=True)


def stack_kernel(layout, *refs):
    out, top = refs[-1], 0
    for parts in layout:
        left, rows = 0, refs[parts[0][0]].shape[0]
        for index, start, columns in parts:
            out[top : top + rows, left : left + columns] = refs[index][:, start : start + columns]
            left += columns
        top += rows


def copy_kernel(block, out):
    rows = min(block.shape[0], out.shape[0])
    out[:rows, :] = block[:rows, :]
    if out.shape[0] > rows:
        out[rows:, :] = block[: out.shape[0] - rows, :]


def dense_kernel(size, picks_chip, rest_chip, chosen_ref, *refs):
    chips = size // 2
    counts, own, sib, *outs, select_ref = refs
    slots, picks = own.shape[0], chosen_ref.shape[1]
    rows_chip = picks_chip + rest_chip
    me = lax.axis_index("mem")
    offsets = [jnp.zeros((1, 1), jnp.int32) for _ in range(2)]
    for d in range(chips):
        for h in range(2):
            origin = lax.bitwise_xor(me, 2 * d + h)
            for k in range(2):
                before = (origin < lax.bitwise_xor(me, k)).astype(jnp.int32)
                offsets[k] += counts[d : d + 1, h : h + 1] * before
    lane = lax.broadcasted_iota(jnp.int32, (1, 2 * slots), 1)
    first = lane < slots
    within = jnp.where(first, lane, lane - slots)
    alive = within < jnp.where(first, counts[:1, :1], counts[:1, 1:2])
    position = jnp.where(alive, within + jnp.where(first, offsets[0], offsets[1]), -1)

    chosen = chosen_ref[...]

    def column(start, length):
        row = lax.broadcasted_iota(jnp.int32, (length, picks), 0)
        across = lax.broadcasted_iota(jnp.int32, (length, picks), 1)
        return jnp.sum(jnp.where(across == row + start, chosen, 0), axis=1, keepdims=True)

    ids = column(0, picks)
    below = jnp.sum((ids < position).astype(jnp.int32), axis=0, keepdims=True)
    taken = jnp.sum((ids == position).astype(jnp.int32), axis=0, keepdims=True)
    rank = jnp.where(alive & (taken == 0), position - below, -1)
    place = lax.broadcasted_iota(jnp.int32, (rest_chip, 1), 0)
    for d in range(chips):
        owner = lax.bitwise_xor(me // 2, d)
        top = d * rows_chip
        hit = column(owner * picks_chip, picks_chip) == position
        select_ref[top : top + picks_chip, :] = hit.astype(F32).astype(BF16)
        hit = place + owner * rest_chip == rank
        select_ref[top + picks_chip : top + rows_chip, :] = hit.astype(F32).astype(BF16)

    for t in range(0, own.shape[1], TILE):
        at = slice(t, t + TILE)
        rows = jnp.concatenate([own[:, at], sib[:, at]], axis=0)
        found = jnp.dot(select_ref[...], rows, preferred_element_type=F32).astype(BF16)
        for d, out in enumerate(outs):
            out[:, at] = found[d * rows_chip : (d + 1) * rows_chip]


def sum_kernel(*refs):
    *parts, out, picks_ref = refs
    total = parts[0][...]
    for ref in parts[1:]:
        total += ref[...]
    out[...] = total
    picks_ref[...] = total[: picks_ref.shape[0], :]


def row_norms(rows):
    rows = rows.astype(F32)
    return jnp.sum(rows * rows, axis=1, keepdims=True)


def gaps_to(rows_ref, norms, cand):
    inner = lax.dot_general(
        rows_ref[...], cand, (((1,), (1,)), ((), ())), preferred_element_type=F32
    )
    return norms - 2.0 * inner


def tiles_of(cand_ref):
    return [slice(t, t + TILE) for t in range(0, cand_ref.shape[0], TILE)]


def lay_out(parts, rows_ref):
    left = 0
    for part in parts:
        rows_ref[:, left : left + part.shape[1]] = part[: rows_ref.shape[0], :]
        left += part.shape[1]
    return row_norms(rows_ref[...])


def row_masks(picks_chip, rows_chip, own_rows, rows):
    row = lax.broadcasted_iota(jnp.int32, (rows, 1), 0)
    own = row < own_rows
    pick = (lax.rem(row, rows_chip) < picks_chip) | ~own
    return jnp.where(own, 0.0, jnp.inf), jnp.where(pick, 0.0, jnp.inf)


def least(gaps):
    return jnp.min(gaps, axis=0, keepdims=True)


def first_kernel(chip_rows, cand_ref, norm_ref, own, sib, near_ref, best_ref, rows_ref):
    norms = lay_out((own, sib), rows_ref)
    no_row, no_pick = row_masks(*chip_rows, norms.shape[0])
    for at in tiles_of(cand_ref):
        gaps = gaps_to(rows_ref, norms, cand_ref[at, :])
        near_ref[:, at] = least(gaps + no_row) + norm_ref[:, at]
        best_ref[:, at] = least(gaps + no_pick)


def next_kernel(blocks, cand_ref, best_ref, *refs):
    *parts, out, rows_ref = refs
    norms, count, rows = [], len(parts) // blocks, rows_ref.shape[0] // blocks
    for b in range(blocks):
        block = rows_ref.at[b * rows : (b + 1) * rows, :]
        norms.append(lay_out(parts[b * count : (b + 1) * count], block))
    norms = jnp.concatenate(norms, axis=0)
    for at in tiles_of(cand_ref):
        gaps = gaps_to(rows_ref, norms, cand_ref[at, :])
        out[:, at] = jnp.minimum(least(gaps), best_ref[:, at])


def half_kernel(cand_ref, *refs):
    *corner, out, rows_ref = refs
    norms = lay_out(corner, rows_ref)
    for at in tiles_of(cand_ref):
        out[:, at] = gaps_to(rows_ref, norms, cand_ref[at, : rows_ref.shape[1]])


def last_kernel(cand_ref, norm_ref, best_ref, part_ref, *refs):
    *corner, out, rows_ref = refs
    norms = lay_out(corner, rows_ref)
    for at in tiles_of(cand_ref):
        gaps = part_ref[:, at] + gaps_to(rows_ref, norms, cand_ref[at, rows_ref.shape[1] :])
        out[:, at] = jnp.minimum(least(gaps), best_ref[:, at]) + norm_ref[:, at]


def body(candidates, round_one, counts, chosen):
    size, groups = lax.axis_size("mem"), lax.axis_size("grp")
    slots, width = round_one.shape
    half, chips = width // 2, size // 2
    picks, rows = chosen.shape[1], candidates.shape[0]
    picks_chip = picks // chips
    rest_chip = (size * slots * 3 // 8 - picks) // chips
    rows_chip = picks_chip + rest_chip
    live = chips * rows_chip

    def bf16(*dims):
        return jax.ShapeDtypeStruct(dims, BF16)

    def stack(*blocks, after=()):
        operands, layout = [], []
        for block in blocks:
            parts = [p if isinstance(p, tuple) else (p, 0, p.shape[1]) for p in block]
            layout.append([(len(operands) + i, *p[1:]) for i, p in enumerate(parts)])
            operands += [p[0] for p in parts]
        shape = bf16(
            sum(operands[parts[0][0]].shape[0] for parts in layout), sum(p[2] for p in layout[0])
        )
        return call(
            functools.partial(stack_kernel, layout), "stack", shape, operands, after=after, weight=0
        )

    def copy(block, count, after):
        shape = bf16(count, block.shape[1])
        return call(copy_kernel, "copy", shape, (block,), after=after, weight=0)

    line = jax.ShapeDtypeStruct((1, rows), F32)
    tile = jax.ShapeDtypeStruct((8, 128), jnp.int32)
    count = call(
        spread_kernel, "spread", tile, (counts,), specs=[pl.BlockSpec(memory_space=pltpu.SMEM)]
    )
    pair = call(pair_kernel, "pair", tile, (count, flip_permute(count, size, 1)))
    group_counts = pair
    for stage in range(chips.bit_length() - 1):
        group_counts = call(
            functools.partial(more_kernel, 1 << stage), "more_counts", tile,
            (group_counts, flip_permute(group_counts, size, 2 << stage)),
        )
    own, send = call(split_kernel, "split", [bf16(slots, half)] * 2, (round_one,))
    sib = flip_permute(send, size, 1)

    parts = call(
        functools.partial(dense_kernel, size, picks_chip, rest_chip), "dense",
        [bf16(rows_chip, half)] * chips, (chosen, group_counts, own, sib),
        scratch=[pltpu.VMEM((live, 2 * slots), BF16)],
    )
    cand, norm = call(
        load_kernel, "load", [bf16(rows, width), line], (candidates,),
        specs=[pl.BlockSpec(memory_space=pltpu.HBM)], after=parts[:1],
        scratch=[pltpu.SemaphoreType.DMA((rows // TILE * 2,))], limit=42 * MIB,
    )
    got = [flip_permute(parts[d], size, 2 * d) for d in range(1, chips)]
    owned, picked = call(
        sum_kernel, "owned", [bf16(rows_chip, half), bf16(picks_chip, half)], (parts[0], *got),
        after=(norm,),
    )

    shifted = [
        lax.ppermute(picked, "grp", [(g, (g + k) % groups) for g in range(groups)])
        for k in range(1, groups)
    ]

    if chips == 4:
        quarter = half // 2
        own_x, own_y = (flip_permute(owned, size, flip) for flip in (2, 4))
        own_left = flip_permute(stack([(own_x, 0, quarter)]), size, 4)
        own_right = flip_permute(stack([(own_y, quarter, quarter)]), size, 2)
        wait = (own_left, own_right)
        low = stack(*[[(b, 0, quarter)] for b in shifted], after=wait)
        high = stack(*[[(b, quarter, quarter)] for b in shifted], after=wait)
        low_x, high_y = flip_permute(low, size, 2), flip_permute(high, size, 4)
        high_x, low_y = flip_permute(high, size, 2), flip_permute(low, size, 4)
        first = stack([owned], [own_x], [own_y], [own_left, own_right], [low, high])
        others = ([low_x, high_x], [low_y, high_y])
    else:
        far = to_chips(stack(*[[b] for b in shifted]), size)
        first = stack(*[[b] for b in to_chips(owned, size)], [far[0]])
        others = [[b] for b in far[1:-1]]

    near, best = call(
        functools.partial(first_kernel, (picks_chip, rows_chip, live)),
        "products", [line] * 2, (cand, norm, first, flip_permute(first, size, 1)),
        scratch=[pltpu.VMEM((first.shape[0], width), BF16)], weight=WEIGHT // 10,
    )
    rows_end = (groups - 1) * picks_chip
    if chips == 4:
        left = copy(low_x, rows_end + 16, (best,))
        right = copy(high_y, rows_end + 16, (best,))
        corner = (flip_permute(left, size, 4), flip_permute(right, size, 2))
    else:
        corner = (far[-1],)
    operands, handed = [], (left, right) if chips == 4 else ()
    for block in others:
        operands += block
        for b in block:
            after = (best, *handed)
            operands.append(flip_permute(stack([b], after=after), size, 1))
    best = call(
        functools.partial(next_kernel, len(others)), "products_next", line, (cand, best, *operands),
        scratch=[pltpu.VMEM((len(others) * others[0][0].shape[0], width), BF16)], weight=0,
    )
    sent = [copy(part, rows_end, (best,)) for part in corner]
    swapped = [flip_permute(part, size, 1) for part in sent]
    scratch = [pltpu.VMEM((rows_end, half), BF16)]
    part = call(
        half_kernel, "products_half", jax.ShapeDtypeStruct((rows_end, rows), F32), (cand, *corner),
        scratch=scratch, after=(best,),
    )
    final = call(
        last_kernel, "products_last", line, (cand, norm, best, part, *swapped), scratch=scratch
    )
    return near.reshape(-1), final.reshape(-1)


def solution(mesh):
    in_specs = (P(("grp", "mem"), None), P(("grp", "mem"), None), P("grp", "mem"), P("grp", None))
    out_specs = (P(("grp", "mem")), P(("grp", "mem")))
    return jax.shard_map(body, mesh=mesh, in_specs=in_specs, out_specs=out_specs, check_vma=False)
```

```python
import functools

import jax
import jax.numpy as jnp
from jax import lax
from jax.experimental import pallas as pl
from jax.experimental.pallas import tpu as pltpu
from jax.sharding import PartitionSpec as P

TILE = 256
MIB = 1024 * 1024
WEIGHT = 10**10
F32, BF16 = jnp.float32, jnp.bfloat16


def flip_permute(block, size, flip):
    return lax.ppermute(block, "mem", [(m, m ^ flip) for m in range(size)])


def to_chips(block, size):
    return [block] + [flip_permute(block, size, 2 * d) for d in range(1, size // 2)]


def vmem_specs(count):
    return [pl.BlockSpec(memory_space=pltpu.VMEM)] * count


def call(kernel, name, out_shape, operands, specs=None, scratch=(), after=(), limit=28 * MIB, weight=WEIGHT):
    shapes = jax.tree.leaves(out_shape)
    moved = sum(a.size * a.dtype.itemsize for a in list(operands) + shapes)
    count = len(operands)

    def run(*refs):
        kernel(*refs[:count], *refs[count + len(after) :])

    return pl.pallas_call(
        run,
        out_shape=out_shape,
        in_specs=(specs or vmem_specs(count)) + [pl.BlockSpec(memory_space=pl.ANY)] * len(after),
        out_specs=jax.tree.map(lambda _: pl.BlockSpec(memory_space=pltpu.VMEM), out_shape),
        scratch_shapes=scratch,
        compiler_params=pltpu.CompilerParams(vmem_limit_bytes=limit),
        cost_estimate=pl.CostEstimate(flops=weight, bytes_accessed=moved, transcendentals=0),
        name=name,
    )(*operands, *after)


def spread_kernel(count_ref, out):
    out[...] = jnp.broadcast_to(count_ref[0, 0], out.shape)


def pair_kernel(own, sib, out):
    lane = lax.broadcasted_iota(jnp.int32, out.shape, 1)
    out[...] = jnp.where(lane == 0, own[...], sib[...])


def split_kernel(rows_ref, keep_ref, send_ref):
    half = keep_ref.shape[1]
    core = lax.rem(lax.axis_index("mem"), 2)
    keep_ref[...] = rows_ref[:, pl.ds(pl.multiple_of(core * half, half), half)]
    send_ref[...] = rows_ref[:, pl.ds(pl.multiple_of((1 - core) * half, half), half)]


def load_kernel(cand_hbm, cand_ref, norm_ref, sems):
    half = cand_ref.shape[1] // 2
    core = lax.rem(lax.axis_index("mem"), 2)
    tiles, copies = cand_ref.shape[0] // TILE, []
    for t in range(tiles):
        at = pl.ds(t * TILE, TILE)
        for k, own in enumerate((core, 1 - core)):
            copies.append(
                pltpu.make_async_copy(
                    cand_hbm.at[at, pl.ds(pl.multiple_of(own * half, half), half)],
                    cand_ref.at[at, pl.ds(k * half, half)],
                    sems.at[len(copies)],
                )
            )
    for copy in copies:
        copy.start()
    for t in range(tiles):
        for copy in copies[2 * t : 2 * t + 2]:
            copy.wait()
        squares = jnp.zeros((TILE, 128), F32)
        for k in range(0, cand_ref.shape[1], 128):
            entries = cand_ref[t * TILE : (t + 1) * TILE, k : k + 128].astype(F32)
            squares += entries * entries
        norm_ref[:, t * TILE : (t + 1) * TILE] = jnp.sum(squares.T, axis=0, keepdims=True)


def stack_kernel(layout, *refs):
    out, top = refs[-1], 0
    for parts in layout:
        left, rows = 0, refs[parts[0][0]].shape[0]
        for index, start, columns in parts:
            out[top : top + rows, left : left + columns] = refs[index][:, start : start + columns]
            left += columns
        top += rows


def copy_kernel(block, out):
    rows = min(block.shape[0], out.shape[0])
    out[:rows, :] = block[:rows, :]
    if out.shape[0] > rows:
        out[rows:, :] = block[: out.shape[0] - rows, :]


def dense_kernel(size, picks_chip, rest_chip, chosen_ref, *refs):
    chips = size // 2
    counts, (own, sib, *outs, select_ref) = refs[:chips], refs[chips:]
    slots, picks = own.shape[0], chosen_ref.shape[1]
    rows_chip = picks_chip + rest_chip
    me = lax.axis_index("mem")
    offsets = [jnp.zeros((1, 1), jnp.int32) for _ in range(2)]
    for d, ref in enumerate(counts):
        for h in range(2):
            origin = lax.bitwise_xor(me, 2 * d + h)
            for k in range(2):
                before = (origin < lax.bitwise_xor(me, k)).astype(jnp.int32)
                offsets[k] += ref[:1, h : h + 1] * before
    lane = lax.broadcasted_iota(jnp.int32, (1, 2 * slots), 1)
    first = lane < slots
    within = jnp.where(first, lane, lane - slots)
    alive = within < jnp.where(first, counts[0][:1, :1], counts[0][:1, 1:2])
    position = jnp.where(alive, within + jnp.where(first, offsets[0], offsets[1]), -1)

    chosen = chosen_ref[...]

    def column(start, length):
        row = lax.broadcasted_iota(jnp.int32, (length, picks), 0)
        across = lax.broadcasted_iota(jnp.int32, (length, picks), 1)
        return jnp.sum(jnp.where(across == row + start, chosen, 0), axis=1, keepdims=True)

    ids = column(0, picks)
    below = jnp.sum((ids < position).astype(jnp.int32), axis=0, keepdims=True)
    taken = jnp.sum((ids == position).astype(jnp.int32), axis=0, keepdims=True)
    rank = jnp.where(alive & (taken == 0), position - below, -1)
    place = lax.broadcasted_iota(jnp.int32, (rest_chip, 1), 0)
    for d in range(chips):
        owner = lax.bitwise_xor(me // 2, d)
        top = d * rows_chip
        hit = column(owner * picks_chip, picks_chip) == position
        select_ref[top : top + picks_chip, :] = hit.astype(F32).astype(BF16)
        hit = place + owner * rest_chip == rank
        select_ref[top + picks_chip : top + rows_chip, :] = hit.astype(F32).astype(BF16)

    for t in range(0, own.shape[1], TILE):
        at = slice(t, t + TILE)
        rows = jnp.concatenate([own[:, at], sib[:, at]], axis=0)
        found = jnp.dot(select_ref[...], rows, preferred_element_type=F32).astype(BF16)
        for d, out in enumerate(outs):
            out[:, at] = found[d * rows_chip : (d + 1) * rows_chip]


def sum_kernel(*refs):
    *parts, low, high, picks_ref = refs
    total = parts[0][...]
    for ref in parts[1:]:
        total += ref[...]
    low[...] = total[:, : low.shape[1]]
    high[...] = total[:, low.shape[1] :]
    picks_ref[...] = total[: picks_ref.shape[0], :]


def row_norms(rows):
    rows = rows.astype(F32)
    return jnp.sum(rows * rows, axis=1, keepdims=True)


def gaps_to(rows_ref, norms, cand):
    inner = lax.dot_general(
        rows_ref[...], cand, (((1,), (1,)), ((), ())), preferred_element_type=F32
    )
    return norms - 2.0 * inner


def tiles_of(cand_ref):
    return [slice(t, t + TILE) for t in range(0, cand_ref.shape[0], TILE)]


def lay_out(parts, rows_ref):
    left = 0
    for part in parts:
        rows_ref[:, left : left + part.shape[1]] = part[: rows_ref.shape[0], :]
        left += part.shape[1]
    return row_norms(rows_ref[...])


def row_masks(picks_chip, rows_chip, own_rows, rows):
    row = lax.broadcasted_iota(jnp.int32, (rows, 1), 0)
    own = row < own_rows
    pick = (lax.rem(row, rows_chip) < picks_chip) | ~own
    return jnp.where(own, 0.0, jnp.inf), jnp.where(pick, 0.0, jnp.inf)


def least(gaps):
    return jnp.min(gaps, axis=0, keepdims=True)


def first_kernel(chip_rows, cand_ref, norm_ref, own, sib, near_ref, best_ref, rows_ref):
    norms = lay_out((own, sib), rows_ref)
    no_row, no_pick = row_masks(*chip_rows, norms.shape[0])
    for at in tiles_of(cand_ref):
        gaps = gaps_to(rows_ref, norms, cand_ref[at, :])
        near_ref[:, at] = least(gaps + no_row) + norm_ref[:, at]
        best_ref[:, at] = least(gaps + no_pick)


def next_kernel(blocks, cand_ref, best_ref, *refs):
    *parts, out, rows_ref = refs
    norms, count, rows = [], len(parts) // blocks, rows_ref.shape[0] // blocks
    for b in range(blocks):
        block = rows_ref.at[b * rows : (b + 1) * rows, :]
        norms.append(lay_out(parts[b * count : (b + 1) * count], block))
    norms = jnp.concatenate(norms, axis=0)
    for at in tiles_of(cand_ref):
        gaps = gaps_to(rows_ref, norms, cand_ref[at, :])
        out[:, at] = jnp.minimum(least(gaps), best_ref[:, at])


def half_kernel(cand_ref, *refs):
    *corner, out, rows_ref = refs
    norms = lay_out(corner, rows_ref)
    for at in tiles_of(cand_ref):
        out[:, at] = gaps_to(rows_ref, norms, cand_ref[at, : rows_ref.shape[1]])


def last_kernel(cand_ref, norm_ref, best_ref, part_ref, *refs):
    *corner, out, rows_ref = refs
    norms = lay_out(corner, rows_ref)
    for at in tiles_of(cand_ref):
        gaps = part_ref[:, at] + gaps_to(rows_ref, norms, cand_ref[at, rows_ref.shape[1] :])
        out[:, at] = jnp.minimum(least(gaps), best_ref[:, at]) + norm_ref[:, at]


def body(candidates, round_one, counts, chosen):
    size, groups = lax.axis_size("mem"), lax.axis_size("grp")
    slots, width = round_one.shape
    half, chips = width // 2, size // 2
    picks, rows = chosen.shape[1], candidates.shape[0]
    picks_chip = picks // chips
    rest_chip = (size * slots * 3 // 8 - picks) // chips
    rows_chip = picks_chip + rest_chip
    live = chips * rows_chip

    def bf16(*dims):
        return jax.ShapeDtypeStruct(dims, BF16)

    def stack(*blocks, after=()):
        operands, layout = [], []
        for block in blocks:
            parts = [p if isinstance(p, tuple) else (p, 0, p.shape[1]) for p in block]
            layout.append([(len(operands) + i, *p[1:]) for i, p in enumerate(parts)])
            operands += [p[0] for p in parts]
        shape = bf16(
            sum(operands[parts[0][0]].shape[0] for parts in layout), sum(p[2] for p in layout[0])
        )
        return call(
            functools.partial(stack_kernel, layout), "stack", shape, operands, after=after, weight=0
        )

    def copy(block, count, after):
        shape = bf16(count, block.shape[1])
        return call(copy_kernel, "copy", shape, (block,), after=after, weight=0)

    line = jax.ShapeDtypeStruct((1, rows), F32)
    tile = jax.ShapeDtypeStruct((8, 128), jnp.int32)
    count = call(
        spread_kernel, "spread", tile, (counts,), specs=[pl.BlockSpec(memory_space=pltpu.SMEM)]
    )
    pair = call(pair_kernel, "pair", tile, (count, flip_permute(count, size, 1)))
    pairs = to_chips(pair, size)
    own, send = call(split_kernel, "split", [bf16(slots, half)] * 2, (round_one,))
    sib = flip_permute(send, size, 1)

    parts = call(
        functools.partial(dense_kernel, size, picks_chip, rest_chip), "dense",
        [bf16(rows_chip, half)] * chips, (chosen, *pairs, own, sib),
        scratch=[pltpu.VMEM((live, 2 * slots), BF16)],
    )
    cand, norm = call(
        load_kernel, "load", [bf16(rows, width), line], (candidates,),
        specs=[pl.BlockSpec(memory_space=pltpu.HBM)], after=parts[:1],
        scratch=[pltpu.SemaphoreType.DMA((rows // TILE * 2,))], limit=42 * MIB,
    )
    got = [flip_permute(parts[d], size, 2 * d) for d in range(1, chips)]
    quarter = half // 2
    *owned, picked = call(
        sum_kernel, "owned", [bf16(rows_chip, quarter)] * 2 + [bf16(picks_chip, half)],
        (parts[0], *got),
        after=(norm,),
    )

    shifted = [
        lax.ppermute(picked, "grp", [(g, (g + k) % groups) for g in range(groups)])
        for k in range(1, groups)
    ]

    if chips == 4:
        own_x, own_y = ([flip_permute(part, size, flip) for part in owned] for flip in (2, 4))
        own_left, own_right = flip_permute(own_x[0], size, 4), flip_permute(own_y[1], size, 2)
        wait = (own_left, own_right)
        low = stack(*[[(b, 0, quarter)] for b in shifted], after=wait)
        high = stack(*[[(b, quarter, quarter)] for b in shifted], after=wait)
        low_x, high_y = flip_permute(low, size, 2), flip_permute(high, size, 4)
        high_x, low_y = flip_permute(high, size, 2), flip_permute(low, size, 4)
        first = stack(owned, own_x, own_y, [own_left, own_right], [low, high])
        others = ([low_x, high_x], [low_y, high_y])
    else:
        far = to_chips(stack(*[[b] for b in shifted]), size)
        first = stack(*[[b] for b in to_chips(stack(owned), size)], [far[0]])
        others = [[b] for b in far[1:-1]]

    near, best = call(
        functools.partial(first_kernel, (picks_chip, rows_chip, live)),
        "products", [line] * 2, (cand, norm, first, flip_permute(first, size, 1)),
        scratch=[pltpu.VMEM((first.shape[0], width), BF16)], weight=WEIGHT // 10,
    )
    rows_end = (groups - 1) * picks_chip
    if chips == 4:
        left = copy(low_x, rows_end + 16, (best,))
        right = copy(high_y, rows_end + 16, (best,))
        corner = (flip_permute(left, size, 4), flip_permute(right, size, 2))
    else:
        corner = (far[-1],)
    operands, handed = [], (left, right) if chips == 4 else ()
    for block in others:
        operands += block
        for b in block:
            after = (best, *handed)
            operands.append(flip_permute(stack([b], after=after), size, 1))
    best = call(
        functools.partial(next_kernel, len(others)), "products_next", line, (cand, best, *operands),
        scratch=[pltpu.VMEM((len(others) * others[0][0].shape[0], width), BF16)], weight=0,
    )
    sent = [copy(part, rows_end, (best,)) for part in corner]
    swapped = [flip_permute(part, size, 1) for part in sent]
    scratch = [pltpu.VMEM((rows_end, half), BF16)]
    part = call(
        half_kernel, "products_half", jax.ShapeDtypeStruct((rows_end, rows), F32), (cand, *corner),
        scratch=scratch, after=(best,),
    )
    final = call(
        last_kernel, "products_last", line, (cand, norm, best, part, *swapped), scratch=scratch
    )
    return near.reshape(-1), final.reshape(-1)


def solution(mesh):
    in_specs = (P(("grp", "mem"), None), P(("grp", "mem"), None), P("grp", "mem"), P("grp", None))
    out_specs = (P(("grp", "mem")), P(("grp", "mem")))
    return jax.shard_map(body, mesh=mesh, in_specs=in_specs, out_specs=out_specs, check_vma=False)
```

```python
import functools

import jax
import jax.numpy as jnp
from jax import lax
from jax.experimental import pallas as pl
from jax.experimental.pallas import tpu as pltpu
from jax.sharding import PartitionSpec as P

TILE = 256
MIB = 1024 * 1024
WEIGHT = 10**10
F32, BF16 = jnp.float32, jnp.bfloat16


def flip_permute(block, size, flip):
    return lax.ppermute(block, "mem", [(m, m ^ flip) for m in range(size)])


def to_chips(block, size):
    return [block] + [flip_permute(block, size, 2 * d) for d in range(1, size // 2)]


def vmem_specs(count):
    return [pl.BlockSpec(memory_space=pltpu.VMEM)] * count


def call(kernel, name, out_shape, operands, specs=None, scratch=(), after=(), limit=28 * MIB, weight=WEIGHT):
    shapes = jax.tree.leaves(out_shape)
    moved = sum(a.size * a.dtype.itemsize for a in list(operands) + shapes)
    count = len(operands)

    def run(*refs):
        kernel(*refs[:count], *refs[count + len(after) :])

    return pl.pallas_call(
        run,
        out_shape=out_shape,
        in_specs=(specs or vmem_specs(count)) + [pl.BlockSpec(memory_space=pl.ANY)] * len(after),
        out_specs=jax.tree.map(lambda _: pl.BlockSpec(memory_space=pltpu.VMEM), out_shape),
        scratch_shapes=scratch,
        compiler_params=pltpu.CompilerParams(vmem_limit_bytes=limit),
        cost_estimate=pl.CostEstimate(flops=weight, bytes_accessed=moved, transcendentals=0),
        name=name,
    )(*operands, *after)


def spread_kernel(count_ref, out):
    out[...] = jnp.broadcast_to(count_ref[0, 0], out.shape)


def pair_kernel(own, sib, out):
    lane = lax.broadcasted_iota(jnp.int32, out.shape, 1)
    out[...] = jnp.where(lane == 0, own[...], sib[...])


def split_kernel(rows_ref, keep_ref, send_ref):
    half = keep_ref.shape[1]
    core = lax.rem(lax.axis_index("mem"), 2)
    keep_ref[...] = rows_ref[:, pl.ds(pl.multiple_of(core * half, half), half)]
    send_ref[...] = rows_ref[:, pl.ds(pl.multiple_of((1 - core) * half, half), half)]


def load_kernel(cand_hbm, cand_ref, norm_ref, sems):
    half = cand_ref.shape[1] // 2
    core = lax.rem(lax.axis_index("mem"), 2)
    tiles, copies = cand_ref.shape[0] // TILE, []
    for t in range(tiles):
        at = pl.ds(t * TILE, TILE)
        for k, own in enumerate((core, 1 - core)):
            copies.append(
                pltpu.make_async_copy(
                    cand_hbm.at[at, pl.ds(pl.multiple_of(own * half, half), half)],
                    cand_ref.at[at, pl.ds(k * half, half)],
                    sems.at[len(copies)],
                )
            )
    for copy in copies:
        copy.start()
    for t in range(tiles):
        for copy in copies[2 * t : 2 * t + 2]:
            copy.wait()
        squares = jnp.zeros((TILE, 128), F32)
        for k in range(0, cand_ref.shape[1], 128):
            entries = cand_ref[t * TILE : (t + 1) * TILE, k : k + 128].astype(F32)
            squares += entries * entries
        norm_ref[:, t * TILE : (t + 1) * TILE] = jnp.sum(squares.T, axis=0, keepdims=True)


def stack_kernel(layout, *refs):
    out, top = refs[-1], 0
    for parts in layout:
        left, rows = 0, refs[parts[0][0]].shape[0]
        for index, start, columns in parts:
            out[top : top + rows, left : left + columns] = refs[index][:, start : start + columns]
            left += columns
        top += rows


def copy_kernel(block, out):
    rows = min(block.shape[0], out.shape[0])
    out[:rows, :] = block[:rows, :]
    if out.shape[0] > rows:
        out[rows:, :] = block[: out.shape[0] - rows, :]


def dense_kernel(size, picks_chip, rest_chip, chosen_ref, *refs):
    chips = size // 2
    counts, (own, sib, *outs, select_ref) = refs[:chips], refs[chips:]
    slots, picks = own.shape[0], chosen_ref.shape[1]
    rows_chip = picks_chip + rest_chip
    me = lax.axis_index("mem")
    offsets = [jnp.zeros((1, 1), jnp.int32) for _ in range(2)]
    for d, ref in enumerate(counts):
        for h in range(2):
            origin = lax.bitwise_xor(me, 2 * d + h)
            for k in range(2):
                before = (origin < lax.bitwise_xor(me, k)).astype(jnp.int32)
                offsets[k] += ref[:1, h : h + 1] * before
    lane = lax.broadcasted_iota(jnp.int32, (1, 2 * slots), 1)
    first = lane < slots
    within = jnp.where(first, lane, lane - slots)
    alive = within < jnp.where(first, counts[0][:1, :1], counts[0][:1, 1:2])
    position = jnp.where(alive, within + jnp.where(first, offsets[0], offsets[1]), -1)

    chosen = chosen_ref[...]

    def column(start, length):
        row = lax.broadcasted_iota(jnp.int32, (length, picks), 0)
        across = lax.broadcasted_iota(jnp.int32, (length, picks), 1)
        return jnp.sum(jnp.where(across == row + start, chosen, 0), axis=1, keepdims=True)

    ids = column(0, picks)
    below = jnp.sum((ids < position).astype(jnp.int32), axis=0, keepdims=True)
    taken = jnp.sum((ids == position).astype(jnp.int32), axis=0, keepdims=True)
    rank = jnp.where(alive & (taken == 0), position - below, -1)
    place = lax.broadcasted_iota(jnp.int32, (rest_chip, 1), 0)
    for d in range(chips):
        owner = lax.bitwise_xor(me // 2, d)
        top = d * rows_chip
        hit = column(owner * picks_chip, picks_chip) == position
        select_ref[top : top + picks_chip, :] = hit.astype(F32).astype(BF16)
        hit = place + owner * rest_chip == rank
        select_ref[top + picks_chip : top + rows_chip, :] = hit.astype(F32).astype(BF16)

    for t in range(0, own.shape[1], TILE):
        at = slice(t, t + TILE)
        rows = jnp.concatenate([own[:, at], sib[:, at]], axis=0)
        found = jnp.dot(select_ref[...], rows, preferred_element_type=F32).astype(BF16)
        for d, out in enumerate(outs):
            out[:, at] = found[d * rows_chip : (d + 1) * rows_chip]


def sum_kernel(*refs):
    *parts, out, picks_ref = refs
    total = parts[0][...]
    for ref in parts[1:]:
        total += ref[...]
    out[...] = total
    picks_ref[...] = total[: picks_ref.shape[0], :]


def row_norms(rows):
    rows = rows.astype(F32)
    return jnp.sum(rows * rows, axis=1, keepdims=True)


def gaps_to(rows_ref, norms, cand):
    inner = lax.dot_general(
        rows_ref[...], cand, (((1,), (1,)), ((), ())), preferred_element_type=F32
    )
    return norms - 2.0 * inner


def tiles_of(cand_ref):
    return [slice(t, t + 2 * TILE) for t in range(0, cand_ref.shape[0], 2 * TILE)]


def lay_out(parts, rows_ref):
    left = 0
    for part in parts:
        rows_ref[:, left : left + part.shape[1]] = part[: rows_ref.shape[0], :]
        left += part.shape[1]
    return row_norms(rows_ref[...])


def row_masks(picks_chip, rows_chip, own_rows, rows):
    row = lax.broadcasted_iota(jnp.int32, (rows, 1), 0)
    own = row < own_rows
    pick = (lax.rem(row, rows_chip) < picks_chip) | ~own
    return jnp.where(own, 0.0, jnp.inf), jnp.where(pick, 0.0, jnp.inf)


def least(gaps):
    return jnp.min(gaps, axis=0, keepdims=True)


def first_kernel(chip_rows, cand_ref, norm_ref, own, sib, near_ref, best_ref, rows_ref):
    norms = lay_out((own, sib), rows_ref)
    no_row, no_pick = row_masks(*chip_rows, norms.shape[0])
    for at in tiles_of(cand_ref):
        gaps = gaps_to(rows_ref, norms, cand_ref[at, :])
        near_ref[:, at] = least(gaps + no_row) + norm_ref[:, at]
        best_ref[:, at] = least(gaps + no_pick)


def next_kernel(blocks, cand_ref, best_ref, *refs):
    *parts, out, rows_ref = refs
    norms, count, rows = [], len(parts) // blocks, rows_ref.shape[0] // blocks
    for b in range(blocks):
        block = rows_ref.at[b * rows : (b + 1) * rows, :]
        norms.append(lay_out(parts[b * count : (b + 1) * count], block))
    norms = jnp.concatenate(norms, axis=0)
    for at in tiles_of(cand_ref):
        gaps = gaps_to(rows_ref, norms, cand_ref[at, :])
        out[:, at] = jnp.minimum(least(gaps), best_ref[:, at])


def half_kernel(cand_ref, *refs):
    *corner, out, rows_ref = refs
    norms = lay_out(corner, rows_ref)
    for at in tiles_of(cand_ref):
        out[:, at] = gaps_to(rows_ref, norms, cand_ref[at, : rows_ref.shape[1]])


def last_kernel(cand_ref, norm_ref, best_ref, part_ref, *refs):
    *corner, out, rows_ref = refs
    norms = lay_out(corner, rows_ref)
    for at in tiles_of(cand_ref):
        gaps = part_ref[:, at] + gaps_to(rows_ref, norms, cand_ref[at, rows_ref.shape[1] :])
        out[:, at] = jnp.minimum(least(gaps), best_ref[:, at]) + norm_ref[:, at]


def body(candidates, round_one, counts, chosen):
    size, groups = lax.axis_size("mem"), lax.axis_size("grp")
    slots, width = round_one.shape
    half, chips = width // 2, size // 2
    picks, rows = chosen.shape[1], candidates.shape[0]
    picks_chip = picks // chips
    rest_chip = (size * slots * 3 // 8 - picks) // chips
    rows_chip = picks_chip + rest_chip
    live = chips * rows_chip

    def bf16(*dims):
        return jax.ShapeDtypeStruct(dims, BF16)

    def stack(*blocks, after=()):
        operands, layout = [], []
        for block in blocks:
            parts = [p if isinstance(p, tuple) else (p, 0, p.shape[1]) for p in block]
            layout.append([(len(operands) + i, *p[1:]) for i, p in enumerate(parts)])
            operands += [p[0] for p in parts]
        shape = bf16(
            sum(operands[parts[0][0]].shape[0] for parts in layout), sum(p[2] for p in layout[0])
        )
        return call(
            functools.partial(stack_kernel, layout), "stack", shape, operands, after=after, weight=0
        )

    def copy(block, count, after):
        shape = bf16(count, block.shape[1])
        return call(copy_kernel, "copy", shape, (block,), after=after, weight=0)

    line = jax.ShapeDtypeStruct((1, rows), F32)
    tile = jax.ShapeDtypeStruct((8, 128), jnp.int32)
    count = call(
        spread_kernel, "spread", tile, (counts,), specs=[pl.BlockSpec(memory_space=pltpu.SMEM)]
    )
    pair = call(pair_kernel, "pair", tile, (count, flip_permute(count, size, 1)))
    pairs = to_chips(pair, size)
    own, send = call(split_kernel, "split", [bf16(slots, half)] * 2, (round_one,))
    sib = flip_permute(send, size, 1)

    parts = call(
        functools.partial(dense_kernel, size, picks_chip, rest_chip), "dense",
        [bf16(rows_chip, half)] * chips, (chosen, *pairs, own, sib),
        scratch=[pltpu.VMEM((live, 2 * slots), BF16)],
    )
    cand, norm = call(
        load_kernel, "load", [bf16(rows, width), line], (candidates,),
        specs=[pl.BlockSpec(memory_space=pltpu.HBM)], after=parts[:1],
        scratch=[pltpu.SemaphoreType.DMA((rows // TILE * 2,))], limit=42 * MIB,
    )
    got = [flip_permute(parts[d], size, 2 * d) for d in range(1, chips)]
    owned, picked = call(
        sum_kernel, "owned", [bf16(rows_chip, half), bf16(picks_chip, half)], (parts[0], *got),
        after=(norm,),
    )

    shifted = [
        lax.ppermute(picked, "grp", [(g, (g + k) % groups) for g in range(groups)])
        for k in range(1, groups)
    ]

    if chips == 4:
        quarter = half // 2
        own_x, own_y = (flip_permute(owned, size, flip) for flip in (2, 4))
        own_left = flip_permute(stack([(own_x, 0, quarter)]), size, 4)
        own_right = flip_permute(stack([(own_y, quarter, quarter)]), size, 2)
        wait = (own_left, own_right)
        low = stack(*[[(b, 0, quarter)] for b in shifted], after=wait)
        high = stack(*[[(b, quarter, quarter)] for b in shifted], after=wait)
        low_x, high_y = flip_permute(low, size, 2), flip_permute(high, size, 4)
        high_x, low_y = flip_permute(high, size, 2), flip_permute(low, size, 4)
        first = stack([owned], [own_x], [own_y], [own_left, own_right], [low, high])
        others = ([low_x, high_x], [low_y, high_y])
    else:
        far = to_chips(stack(*[[b] for b in shifted]), size)
        first = stack(*[[b] for b in to_chips(owned, size)], [far[0]])
        others = [[b] for b in far[1:-1]]

    near, best = call(
        functools.partial(first_kernel, (picks_chip, rows_chip, live)),
        "products", [line] * 2, (cand, norm, first, flip_permute(first, size, 1)),
        scratch=[pltpu.VMEM((first.shape[0], width), BF16)], weight=WEIGHT // 10,
    )
    rows_end = (groups - 1) * picks_chip
    if chips == 4:
        left = copy(low_x, rows_end + 16, (best,))
        right = copy(high_y, rows_end + 16, (best,))
        corner = (flip_permute(left, size, 4), flip_permute(right, size, 2))
    else:
        corner = (far[-1],)
    operands, handed = [], (left, right) if chips == 4 else ()
    for block in others:
        operands += block
        for b in block:
            after = (best, *handed)
            operands.append(flip_permute(stack([b], after=after), size, 1))
    best = call(
        functools.partial(next_kernel, len(others)), "products_next", line, (cand, best, *operands),
        scratch=[pltpu.VMEM((len(others) * others[0][0].shape[0], width), BF16)], weight=0,
    )
    sent = [copy(part, rows_end, (best,)) for part in corner]
    swapped = [flip_permute(part, size, 1) for part in sent]
    scratch = [pltpu.VMEM((rows_end, half), BF16)]
    part = call(
        half_kernel, "products_half", jax.ShapeDtypeStruct((rows_end, rows), F32), (cand, *corner),
        scratch=scratch, after=(best,),
    )
    final = call(
        last_kernel, "products_last", line, (cand, norm, best, part, *swapped), scratch=scratch
    )
    return near.reshape(-1), final.reshape(-1)


def solution(mesh):
    in_specs = (P(("grp", "mem"), None), P(("grp", "mem"), None), P("grp", "mem"), P("grp", None))
    out_specs = (P(("grp", "mem")), P(("grp", "mem")))
    return jax.shard_map(body, mesh=mesh, in_specs=in_specs, out_specs=out_specs, check_vma=False)
```

```python
import functools

import jax
import jax.numpy as jnp
from jax import lax
from jax.experimental import pallas as pl
from jax.experimental.pallas import tpu as pltpu
from jax.sharding import PartitionSpec as P

TILE = 256
MIB = 1024 * 1024
WEIGHT = 10**10
F32, BF16 = jnp.float32, jnp.bfloat16


def flip_permute(block, size, flip):
    return lax.ppermute(block, "mem", [(m, m ^ flip) for m in range(size)])


def to_chips(block, size):
    return [block] + [flip_permute(block, size, 2 * d) for d in range(1, size // 2)]


def vmem_specs(count):
    return [pl.BlockSpec(memory_space=pltpu.VMEM)] * count


def call(kernel, name, out_shape, operands, specs=None, scratch=(), after=(), limit=28 * MIB, weight=WEIGHT):
    shapes = jax.tree.leaves(out_shape)
    moved = sum(a.size * a.dtype.itemsize for a in list(operands) + shapes)
    count = len(operands)

    def run(*refs):
        kernel(*refs[:count], *refs[count + len(after) :])

    return pl.pallas_call(
        run,
        out_shape=out_shape,
        in_specs=(specs or vmem_specs(count)) + [pl.BlockSpec(memory_space=pl.ANY)] * len(after),
        out_specs=jax.tree.map(lambda _: pl.BlockSpec(memory_space=pltpu.VMEM), out_shape),
        scratch_shapes=scratch,
        compiler_params=pltpu.CompilerParams(vmem_limit_bytes=limit),
        cost_estimate=pl.CostEstimate(flops=weight, bytes_accessed=moved, transcendentals=0),
        name=name,
    )(*operands, *after)


def spread_kernel(count_ref, out):
    out[...] = jnp.broadcast_to(count_ref[0, 0], out.shape)


def pair_kernel(own, sib, out):
    lane = lax.broadcasted_iota(jnp.int32, out.shape, 1)
    out[...] = jnp.where(lane == 0, own[...], sib[...])


def split_kernel(rows_ref, keep_ref, send_ref):
    half = keep_ref.shape[1]
    core = lax.rem(lax.axis_index("mem"), 2)
    keep_ref[...] = rows_ref[:, pl.ds(pl.multiple_of(core * half, half), half)]
    send_ref[...] = rows_ref[:, pl.ds(pl.multiple_of((1 - core) * half, half), half)]


def load_kernel(cand_hbm, cand_ref, norm_ref, sems):
    half = cand_ref.shape[1] // 2
    core = lax.rem(lax.axis_index("mem"), 2)
    tiles, copies = cand_ref.shape[0] // TILE, []
    for t in range(tiles):
        at = pl.ds(t * TILE, TILE)
        for k, own in enumerate((core, 1 - core)):
            copies.append(
                pltpu.make_async_copy(
                    cand_hbm.at[at, pl.ds(pl.multiple_of(own * half, half), half)],
                    cand_ref.at[at, pl.ds(k * half, half)],
                    sems.at[len(copies)],
                )
            )
    for copy in copies:
        copy.start()
    for t in range(tiles):
        for copy in copies[2 * t : 2 * t + 2]:
            copy.wait()
        squares = jnp.zeros((TILE, 128), F32)
        for k in range(0, cand_ref.shape[1], 128):
            entries = cand_ref[t * TILE : (t + 1) * TILE, k : k + 128].astype(F32)
            squares += entries * entries
        norm_ref[:, t * TILE : (t + 1) * TILE] = jnp.sum(squares.T, axis=0, keepdims=True)


def stack_kernel(layout, *refs):
    out, top = refs[-1], 0
    for parts in layout:
        left, rows = 0, refs[parts[0][0]].shape[0]
        for index, start, columns in parts:
            out[top : top + rows, left : left + columns] = refs[index][:, start : start + columns]
            left += columns
        top += rows


def copy_kernel(block, out):
    rows = min(block.shape[0], out.shape[0])
    out[:rows, :] = block[:rows, :]
    if out.shape[0] > rows:
        out[rows:, :] = block[: out.shape[0] - rows, :]


def dense_kernel(size, picks_chip, rest_chip, chosen_ref, *refs):
    chips = size // 2
    counts, (own, sib, *outs, select_ref) = refs[:chips], refs[chips:]
    slots, picks = own.shape[0], chosen_ref.shape[1]
    rows_chip = picks_chip + rest_chip
    me = lax.axis_index("mem")
    offsets = [jnp.zeros((1, 1), jnp.int32) for _ in range(2)]
    for d, ref in enumerate(counts):
        for h in range(2):
            origin = lax.bitwise_xor(me, 2 * d + h)
            for k in range(2):
                before = (origin < lax.bitwise_xor(me, k)).astype(jnp.int32)
                offsets[k] += ref[:1, h : h + 1] * before
    lane = lax.broadcasted_iota(jnp.int32, (1, 2 * slots), 1)
    first = lane < slots
    within = jnp.where(first, lane, lane - slots)
    alive = within < jnp.where(first, counts[0][:1, :1], counts[0][:1, 1:2])
    position = jnp.where(alive, within + jnp.where(first, offsets[0], offsets[1]), -1)

    chosen = chosen_ref[...]

    def column(start, length):
        row = lax.broadcasted_iota(jnp.int32, (length, picks), 0)
        across = lax.broadcasted_iota(jnp.int32, (length, picks), 1)
        return jnp.sum(jnp.where(across == row + start, chosen, 0), axis=1, keepdims=True)

    ids = column(0, picks)
    below = jnp.sum((ids < position).astype(jnp.int32), axis=0, keepdims=True)
    taken = jnp.sum((ids == position).astype(jnp.int32), axis=0, keepdims=True)
    rank = jnp.where(alive & (taken == 0), position - below, -1)
    place = lax.broadcasted_iota(jnp.int32, (rest_chip, 1), 0)
    for d in range(chips):
        owner = lax.bitwise_xor(me // 2, d)
        top = d * rows_chip
        hit = column(owner * picks_chip, picks_chip) == position
        select_ref[top : top + picks_chip, :] = hit.astype(F32).astype(BF16)
        hit = place + owner * rest_chip == rank
        select_ref[top + picks_chip : top + rows_chip, :] = hit.astype(F32).astype(BF16)

    for t in range(0, own.shape[1], TILE):
        at = slice(t, t + TILE)
        rows = jnp.concatenate([own[:, at], sib[:, at]], axis=0)
        found = jnp.dot(select_ref[...], rows, preferred_element_type=F32).astype(BF16)
        for d, out in enumerate(outs):
            out[:, at] = found[d * rows_chip : (d + 1) * rows_chip]


def sum_kernel(*refs):
    *parts, out, picks_ref = refs
    total = parts[0][...]
    for ref in parts[1:]:
        total += ref[...]
    out[...] = total
    picks_ref[...] = total[: picks_ref.shape[0], :]


def row_norms(rows):
    rows = rows.astype(F32)
    return jnp.sum(rows * rows, axis=1, keepdims=True)


def gaps_to(rows_ref, norms, cand):
    inner = lax.dot_general(
        rows_ref[...], cand, (((1,), (1,)), ((), ())), preferred_element_type=F32
    )
    return norms - 2.0 * inner


def tiles_of(cand_ref):
    return [slice(t, t + TILE) for t in range(0, cand_ref.shape[0], TILE)]


def lay_out(parts, rows_ref):
    left = 0
    for part in parts:
        rows_ref[:, left : left + part.shape[1]] = part[: rows_ref.shape[0], :]
        left += part.shape[1]
    return row_norms(rows_ref[...])


def row_masks(picks_chip, rows_chip, own_rows, rows):
    row = lax.broadcasted_iota(jnp.int32, (rows, 1), 0)
    own = row < own_rows
    pick = (lax.rem(row, rows_chip) < picks_chip) | ~own
    return jnp.where(own, 0.0, jnp.inf), jnp.where(pick, 0.0, jnp.inf)


def least(gaps):
    return jnp.min(gaps, axis=0, keepdims=True)


def first_kernel(chip_rows, cand_ref, norm_ref, own, sib, near_ref, best_ref, rows_ref):
    norms = lay_out((own, sib), rows_ref)
    no_row, no_pick = row_masks(*chip_rows, norms.shape[0])
    for at in tiles_of(cand_ref):
        gaps = gaps_to(rows_ref, norms, cand_ref[at, :])
        near_ref[:, at] = least(gaps + no_row) + norm_ref[:, at]
        best_ref[:, at] = least(gaps + no_pick)


def next_kernel(blocks, cand_ref, best_ref, *refs):
    *parts, out, rows_ref = refs
    norms, count, rows = [], len(parts) // blocks, rows_ref.shape[0] // blocks
    for b in range(blocks):
        block = rows_ref.at[b * rows : (b + 1) * rows, :]
        norms.append(lay_out(parts[b * count : (b + 1) * count], block))
    norms = jnp.concatenate(norms, axis=0)
    for at in tiles_of(cand_ref):
        gaps = gaps_to(rows_ref, norms, cand_ref[at, :])
        out[:, at] = jnp.minimum(least(gaps), best_ref[:, at])


def half_kernel(cand_ref, *refs):
    *corner, out, rows_ref = refs
    norms = lay_out(corner, rows_ref)
    for at in tiles_of(cand_ref):
        out[:, at] = gaps_to(rows_ref, norms, cand_ref[at, : rows_ref.shape[1]])


def last_kernel(cand_ref, norm_ref, best_ref, part_ref, *refs):
    *corner, out, rows_ref = refs
    norms = lay_out(corner, rows_ref)
    for at in tiles_of(cand_ref):
        gaps = part_ref[:, at] + gaps_to(rows_ref, norms, cand_ref[at, rows_ref.shape[1] :])
        out[:, at] = jnp.minimum(least(gaps), best_ref[:, at]) + norm_ref[:, at]


def body(candidates, round_one, counts, chosen):
    size, groups = lax.axis_size("mem"), lax.axis_size("grp")
    slots, width = round_one.shape
    half, chips = width // 2, size // 2
    picks, rows = chosen.shape[1], candidates.shape[0]
    picks_chip = picks // chips
    rest_chip = (size * slots * 3 // 8 - picks) // chips
    rows_chip = picks_chip + rest_chip
    live = chips * rows_chip

    def bf16(*dims):
        return jax.ShapeDtypeStruct(dims, BF16)

    def stack(*blocks, after=()):
        operands, layout = [], []
        for block in blocks:
            parts = [p if isinstance(p, tuple) else (p, 0, p.shape[1]) for p in block]
            layout.append([(len(operands) + i, *p[1:]) for i, p in enumerate(parts)])
            operands += [p[0] for p in parts]
        shape = bf16(
            sum(operands[parts[0][0]].shape[0] for parts in layout), sum(p[2] for p in layout[0])
        )
        return call(
            functools.partial(stack_kernel, layout), "stack", shape, operands, after=after, weight=0
        )

    def copy(block, count, after):
        shape = bf16(count, block.shape[1])
        return call(copy_kernel, "copy", shape, (block,), after=after, weight=0)

    line = jax.ShapeDtypeStruct((1, rows), F32)
    tile = jax.ShapeDtypeStruct((8, 128), jnp.int32)
    count = call(
        spread_kernel, "spread", tile, (counts,), specs=[pl.BlockSpec(memory_space=pltpu.SMEM)]
    )
    pair = call(pair_kernel, "pair", tile, (count, flip_permute(count, size, 1)))
    pairs = to_chips(pair, size)
    own, send = call(split_kernel, "split", [bf16(slots, half)] * 2, (round_one,))
    sib = flip_permute(send, size, 1)

    parts = call(
        functools.partial(dense_kernel, size, picks_chip, rest_chip), "dense",
        [bf16(rows_chip, half)] * chips, (chosen, *pairs, own, sib),
        scratch=[pltpu.VMEM((live, 2 * slots), BF16)],
    )
    cand, norm = call(
        load_kernel, "load", [bf16(rows, width), line], (candidates,),
        specs=[pl.BlockSpec(memory_space=pltpu.HBM)], after=parts[:1],
        scratch=[pltpu.SemaphoreType.DMA((rows // TILE * 2,))], limit=42 * MIB,
    )
    got = [flip_permute(parts[d], size, 2 * d) for d in range(1, chips)]
    owned, picked = call(
        sum_kernel, "owned", [bf16(rows_chip, half), bf16(picks_chip, half)], (parts[0], *got),
        after=(norm,),
    )

    shifted = [
        lax.ppermute(picked, "grp", [(g, (g + k) % groups) for g in range(groups)])
        for k in sorted(range(1, groups), key=lambda k: abs(2 * k - groups))
    ]

    if chips == 4:
        quarter = half // 2
        own_x, own_y = (flip_permute(owned, size, flip) for flip in (2, 4))
        own_left = flip_permute(stack([(own_x, 0, quarter)]), size, 4)
        own_right = flip_permute(stack([(own_y, quarter, quarter)]), size, 2)
        wait = (own_left, own_right)
        low = stack(*[[(b, 0, quarter)] for b in shifted], after=wait)
        high = stack(*[[(b, quarter, quarter)] for b in shifted], after=wait)
        low_x, high_y = flip_permute(low, size, 2), flip_permute(high, size, 4)
        high_x, low_y = flip_permute(high, size, 2), flip_permute(low, size, 4)
        first = stack([owned], [own_x], [own_y], [own_left, own_right], [low, high])
        others = ([low_x, high_x], [low_y, high_y])
    else:
        far = to_chips(stack(*[[b] for b in shifted]), size)
        first = stack(*[[b] for b in to_chips(owned, size)], [far[0]])
        others = [[b] for b in far[1:-1]]

    near, best = call(
        functools.partial(first_kernel, (picks_chip, rows_chip, live)),
        "products", [line] * 2, (cand, norm, first, flip_permute(first, size, 1)),
        scratch=[pltpu.VMEM((first.shape[0], width), BF16)], weight=WEIGHT // 10,
    )
    rows_end = (groups - 1) * picks_chip
    if chips == 4:
        left = copy(low_x, rows_end + 16, (best,))
        right = copy(high_y, rows_end + 16, (best,))
        corner = (flip_permute(left, size, 4), flip_permute(right, size, 2))
    else:
        corner = (far[-1],)
    operands, handed = [], (left, right) if chips == 4 else ()
    for block in others:
        operands += block
        for b in block:
            after = (best, *handed)
            operands.append(flip_permute(stack([b], after=after), size, 1))
    best = call(
        functools.partial(next_kernel, len(others)), "products_next", line, (cand, best, *operands),
        scratch=[pltpu.VMEM((len(others) * others[0][0].shape[0], width), BF16)], weight=0,
    )
    sent = [copy(part, rows_end, (best,)) for part in corner]
    swapped = [flip_permute(part, size, 1) for part in sent]
    scratch = [pltpu.VMEM((rows_end, half), BF16)]
    part = call(
        half_kernel, "products_half", jax.ShapeDtypeStruct((rows_end, rows), F32), (cand, *corner),
        scratch=scratch, after=(best,),
    )
    final = call(
        last_kernel, "products_last", line, (cand, norm, best, part, *swapped), scratch=scratch
    )
    return near.reshape(-1), final.reshape(-1)


def solution(mesh):
    in_specs = (P(("grp", "mem"), None), P(("grp", "mem"), None), P("grp", "mem"), P("grp", None))
    out_specs = (P(("grp", "mem")), P(("grp", "mem")))
    return jax.shard_map(body, mesh=mesh, in_specs=in_specs, out_specs=out_specs, check_vma=False)
```

```python
import functools

import jax
import jax.numpy as jnp
from jax import lax
from jax.experimental import pallas as pl
from jax.experimental.pallas import tpu as pltpu
from jax.sharding import PartitionSpec as P

TILE = 256
MIB = 1024 * 1024
WEIGHT = 10**10
F32, BF16 = jnp.float32, jnp.bfloat16


def flip_permute(block, size, flip):
    return lax.ppermute(block, "mem", [(m, m ^ flip) for m in range(size)])


def to_chips(block, size):
    return [block] + [flip_permute(block, size, 2 * d) for d in range(1, size // 2)]


def vmem_specs(count):
    return [pl.BlockSpec(memory_space=pltpu.VMEM)] * count


def call(kernel, name, out_shape, operands, specs=None, scratch=(), after=(), limit=28 * MIB, weight=WEIGHT):
    shapes = jax.tree.leaves(out_shape)
    moved = sum(a.size * a.dtype.itemsize for a in list(operands) + shapes)
    count = len(operands)

    def run(*refs):
        kernel(*refs[:count], *refs[count + len(after) :])

    return pl.pallas_call(
        run,
        out_shape=out_shape,
        in_specs=(specs or vmem_specs(count)) + [pl.BlockSpec(memory_space=pl.ANY)] * len(after),
        out_specs=jax.tree.map(lambda _: pl.BlockSpec(memory_space=pltpu.VMEM), out_shape),
        scratch_shapes=scratch,
        compiler_params=pltpu.CompilerParams(vmem_limit_bytes=limit),
        cost_estimate=pl.CostEstimate(flops=weight, bytes_accessed=moved, transcendentals=0),
        name=name,
    )(*operands, *after)


def spread_kernel(count_ref, out):
    out[...] = jnp.broadcast_to(count_ref[0, 0], out.shape)


def pair_kernel(own, sib, out):
    lane = lax.broadcasted_iota(jnp.int32, out.shape, 1)
    out[...] = jnp.where(lane == 0, own[...], sib[...])


def split_kernel(rows_ref, keep_ref, send_ref):
    half = keep_ref.shape[1]
    core = lax.rem(lax.axis_index("mem"), 2)
    keep_ref[...] = rows_ref[:, pl.ds(pl.multiple_of(core * half, half), half)]
    send_ref[...] = rows_ref[:, pl.ds(pl.multiple_of((1 - core) * half, half), half)]


def load_kernel(cand_hbm, cand_ref, norm_ref, sems):
    half = cand_ref.shape[1] // 2
    core = lax.rem(lax.axis_index("mem"), 2)
    tiles, copies = cand_ref.shape[0] // TILE, []
    for t in range(tiles):
        at = pl.ds(t * TILE, TILE)
        for k, own in enumerate((core, 1 - core)):
            copies.append(
                pltpu.make_async_copy(
                    cand_hbm.at[at, pl.ds(pl.multiple_of(own * half, half), half)],
                    cand_ref.at[at, pl.ds(k * half, half)],
                    sems.at[len(copies)],
                )
            )
    for copy in copies:
        copy.start()
    for t in range(tiles):
        for copy in copies[2 * t : 2 * t + 2]:
            copy.wait()
        squares = jnp.zeros((TILE, 128), F32)
        for k in range(0, cand_ref.shape[1], 128):
            entries = cand_ref[t * TILE : (t + 1) * TILE, k : k + 128].astype(F32)
            squares += entries * entries
        norm_ref[:, t * TILE : (t + 1) * TILE] = jnp.sum(squares.T, axis=0, keepdims=True)


def stack_kernel(layout, *refs):
    out, top = refs[-1], 0
    for parts in layout:
        left, rows = 0, refs[parts[0][0]].shape[0]
        for index, start, columns in parts:
            out[top : top + rows, left : left + columns] = refs[index][:, start : start + columns]
            left += columns
        top += rows


def copy_kernel(block, out):
    rows = min(block.shape[0], out.shape[0])
    out[:rows, :] = block[:rows, :]
    if out.shape[0] > rows:
        out[rows:, :] = block[: out.shape[0] - rows, :]


def dense_kernel(size, picks_chip, rest_chip, chosen_ref, *refs):
    chips = size // 2
    counts, (own, sib, *outs, select_ref) = refs[:chips], refs[chips:]
    slots, picks = own.shape[0], chosen_ref.shape[1]
    rows_chip = picks_chip + rest_chip
    me = lax.axis_index("mem")
    offsets = [jnp.zeros((1, 1), jnp.int32) for _ in range(2)]
    for d, ref in enumerate(counts):
        for h in range(2):
            origin = lax.bitwise_xor(me, 2 * d + h)
            for k in range(2):
                before = (origin < lax.bitwise_xor(me, k)).astype(jnp.int32)
                offsets[k] += ref[:1, h : h + 1] * before
    lane = lax.broadcasted_iota(jnp.int32, (1, 2 * slots), 1)
    first = lane < slots
    within = jnp.where(first, lane, lane - slots)
    alive = within < jnp.where(first, counts[0][:1, :1], counts[0][:1, 1:2])
    position = jnp.where(alive, within + jnp.where(first, offsets[0], offsets[1]), -1)

    chosen = chosen_ref[...]

    def column(start, length):
        row = lax.broadcasted_iota(jnp.int32, (length, picks), 0)
        across = lax.broadcasted_iota(jnp.int32, (length, picks), 1)
        return jnp.sum(jnp.where(across == row + start, chosen, 0), axis=1, keepdims=True)

    ids = column(0, picks)
    below = jnp.sum((ids < position).astype(jnp.int32), axis=0, keepdims=True)
    taken = jnp.sum((ids == position).astype(jnp.int32), axis=0, keepdims=True)
    rank = jnp.where(alive & (taken == 0), position - below, -1)
    place = lax.broadcasted_iota(jnp.int32, (rest_chip, 1), 0)
    for d in range(chips):
        owner = lax.bitwise_xor(me // 2, d)
        top = d * rows_chip
        hit = column(owner * picks_chip, picks_chip) == position
        select_ref[top : top + picks_chip, :] = hit.astype(F32).astype(BF16)
        hit = place + owner * rest_chip == rank
        select_ref[top + picks_chip : top + rows_chip, :] = hit.astype(F32).astype(BF16)

    for t in range(0, own.shape[1], TILE):
        at = slice(t, t + TILE)
        rows = jnp.concatenate([own[:, at], sib[:, at]], axis=0)
        found = jnp.dot(select_ref[...], rows, preferred_element_type=F32).astype(BF16)
        for d, out in enumerate(outs):
            out[:, at] = found[d * rows_chip : (d + 1) * rows_chip]


def sum_kernel(*refs):
    *parts, out, picks_ref = refs
    total = parts[0][...]
    for ref in parts[1:]:
        total += ref[...]
    out[...] = total
    picks_ref[...] = total[: picks_ref.shape[0], :]


def row_norms(rows):
    rows = rows.astype(F32)
    return jnp.sum(rows * rows, axis=1, keepdims=True)


def gaps_to(rows_ref, norms, cand):
    inner = lax.dot_general(
        rows_ref[...], cand, (((1,), (1,)), ((), ())), preferred_element_type=F32
    )
    return norms - 2.0 * inner


def tiles_of(cand_ref):
    return [slice(t, t + TILE) for t in range(0, cand_ref.shape[0], TILE)]


def lay_out(parts, rows_ref):
    left = 0
    for part in parts:
        rows_ref[:, left : left + part.shape[1]] = part[: rows_ref.shape[0], :]
        left += part.shape[1]
    return row_norms(rows_ref[...])


def row_masks(picks_chip, rows_chip, own_rows, rows):
    row = lax.broadcasted_iota(jnp.int32, (rows, 1), 0)
    own = row < own_rows
    pick = (lax.rem(row, rows_chip) < picks_chip) | ~own
    return jnp.where(own, 0.0, jnp.inf), jnp.where(pick, 0.0, jnp.inf)


def least(gaps):
    return jnp.min(gaps, axis=0, keepdims=True)


def first_kernel(chip_rows, cand_ref, norm_ref, own, sib, near_ref, best_ref, rows_ref):
    norms = lay_out((own, sib), rows_ref)
    no_row, no_pick = row_masks(*chip_rows, norms.shape[0])
    for at in tiles_of(cand_ref):
        gaps = gaps_to(rows_ref, norms, cand_ref[at, :])
        near_ref[:, at] = least(gaps + no_row) + norm_ref[:, at]
        best_ref[:, at] = least(gaps + no_pick)


def next_kernel(blocks, cand_ref, best_ref, *refs):
    *parts, out, rows_ref = refs
    norms, count, rows = [], len(parts) // blocks, rows_ref.shape[0] // blocks
    for b in range(blocks):
        block = rows_ref.at[b * rows : (b + 1) * rows, :]
        norms.append(lay_out(parts[b * count : (b + 1) * count], block))
    norms = jnp.concatenate(norms, axis=0)
    for at in tiles_of(cand_ref):
        gaps = gaps_to(rows_ref, norms, cand_ref[at, :])
        out[:, at] = jnp.minimum(least(gaps), best_ref[:, at])


def half_kernel(cand_ref, *refs):
    *corner, out, rows_ref = refs
    norms = lay_out(corner, rows_ref)
    for at in tiles_of(cand_ref):
        out[:, at] = gaps_to(rows_ref, norms, cand_ref[at, : rows_ref.shape[1]])


def last_kernel(cand_ref, norm_ref, best_ref, part_ref, *refs):
    *corner, out, rows_ref = refs
    norms = lay_out(corner, rows_ref)
    for at in tiles_of(cand_ref):
        gaps = part_ref[:, at] + gaps_to(rows_ref, norms, cand_ref[at, rows_ref.shape[1] :])
        out[:, at] = jnp.minimum(least(gaps), best_ref[:, at]) + norm_ref[:, at]


def body(candidates, round_one, counts, chosen):
    size, groups = lax.axis_size("mem"), lax.axis_size("grp")
    slots, width = round_one.shape
    half, chips = width // 2, size // 2
    picks, rows = chosen.shape[1], candidates.shape[0]
    picks_chip = picks // chips
    rest_chip = (size * slots * 3 // 8 - picks) // chips
    rows_chip = picks_chip + rest_chip
    live = chips * rows_chip

    def bf16(*dims):
        return jax.ShapeDtypeStruct(dims, BF16)

    def stack(*blocks, after=()):
        operands, layout = [], []
        for block in blocks:
            parts = [p if isinstance(p, tuple) else (p, 0, p.shape[1]) for p in block]
            layout.append([(len(operands) + i, *p[1:]) for i, p in enumerate(parts)])
            operands += [p[0] for p in parts]
        shape = bf16(
            sum(operands[parts[0][0]].shape[0] for parts in layout), sum(p[2] for p in layout[0])
        )
        return call(
            functools.partial(stack_kernel, layout), "stack", shape, operands, after=after, weight=0
        )

    def copy(block, count, after):
        shape = bf16(count, block.shape[1])
        return call(copy_kernel, "copy", shape, (block,), after=after, weight=0)

    line = jax.ShapeDtypeStruct((1, rows), F32)
    tile = jax.ShapeDtypeStruct((8, 128), jnp.int32)
    count = call(
        spread_kernel, "spread", tile, (counts,), specs=[pl.BlockSpec(memory_space=pltpu.SMEM)]
    )
    pair = call(pair_kernel, "pair", tile, (count, flip_permute(count, size, 1)))
    pairs = to_chips(pair, size)
    own, send = call(split_kernel, "split", [bf16(slots, half)] * 2, (round_one,))
    sib = flip_permute(send, size, 1)

    parts = call(
        functools.partial(dense_kernel, size, picks_chip, rest_chip), "dense",
        [bf16(rows_chip, half)] * chips, (chosen, *pairs, own, sib),
        scratch=[pltpu.VMEM((live, 2 * slots), BF16)],
    )
    cand, norm = call(
        load_kernel, "load", [bf16(rows, width), line], (candidates,),
        specs=[pl.BlockSpec(memory_space=pltpu.HBM)], after=parts[:1],
        scratch=[pltpu.SemaphoreType.DMA((rows // TILE * 2,))], limit=42 * MIB,
    )
    got = [flip_permute(parts[d], size, 2 * d) for d in range(chips - 1, 0, -1)]
    owned, picked = call(
        sum_kernel, "owned", [bf16(rows_chip, half), bf16(picks_chip, half)], (parts[0], *got),
        after=(norm,),
    )

    shifted = [
        lax.ppermute(picked, "grp", [(g, (g + k) % groups) for g in range(groups)])
        for k in range(1, groups)
    ]

    if chips == 4:
        quarter = half // 2
        own_x, own_y = (flip_permute(owned, size, flip) for flip in (2, 4))
        own_left = flip_permute(stack([(own_x, 0, quarter)]), size, 4)
        own_right = flip_permute(stack([(own_y, quarter, quarter)]), size, 2)
        wait = (own_left, own_right)
        low = stack(*[[(b, 0, quarter)] for b in shifted], after=wait)
        high = stack(*[[(b, quarter, quarter)] for b in shifted], after=wait)
        low_x, high_y = flip_permute(low, size, 2), flip_permute(high, size, 4)
        high_x, low_y = flip_permute(high, size, 2), flip_permute(low, size, 4)
        first = stack([owned], [own_x], [own_y], [own_left, own_right], [low, high])
        others = ([low_x, high_x], [low_y, high_y])
    else:
        far = to_chips(stack(*[[b] for b in shifted]), size)
        first = stack(*[[b] for b in to_chips(owned, size)], [far[0]])
        others = [[b] for b in far[1:-1]]

    near, best = call(
        functools.partial(first_kernel, (picks_chip, rows_chip, live)),
        "products", [line] * 2, (cand, norm, first, flip_permute(first, size, 1)),
        scratch=[pltpu.VMEM((first.shape[0], width), BF16)], weight=WEIGHT // 10,
    )
    rows_end = (groups - 1) * picks_chip
    if chips == 4:
        left = copy(low_x, rows_end + 16, (best,))
        right = copy(high_y, rows_end + 16, (best,))
        corner = (flip_permute(left, size, 4), flip_permute(right, size, 2))
    else:
        corner = (far[-1],)
    operands, handed = [], (left, right) if chips == 4 else ()
    for block in others:
        operands += block
        for b in block:
            after = (best, *handed)
            operands.append(flip_permute(stack([b], after=after), size, 1))
    best = call(
        functools.partial(next_kernel, len(others)), "products_next", line, (cand, best, *operands),
        scratch=[pltpu.VMEM((len(others) * others[0][0].shape[0], width), BF16)], weight=0,
    )
    sent = [copy(part, rows_end, (best,)) for part in corner]
    swapped = [flip_permute(part, size, 1) for part in sent]
    scratch = [pltpu.VMEM((rows_end, half), BF16)]
    part = call(
        half_kernel, "products_half", jax.ShapeDtypeStruct((rows_end, rows), F32), (cand, *corner),
        scratch=scratch, after=(best,),
    )
    final = call(
        last_kernel, "products_last", line, (cand, norm, best, part, *swapped), scratch=scratch
    )
    return near.reshape(-1), final.reshape(-1)


def solution(mesh):
    in_specs = (P(("grp", "mem"), None), P(("grp", "mem"), None), P("grp", "mem"), P("grp", None))
    out_specs = (P(("grp", "mem")), P(("grp", "mem")))
    return jax.shard_map(body, mesh=mesh, in_specs=in_specs, out_specs=out_specs, check_vma=False)
```
